128 devices in a mesh: grp: 8 (over x, core), blk: 16 (over y, z).
Axes of the slice: x: 4, y: 4, z: 4, core: 2. Of those that a mesh axis runs over, the one named last changes fastest.
Arguments:
- flow_state: float32 [5, 1024, 4096], P(None, 'grp', 'blk'), may hold values from -6 to 6
- jacobi_x: float32 [5, 5], replicated, may hold values from -2.5 to 2.5
- jacobi_y: float32 [5, 5], replicated, may hold values from -2.5 to 2.5
- slot_tile: int32 [8192], P(('grp', 'blk')), may hold values from -1 to 95, as said below
- slot_cells: int32 [8192, 128], P(('grp', 'blk')), may hold values from 0 to 32767
- slot_normal: float32 [8192, 3, 128], P(('grp', 'blk')), may hold values from -6 to 6
- slot_rbf: bfloat16 [8192, 128, 128], P(('grp', 'blk')), may hold values from -0.5 to 0.5
- disp_in: float32 [1536, 3, 128], P('blk'), may hold values from -24 to 24
- flexibility: float32 [1536, 128, 128], P('blk'), may hold values from -0.5 to 0.5
- secant_v: float32 [24, 1536, 3, 128], P(None, 'blk'), may hold values from -3.4 to 3.4
- secant_w: float32 [24, 1536, 3, 128], P(None, 'blk'), may hold values from -6 to 6
Outputs:
- flow_out: float32 [5, 1024, 4096], P(None, 'grp', 'blk')
- disp_out: float32 [1536, 3, 128], P('blk')
The draws below stay inside these ranges and needn't reach their ends.
Inputs may be any that keep to these rules, and one draw needn't show every extreme that they name: `slot_tile`: each fluid block has at most 4 live slots for each structure partition, its live slots to a partition come first among that partition's 4 slots, and every fluid block fills all 4 slots of one partition.
All inputs are finite; a program needn't handle non-finite values.
Results may differ from the reference program's by a relative error of at most 0.002.
Values may be sent and summed in bfloat16 or wider, within the bound.
A program may use at most 128 MiB of HBM per device.

```python
import jax
import jax.numpy as jnp
from jax import lax

CX = 128
CY = 256
NV = 5
NODE = 128
SEND = 4
ST = 96
COLS = 24
NX = 1024
NY = 4096
FLUID_DEVS = 128
PARTS_SIZE = 16
SLOTS_DEV = 64
SLOTS_ALL = 8192
ST_ALL = 1536


def shared_mode(key):
    return jnp.clip(jax.random.normal(key, (ST_ALL, 3, NODE), jnp.float32), -6.0, 6.0)


def draw_slot_tile(key, part):
    key = jax.random.fold_in(key, 5)
    key_count, key_full, key_tile = jax.random.split(key, 3)
    counts = jax.random.randint(key_count, (FLUID_DEVS, PARTS_SIZE), 0, SEND + 1)
    fullest = jax.random.randint(key_full, (FLUID_DEVS, 1), 0, PARTS_SIZE)
    counts = jnp.where(jnp.arange(PARTS_SIZE)[None, :] == fullest, SEND, counts)
    tiles = jax.random.randint(key_tile, (FLUID_DEVS, PARTS_SIZE, SEND), 0, ST)
    filled = jnp.arange(SEND)[None, None, :] < counts[:, :, None]
    return jnp.where(filled, tiles, -1).reshape(SLOTS_ALL).astype(jnp.int32)


def draw_disp_in(key, part):
    common = shared_mode(key)
    key = jax.random.fold_in(key, 12)
    noise = jnp.clip(jax.random.normal(key, (ST_ALL, 3, NODE), jnp.float32), -6.0, 6.0)
    return noise + 3.0 * common


def draw_secant_v(key, part):
    common = shared_mode(key)
    key = jax.random.fold_in(key, 11)
    key_scale, key_noise = jax.random.split(key)
    scales = jnp.exp(jax.random.uniform(key_scale, (COLS, 1, 1, 1), jnp.float32, -2.0794, -0.9808))
    noise = jnp.clip(jax.random.normal(key_noise, (COLS, ST_ALL, 3, NODE), jnp.float32), -6.0, 6.0)
    return scales * (noise + 0.5 * common[None])


def touch_ends(entries, own_key, least, top_value):
    dims = entries.shape
    index_at = [jax.random.randint(jax.random.fold_in(own_key, axis), (), 0, dims[axis]) for axis in range(len(dims))]
    entries = entries.at[tuple(index_at)].set(least)
    longest = dims.index(max(dims))
    index_at[longest] = (index_at[longest] + 1) % dims[longest]
    return entries.at[tuple(index_at)].set(top_value)


def shard_levels(key, extent, pieces, low, largest):
    level = 1.0
    for axis_at, parts in pieces:
        heights = jax.random.uniform(jax.random.fold_in(jax.random.fold_in(key, 6), axis_at), (parts,), jnp.float32, low / len(pieces), largest / len(pieces))
        level = level * jnp.repeat(jnp.exp(heights), extent[axis_at] // parts).reshape((-1,) + (1,) * (len(extent) - 1 - axis_at))
    return level


def bell_draw(stream_key, extent, width, reach, cuts=(), held_as=jnp.bfloat16):
    level = shard_levels(stream_key, extent, cuts, -0.22, 0.18) if cuts else 1.0
    values = jax.random.normal(stream_key, extent, jnp.float32) * width * level
    return jnp.minimum(jnp.maximum(values, -reach), reach).astype(held_as)


def setup_inputs(seed: int = 0) -> dict:
    seeds = jax.random.split(jax.random.key(seed), 12)
    return {
        "flow_state": bell_draw(seeds[0], (NV, NX, NY), 1.0, 6.0, ((1, 8), (2, 16)), jnp.float32),
        "jacobi_x": bell_draw(seeds[1], (NV, NV), NV ** -0.5, 2.5, (), jnp.float32),
        "jacobi_y": bell_draw(seeds[2], (NV, NV), NV ** -0.5, 2.5, (), jnp.float32),
        "slot_tile": draw_slot_tile(jax.random.fold_in(seeds[11], 71), 0),
        "slot_cells": touch_ends(jax.random.randint(seeds[4], (SLOTS_ALL, NODE), 0, CX * CY), jax.random.fold_in(seeds[4], 1), 0, (CX * CY) - 1).astype(jnp.int32),
        "slot_normal": bell_draw(seeds[5], (SLOTS_ALL, 3, NODE), 1.0, 6.0, ((0, 128),), jnp.float32),
        "slot_rbf": bell_draw(seeds[6], (SLOTS_ALL, NODE, NODE), NODE ** -0.5, 0.5, ((0, 128),)),
        "disp_in": draw_disp_in(jax.random.fold_in(seeds[11], 71), 0),
        "flexibility": bell_draw(seeds[8], (ST_ALL, NODE, NODE), NODE ** -0.5, 0.5, ((0, 16),), jnp.float32),
        "secant_v": draw_secant_v(jax.random.fold_in(seeds[11], 71), 0),
        "secant_w": bell_draw(seeds[10], (COLS, ST_ALL, 3, NODE), 1.0, 6.0, ((1, 16),), jnp.float32),
    }


SECTION_RATES = (0.25, 1.0 / 3.0, 0.5, 1.0)
TIME_STEP = 0.4
DAMPING = 0.25
FORCING = 1.0
HIGH = lax.Precision.HIGHEST

def flow_residual(padded, jacobi_x, jacobi_y):
    centre = padded[:, 1:-1, 1:-1]
    east = padded[:, 2:, 1:-1]
    west = padded[:, :-2, 1:-1]
    north = padded[:, 1:-1, 2:]
    south = padded[:, 1:-1, :-2]
    flux = jnp.einsum('uv,vxy->uxy', jacobi_x, east - west, precision=HIGH)
    flux = flux + jnp.einsum('uv,vxy->uxy', jacobi_y, north - south, precision=HIGH)
    return -0.5 * flux + DAMPING * (east + west + north + south - 4.0 * centre)

def reference(flow_state, jacobi_x, jacobi_y, slot_tile, slot_cells, slot_normal, slot_rbf, disp_in, flexibility, secant_v, secant_w):
    slot_ids = jnp.arange(SLOTS_ALL, dtype=jnp.int32)
    device_of = slot_ids // SLOTS_DEV
    dest_of = slot_ids % SLOTS_DEV // SEND
    live = (slot_tile >= 0).astype(jnp.float32)
    tile_global = (dest_of * ST + jnp.maximum(slot_tile, 0)).astype(jnp.int32)
    row_base = device_of // PARTS_SIZE * CX
    col_base = device_of % PARTS_SIZE * CY
    grid_rows = row_base[:, None] + slot_cells // CY
    grid_cols = col_base[:, None] + slot_cells % CY
    flat_cells = (grid_rows * NY + grid_cols).astype(jnp.int32)
    disp_half = disp_in.astype(jnp.bfloat16)
    fetched = disp_half[tile_global]
    rbf_dev = slot_rbf.reshape(FLUID_DEVS, SLOTS_DEV, NODE, NODE)

    def interp_out(pair):
        return jnp.einsum('sfn,scn->scf', pair[0].astype(jnp.float32), pair[1].astype(jnp.float32))
    node_disp = lax.map(interp_out, (rbf_dev, fetched.reshape(FLUID_DEVS, SLOTS_DEV, 3, NODE)))
    node_disp = node_disp.reshape(SLOTS_ALL, 3, NODE) * live[:, None, None]
    flat_state = flow_state.reshape(NV, NX * NY)
    spread = jnp.transpose(node_disp, (1, 0, 2)).reshape(3, SLOTS_ALL * NODE)
    momentum = flat_state[1:4].at[:, flat_cells.reshape(-1)].add(FORCING * spread)
    forced = jnp.concatenate([flat_state[0:1], momentum, flat_state[4:]], axis=0).reshape(NV, NX, NY)
    current = forced
    for rate in SECTION_RATES:
        padded = jnp.pad(current, ((0, 0), (1, 1), (1, 1)))
        current = forced + rate * TIME_STEP * flow_residual(padded, jacobi_x, jacobi_y)
    flow_out = current
    pressure = flow_out[4].reshape(-1)[flat_cells]
    force = (pressure[:, None, :] * slot_normal * live[:, None, None]).astype(jnp.bfloat16)

    def interp_in(pair):
        return jnp.einsum('sfn,scf->scn', pair[0].astype(jnp.float32), pair[1].astype(jnp.float32))
    slot_load = lax.map(interp_in, (rbf_dev, force.reshape(FLUID_DEVS, SLOTS_DEV, 3, NODE)))
    slot_load = slot_load.reshape(SLOTS_ALL, 3, NODE)
    segment = jnp.where(slot_tile >= 0, tile_global, ST_ALL).astype(jnp.int32)
    loads = jax.ops.segment_sum(slot_load, segment, num_segments=ST_ALL + 1)[:ST_ALL]
    tilde = jnp.einsum('tnm,tcm->tcn', flexibility, loads, precision=HIGH)
    resid = tilde - disp_in
    flat_v = secant_v.reshape(COLS, ST_ALL * 3 * NODE)
    gram = jnp.dot(flat_v, flat_v.T, precision=HIGH)
    rhs = jnp.dot(flat_v, resid.reshape(-1), precision=HIGH)
    factor = jnp.linalg.cholesky(gram)
    coef = -jax.scipy.linalg.cho_solve((factor, True), rhs)
    disp_out = tilde + jnp.einsum('k,ktcn->tcn', coef, secant_w, precision=HIGH)
    return (flow_out, disp_out)
```

```python
import functools

import jax
import jax.numpy as jnp
from jax import lax
from jax.experimental import pallas as pl
from jax.experimental.pallas import tpu as pltpu
from jax.sharding import PartitionSpec as P

RATES = (0.25, 1.0 / 3.0, 0.5, 1.0)
TIME_STEP = 0.4
DAMPING = 0.25
FORCING = 1.0
F32 = jnp.float32
BF16 = jnp.bfloat16
MESH = pl.DeviceIdType.MESH
NG, NB = 8, 16
SEND, ST, COLS, NV = 4, 96, 24, 5
CX, CY = 128, 256
OWN = ST // NG
WIN = 16
NN = (((1,), (0,)), ((), ()))
NT = (((1,), (1,)), ((), ()))


def iota(shape, dim):
    return lax.broadcasted_iota(jnp.int32, shape, dim)


def dot(a, b, dims):
    return lax.dot_general(a, b, dims, preferred_element_type=F32)


def split(x):
    hi = x.astype(BF16)
    return hi, (x - hi.astype(F32)).astype(BF16)


def window(g):
    return lax.div(g * OWN, 8) * 8


def kernel(
    flow_h, jx, jy, tile_h, cells_h, normal_h, rbf_h, disp_h, flex_h, secv_h, secw_h,
    flow_o, disp_o,
    tile, cells, normal, rbf, disp, flex, secv, secw,
    force_q, qa, qb, qout,
    req, land_req, resp, land_disp, dispc, rall, bmat, acc, pack,
    land_below, land_above, land_right, land_left, land_corner,
    nrm, load_out, land_load, oht, part, land_part,
    flexhl, zmat, gsend, land_gg, gsum, land_gb, linv,
    tmsg, land_t, rsend, land_r, coef, dout,
    lsem, osem, bs, br, gs, gr, hs, hr,
):
    g = lax.axis_index("grp")
    b = lax.axis_index("blk")
    a = pl.multiple_of(window(g), 8)
    off = g * OWN - window(g)

    loads = [
        (tile_h, tile),
        (disp_h, disp),
        (cells_h, cells),
        (rbf_h, rbf),
        (flow_h, force_q.at[:, pl.ds(8, CX), pl.ds(0, CY)]),
        (secv_h.at[:, :, pl.ds(a, WIN), :], secv),
        (normal_h, normal),
        (flex_h.at[pl.ds(g * OWN, OWN)], flex),
        (secw_h, secw),
    ]
    loads = [pltpu.make_async_copy(s, d, lsem.at[i]) for i, (s, d) in enumerate(loads)]
    for c in loads:
        c.start()
    l_tile, l_disp, l_cells, l_rbf, l_flow, l_secv, l_normal, l_flex, l_secw = loads

    barrier = pltpu.get_barrier_semaphore()

    def hello_blk(o, _):
        pl.semaphore_signal(barrier, inc=1, device_id=(g, lax.rem(b + o, NB)), device_id_type=MESH)
        return 0

    def hello_grp(o, _):
        pl.semaphore_signal(barrier, inc=1, device_id=(lax.rem(g + o, NG), b), device_id_type=MESH)
        return 0

    lax.fori_loop(1, NB, hello_blk, 0)
    lax.fori_loop(1, NG, hello_grp, 0)
    g_up, g_dn = lax.rem(g + 1, NG), lax.rem(g + NG - 1, NG)
    b_up, b_dn = lax.rem(b + 1, NB), lax.rem(b + NB - 1, NB)
    diagonal = ((g_dn, b_dn), (g_dn, b_up), (g_up, b_dn), (g_up, b_up))
    for dev in diagonal:
        pl.semaphore_signal(barrier, inc=1, device_id=dev, device_id_type=MESH)

    def blk_copy(src, dst, ph, o, dev):
        return pltpu.make_async_remote_copy(
            src_ref=src, dst_ref=dst, send_sem=bs.at[ph, o], recv_sem=br.at[ph, o],
            device_id=(g, dev), device_id_type=MESH,
        )

    def grp_copy(src, dst, ph, o, dev):
        return pltpu.make_async_remote_copy(
            src_ref=src, dst_ref=dst, send_sem=gs.at[ph, o], recv_sem=gr.at[ph, o],
            device_id=(dev, b), device_id_type=MESH,
        )

    def each(n, step):
        def body(o, _):
            step(o)
            return 0

        lax.fori_loop(1, n, body, 0)

    def blk_send(src, land, ph):
        def step(o):
            d = lax.rem(b + o, NB)
            blk_copy(src(d), land.at[b], ph, o, d).start()

        each(NB, step)

    def blk_recv(src, land, ph):
        def step(o):
            d = lax.rem(b + NB - o, NB)
            blk_copy(src(d), land.at[d], ph, o, d).wait_recv()

        each(NB, step)

    def grp_send(src, land, ph):
        def step(o):
            d = lax.rem(g + o, NG)
            grp_copy(src(d), land.at[g], ph, o, d).start()

        each(NG, step)

    def grp_recv(src, land, ph):
        def step(o):
            d = lax.rem(g + NG - o, NG)
            grp_copy(src(d), land.at[d], ph, o, d).wait_recv()

        each(NG, step)

    def sent(n, copy, src, land, ph):
        def step(o):
            copy(src(0), land.at[0], ph, o, 0).wait_send()

        each(n, step)

    l_tile.wait()
    row = iota((NB * 16, 64), 0)
    hit = iota((NB * 16, 64), 1) == lax.shift_right_logical(row, 4) * SEND + (row & 3)
    wanted = jnp.sum(jnp.where(hit, tile[...].astype(F32), 0.0), axis=1, keepdims=True)
    row = iota((NB * 16, 128), 0)
    wanted = jnp.where((row & 15) < 12, jnp.broadcast_to(wanted, (NB * 16, 128)), -1.0)
    req[...] = wanted.reshape(NB, 16, 128)
    land_req[b] = req[b]
    pl.semaphore_wait(barrier, NB - 1 + NG - 1 + 4)
    blk_send(lambda d: req.at[d], land_req, 0)

    l_disp.wait()
    dispc[...] = jnp.zeros(dispc.shape, BF16)
    for c in range(3):
        dispc[128 * c : 128 * c + ST, :] = disp[c].astype(BF16)
    l_cells.wait()

    def rows_of(d, _):
        for j in range(SEND):
            cell = cells[pl.ds(d * SEND + j, 1), :]
            r = (lax.shift_right_logical(cell, 7) & 1) * 128 + lax.shift_right_logical(cell, 8)
            one = jnp.where(iota((256, 128), 0) == r, 1.0, 0.0).astype(BF16)
            rall[d, :, 128 * j : 128 * (j + 1)] = one
        return 0

    lax.fori_loop(0, NB, rows_of, 0)

    blk_recv(lambda d: req.at[d], land_req, 0)
    asked = land_req[...].reshape(NB * 16, 128)
    row = iota((NB * 16, 128), 0)
    tile_lane = iota((NB * 16, 128), 1).astype(F32)
    pick = jnp.concatenate(
        [
            jnp.where((asked == tile_lane) & ((lax.shift_right_logical(row, 2) & 3) == c), 1.0, 0.0).astype(BF16)
            for c in range(3)
        ],
        axis=1,
    )
    resp[...] = dot(pick, dispc[...], NN).astype(BF16).reshape(NB, 16, 128)
    land_disp[b] = resp[b]
    blk_send(lambda d: resp.at[d], land_disp, 1)

    asked_t = asked.T[0:1, :]
    rr, kk = iota((48, NB * 16), 0), iota((48, NB * 16), 1)
    w = rr & 15
    same_c = (lax.shift_right_logical(kk, 2) & 3) == lax.shift_right_logical(rr, 4)
    for p in range(NG):
        first = (p * OWN) // 8 * 8
        skip = p * OWN - first
        ok = same_c & (w >= skip) & (w < skip + OWN)
        oht[48 * p : 48 * (p + 1), :] = jnp.where(ok & (asked_t == (w + first).astype(F32)), 1.0, 0.0).astype(BF16)
    l_secv.wait()
    zero8 = jnp.zeros((8, 128), F32)
    for c in range(3):
        for i in range(WIN):
            x = secv[:, c, i, :]
            x = jnp.where((i >= off) & (i < off + OWN), x, 0.0)
            x = jnp.concatenate([x, zero8], axis=0)
            hi, lo = split(x)
            at = (c * WIN + i) * 128
            zmat[0:32, at : at + 128] = hi
            zmat[32:64, at : at + 128] = lo
    zz = zmat[...]
    top = dot(zz, zz[0:32], NT)
    low = dot(zz, zz[32:64], NT)
    gram = top[0:32] + top[32:64] + low[0:32] + low[32:64]
    gsend[...] = jnp.zeros(gsend.shape, F32)
    gsend[:, 0:32] = gram
    land_gg[g] = gsend[...]
    grp_send(lambda d: gsend, land_gg, 0)

    blk_recv(lambda d: resp.at[d], land_disp, 1)
    l_rbf.wait()
    acc[...] = jnp.zeros(acc.shape, F32)

    def spread(d, _):
        x = land_disp[d]
        base = pl.multiple_of(d * SEND, SEND)
        weights = rbf[pl.ds(base, SEND)].reshape(SEND * 128, 128)
        o = dot(x, weights, NT)
        for j in range(SEND):
            cell = cells[pl.ds(d * SEND + j, 1), :]
            mask = iota((128, 128), 0) == (cell & 127)
            for c in range(3):
                v = o[4 * c + j : 4 * c + j + 1, 128 * j : 128 * (j + 1)] * FORCING
                vh = v.astype(BF16).astype(F32)
                vl = v - vh
                at = c * 256
                bmat[at : at + 128, 128 * j : 128 * (j + 1)] = jnp.where(mask, vh, 0.0).astype(BF16)
                bmat[at + 128 : at + 256, 128 * j : 128 * (j + 1)] = jnp.where(mask, vl, 0.0).astype(BF16)
        acc[...] += dot(bmat[...], rall[d], NT)
        return 0

    lax.fori_loop(0, NB, spread, 0)
    l_flow.wait()
    for c in range(3):
        s = acc[256 * c : 256 * c + 128, :] + acc[256 * c + 128 : 256 * c + 256, :]
        force_q[1 + c, 8 : 8 + CX, 0:128] += s[:, 0:128].T
        force_q[1 + c, 8 : 8 + CX, 128:256] += s[:, 128:256].T

    lane = iota((128, 128), 1)
    strip = lax.shift_right_logical((lane + 4) & 127, 3)
    packed = jnp.zeros((128, 128), F32)
    for v in range(NV):
        t = jnp.where(lane < 64, force_q[v, 8 : 8 + CX, 0:128], force_q[v, 8 : 8 + CX, 128:256])
        if v:
            t = pltpu.roll(t, 8 * v, 1)
        packed = jnp.where(strip == v, t, packed)
    lane64 = iota((64, 128), 1)
    pack[...] = jnp.where(((lane64 + 4) & 127) < 64, packed[0:64], pltpu.roll(packed[64:128], 64, 1))
    top_rows = force_q.at[:, pl.ds(8, 8), pl.ds(0, CY)]
    low_rows = force_q.at[:, pl.ds(CX, 8), pl.ds(0, CY)]
    halo = [
        (top_rows, land_below, (g_dn, b)),
        (low_rows, land_above, (g_up, b)),
        (pack, land_right, (g, b_dn)),
        (pack, land_left, (g, b_up)),
        (pack.at[pl.ds(0, 8)], land_corner.at[0], (g_dn, b_dn)),
        (pack.at[pl.ds(0, 8)], land_corner.at[1], (g_dn, b_up)),
        (pack.at[pl.ds(56, 8)], land_corner.at[2], (g_up, b_dn)),
        (pack.at[pl.ds(56, 8)], land_corner.at[3], (g_up, b_up)),
    ]
    halo = [
        pltpu.make_async_remote_copy(
            src_ref=s, dst_ref=d, send_sem=hs.at[i], recv_sem=hr.at[i], device_id=dev, device_id_type=MESH
        )
        for i, (s, d, dev) in enumerate(halo)
    ]
    for c in halo:
        c.start()

    grp_recv(lambda d: gsend, land_gg, 0)
    gsum[...] = jnp.sum(land_gg[...], axis=0)
    land_gb[b] = gsum[...]
    blk_send(lambda d: gsum, land_gb, 2)
    l_normal.wait()
    nrm[...] = jnp.zeros(nrm.shape, F32)
    for c in range(3):
        for j in range(SEND):
            nrm[pl.ds(4 * c + j, NB, stride=16), :] = normal[c, pl.ds(j, NB, stride=SEND), :]
    l_flex.wait()
    for i in range(OWN):
        hi, lo = split(flex[i])
        flexhl[128 * i : 128 * (i + 1), 0:128] = hi
        flexhl[128 * i : 128 * (i + 1), 128:256] = lo

    for c in halo:
        c.wait_recv()
    is_up, is_dn = g < NG - 1, g > 0
    is_right, is_left = b < NB - 1, b > 0
    force_q[:, 8 + CX : 16 + CX, 0:CY] = jnp.where(is_up, land_below[...], 0.0)
    force_q[:, 0:8, 0:CY] = jnp.where(is_dn, land_above[...], 0.0)

    def sides(right, left, ok):
        from_right = (iota(right.shape, 1) & 7) < 4
        return jnp.where(from_right, jnp.where(is_right & ok, right, 0.0), jnp.where(is_left & ok, left, 0.0))

    mid = sides(land_right[...], land_left[...], True)
    mid = jnp.concatenate([mid, pltpu.roll(mid, 64, 1)], axis=0)
    below = sides(land_corner[0], land_corner[1], is_up)
    above = pltpu.roll(sides(land_corner[2], land_corner[3], is_dn), 64, 1)
    edge = jnp.concatenate([above, mid, below], axis=0)
    for v in range(NV):
        force_q[v, :, CY : CY + 128] = pltpu.roll(edge, 128 - 8 * v, 1) if v else edge

    lane = iota((8, CY + 128), 1)
    sub = iota((8, CY + 128), 0)
    outside = ((lane >= CY) & (lane < CY + 64) & jnp.logical_not(is_right)) | (
        (lane >= CY + 64) & jnp.logical_not(is_left)
    )
    inside = jnp.where(outside, 0.0, TIME_STEP).astype(F32)
    ax = [[-0.5 * jx[u, v] for v in range(NV)] for u in range(NV)]
    ay = [[-0.5 * jy[u, v] for v in range(NV)] for u in range(NV)]

    def stage(src, dst, rate, last):
        def body(i, _):
            r = pl.multiple_of(i * 8, 8)
            rp = pl.multiple_of(jnp.maximum(i - 1, 0) * 8, 8)
            rn = pl.multiple_of(jnp.minimum(i + 1, 17) * 8, 8)
            row_ok = jnp.where(i == 0, is_dn, jnp.where(i == 17, is_up, True))
            scale = jnp.where(row_ok, rate, 0.0).astype(F32) * inside
            dx, dy, near = [], [], []
            for v in range(NV):
                cur = src[v, pl.ds(r, 8), :]
                up = pltpu.roll(jnp.where(sub == 0, src[v, pl.ds(rn, 8), :], cur), 7, 0)
                dn = pltpu.roll(jnp.where(sub == 7, src[v, pl.ds(rp, 8), :], cur), 1, 0)
                rt = pltpu.roll(cur, CY + 127, 1)
                lt = pltpu.roll(cur, 1, 1)
                dx.append(up - dn)
                dy.append(rt - lt)
                near.append(DAMPING * ((up + dn) + (rt + lt)) - 4.0 * DAMPING * cur)
            for u in range(NV):
                res = near[u]
                for v in range(NV):
                    res = res + ax[u][v] * dx[v] + ay[u][v] * dy[v]
                new = force_q[u, pl.ds(r, 8), :] + scale * res
                if last:
                    qout[u, pl.ds(pl.multiple_of(r - 8, 8), 8), :] = new[:, 0:CY]
                else:
                    dst[u, pl.ds(r, 8), :] = new
            return 0

        lax.fori_loop(1 if last else 0, 17 if last else 18, body, 0)

    stage(force_q, qa, RATES[0], False)
    stage(qa, qb, RATES[1], False)
    stage(qb, qa, RATES[2], False)
    stage(qa, None, RATES[3], True)
    flow_out = pltpu.make_async_copy(qout, flow_o, osem.at[0])
    flow_out.start()

    pres = qout[4]
    pres = jnp.concatenate([pres[:, 0:128].T, pres[:, 128:256].T], axis=1)
    ph, plow = split(pres)
    pres2 = jnp.concatenate([ph, plow], axis=0)
    row16 = iota((16, 128), 0)

    def gather(o, _):
        d = lax.rem(b + o, NB)
        h = dot(pres2, rall[d], NN)
        h = h[0:128] + h[128:256]
        n16 = nrm[pl.ds(pl.multiple_of(d * 16, 16), 16), :]
        forces = []
        for j in range(SEND):
            cell = cells[pl.ds(d * SEND + j, 1), :]
            mask = iota((128, 128), 0) == (cell & 127)
            p = jnp.sum(jnp.where(mask, h[:, 128 * j : 128 * (j + 1)], 0.0), axis=0, keepdims=True)
            forces.append(jnp.where((row16 & 3) == j, n16 * p, 0.0).astype(BF16))
        base = pl.multiple_of(d * SEND, SEND)
        weights = rbf[pl.ds(base, SEND)].reshape(SEND * 128, 128)
        load_out[d] = dot(jnp.concatenate(forces, axis=1), weights, NN)

        @pl.when(o > 0)
        def _():
            blk_copy(load_out.at[d], land_load.at[b], 3, o, d).start()

        return 0

    lax.fori_loop(0, NB, gather, 0)
    land_load[b] = load_out[b]

    blk_recv(lambda d: gsum, land_gb, 2)
    gram = jnp.sum(land_gb[...], axis=0)[0:COLS]
    row = iota((COLS, 128), 0)
    lane = iota((COLS, 128), 1)
    m = jnp.where(lane < COLS, gram, jnp.where(lane == row + 32, 1.0, 0.0))
    fac = jnp.zeros((COLS, 128), F32)
    for k in range(COLS):
        pivot = lax.rsqrt(jnp.broadcast_to(m[k : k + 1, k : k + 1], (1, 128)))
        r = m[k : k + 1, :] * pivot
        col = jnp.broadcast_to(m[:, k : k + 1], (COLS, 128)) * pivot
        fac = jnp.where(row == k, r, fac)
        m = m - jnp.where(row > k, col * r, 0.0)
    linv[...] = jnp.where((lane >= 32) & (lane < 32 + COLS), fac, 0.0)

    blk_recv(lambda d: load_out.at[d], land_load, 3)
    got = land_load[...].reshape(NB * 16, 128)
    hi, lo = split(got)
    sums = dot(oht[...], jnp.concatenate([hi, lo], axis=1), NN)
    part[...] = (sums[:, 0:128] + sums[:, 128:256]).reshape(NG, 48, 128)
    land_part[g] = part[g]
    grp_send(lambda d: part.at[d], land_part, 1)
    grp_recv(lambda d: part.at[d], land_part, 1)
    tile_loads = jnp.sum(land_part[...], axis=0)

    hi, lo = split(tile_loads)
    lhs = jnp.concatenate(
        [jnp.concatenate([hi, hi], axis=1), jnp.concatenate([lo, jnp.zeros_like(lo)], axis=1)], axis=0
    )
    wrow = iota((48, 128), 0) & 15
    tilde = jnp.zeros((48, 128), F32)
    for u in range(OWN // 2):
        o = dot(lhs, flexhl[256 * u : 256 * (u + 1), :], NT)
        o = o[0:48] + o[48:96]
        tilde = tilde + jnp.where(wrow == off + 2 * u, o[:, 0:128], 0.0)
        tilde = tilde + jnp.where(wrow == off + 2 * u + 1, o[:, 128:256], 0.0)
    mine = (wrow >= off) & (wrow < off + OWN)
    d_in = disp[:, pl.ds(a, WIN), :].reshape(48, 128)
    resid = jnp.where(mine, tilde - d_in, 0.0)
    prod = jnp.sum(secv[...].reshape(COLS, 48, 128) * resid[None], axis=1)
    rhs = jnp.sum(prod, axis=1, keepdims=True)
    diag = lane == row + 32
    rhs = jnp.sum(jnp.where(diag, rhs, 0.0), axis=0, keepdims=True)
    tmsg[0:48, :] = tilde
    tmsg[48:56, :] = jnp.broadcast_to(rhs, (8, 128))
    land_t[g] = tmsg[...]
    grp_send(lambda d: tmsg, land_t, 2)
    grp_recv(lambda d: tmsg, land_t, 2)
    rsend[...] = jnp.sum(land_t[:, 48:56, :], axis=0)
    land_r[b] = rsend[...]
    blk_send(lambda d: rsend, land_r, 4)
    l_secw.wait()
    blk_recv(lambda d: rsend, land_r, 4)
    rhs = jnp.sum(land_r[...], axis=0)[0:1]

    li = linv[...]
    y = jnp.sum(li * rhs, axis=1, keepdims=True)
    x = jnp.sum(li * y, axis=0, keepdims=True)
    x = -jnp.sum(jnp.where(diag, x, 0.0), axis=1, keepdims=True)
    coef[...] = jnp.broadcast_to(x, (COLS, 128))
    for q in range(ST // 8):
        p, part_at = 2 * (q // 3), q % 3
        for c in range(3):
            if part_at == 0:
                t = land_t[p, 16 * c : 16 * c + 8, :]
            elif part_at == 1:
                t = land_t[p, 16 * c + 8 : 16 * c + 16, :] + land_t[p + 1, 16 * c : 16 * c + 8, :]
            else:
                t = land_t[p + 1, 16 * c + 8 : 16 * c + 16, :]
            for k in range(COLS):
                t = t + coef[k : k + 1, :] * secw[k, c, 8 * q : 8 * q + 8, :]
            dout[c, 8 * q : 8 * q + 8, :] = t
    disp_out = pltpu.make_async_copy(dout, disp_o, osem.at[1])
    disp_out.start()

    sent(NB, blk_copy, lambda d: req.at[d], land_req, 0)
    sent(NB, blk_copy, lambda d: resp.at[d], land_disp, 1)
    sent(NB, blk_copy, lambda d: gsum, land_gb, 2)
    sent(NB, blk_copy, lambda d: load_out.at[d], land_load, 3)
    sent(NB, blk_copy, lambda d: rsend, land_r, 4)
    sent(NG, grp_copy, lambda d: gsend, land_gg, 0)
    sent(NG, grp_copy, lambda d: part.at[d], land_part, 1)
    sent(NG, grp_copy, lambda d: tmsg, land_t, 2)
    for c in halo:
        c.wait_send()
    flow_out.wait()
    disp_out.wait()


def on_device(flow_state, jx, jy, slot_tile, slot_cells, slot_normal, slot_rbf, disp_in, flex, secv, secw):
    hbm = pl.BlockSpec(memory_space=pl.ANY)
    smem = pl.BlockSpec(memory_space=pltpu.SMEM)
    vm = pltpu.VMEM
    state = (NV, CX + 16, CY + 128)
    scratch = [
        vm((1, 64), jnp.int32),
        vm((64, 128), jnp.int32),
        vm((3, 64, 128), F32),
        vm((64, 128, 128), BF16),
        vm((3, ST, 128), F32),
        vm((OWN, 128, 128), F32),
        vm((COLS, 3, WIN, 128), F32),
        vm((COLS, 3, ST, 128), F32),
        vm(state, F32), vm(state, F32), vm(state, F32), vm((NV, CX, CY), F32),
        vm((NB, 16, 128), F32), vm((NB, 16, 128), F32),
        vm((NB, 16, 128), BF16), vm((NB, 16, 128), BF16),
        vm((384, 128), BF16),
        vm((NB, 256, 512), BF16),
        vm((768, 512), BF16),
        vm((768, 256), F32),
        vm((64, 128), F32),
        vm((NV, 8, CY), F32), vm((NV, 8, CY), F32),
        vm((64, 128), F32), vm((64, 128), F32), vm((4, 8, 128), F32),
        vm((256, 128), F32),
        vm((NB, 16, 128), F32), vm((NB, 16, 128), F32),
        vm((384, 256), BF16),
        vm((NG, 48, 128), F32), vm((NG, 48, 128), F32),
        vm((OWN * 128, 256), BF16),
        vm((64, 48 * 128), BF16),
        vm((32, 128), F32), vm((NG, 32, 128), F32), vm((32, 128), F32), vm((NB, 32, 128), F32),
        vm((COLS, 128), F32),
        vm((56, 128), F32), vm((NG, 56, 128), F32),
        vm((8, 128), F32), vm((NB, 8, 128), F32),
        vm((COLS, 128), F32),
        vm((3, ST, 128), F32),
        pltpu.SemaphoreType.DMA((9,)),
        pltpu.SemaphoreType.DMA((2,)),
        pltpu.SemaphoreType.DMA((5, NB)), pltpu.SemaphoreType.DMA((5, NB)),
        pltpu.SemaphoreType.DMA((3, NG)), pltpu.SemaphoreType.DMA((3, NG)),
        pltpu.SemaphoreType.DMA((8,)), pltpu.SemaphoreType.DMA((8,)),
    ]
    flow_out, disp_out = pl.pallas_call(
        kernel,
        out_shape=(
            jax.ShapeDtypeStruct((NV, CX, CY), F32),
            jax.ShapeDtypeStruct((3, ST, 128), F32),
        ),
        in_specs=[hbm, smem, smem] + [hbm] * 8,
        out_specs=(hbm, hbm),
        scratch_shapes=scratch,
        compiler_params=pltpu.CompilerParams(
            collective_id=0, has_side_effects=True, vmem_limit_bytes=48 * 1024 * 1024
        ),
    )(
        flow_state, jx, jy, slot_tile.reshape(1, -1), slot_cells,
        jnp.transpose(slot_normal, (1, 0, 2)), slot_rbf, jnp.transpose(disp_in, (1, 0, 2)), flex,
        jnp.transpose(secv, (0, 2, 1, 3)), jnp.transpose(secw, (0, 2, 1, 3)),
    )
    return flow_out, jnp.transpose(disp_out, (1, 0, 2))


def solution(mesh):
    placed = (
        P(None, "grp", "blk"), P(), P(),
        P(("grp", "blk")), P(("grp", "blk"), None),
        P(("grp", "blk"), None, None), P(("grp", "blk"), None, None),
        P("blk", None, None), P("blk", None, None),
        P(None, "blk", None, None), P(None, "blk", None, None),
    )
    return jax.shard_map(
        on_device, mesh=mesh, in_specs=placed,
        out_specs=(P(None, "grp", "blk"), P("blk", None, None)), check_vma=False,
    )
```

```python
import functools

import jax
import jax.numpy as jnp
from jax import lax
from jax.experimental import pallas as pl
from jax.experimental.pallas import tpu as pltpu
from jax.sharding import PartitionSpec as P

RATES = (0.25, 1.0 / 3.0, 0.5, 1.0)
TIME_STEP = 0.4
DAMPING = 0.25
FORCING = 1.0
F32 = jnp.float32
BF16 = jnp.bfloat16
MESH = pl.DeviceIdType.MESH
NG, NB = 8, 16
SEND, ST, COLS, NV = 4, 96, 24, 5
CX, CY = 128, 256
OWN = ST // NG
WIN = 16
HOPS = ((0, 1), (0, 3), (1, 0), (3, 0), (1, 1), (1, 3), (3, 1), (3, 3), (0, 2), (2, 0), (1, 2), (3, 2), (2, 1), (2, 3), (0, 0), (2, 2))
BACK = tuple(HOPS.index(((4 - dy) % 4, (4 - dz) % 4)) for dy, dz in HOPS)
ME = HOPS.index((0, 0))
CLASSES = ((0, 4), (4, 10), (10, 14), (15, 16))
NN = (((1,), (0,)), ((), ()))
NT = (((1,), (1,)), ((), ()))


def iota(shape, dim):
    return lax.broadcasted_iota(jnp.int32, shape, dim)


def dot(a, b, dims):
    return lax.dot_general(a, b, dims, preferred_element_type=F32)


def split(x):
    hi = x.astype(BF16)
    return hi, (x - hi.astype(F32)).astype(BF16)


def window(g):
    return lax.div(g * OWN, 8) * 8


def kernel(
    flow_h, jx_h, jy_h, tile_h, cells_h, normal_h, rbf_h, disp_h, flex_h, secv_h, secw_h,
    flow_o, disp_o,
    jx, jy, tile, cells, normal, rbf, disp, flex, secv, secw,
    force_q, qa, qb, qout,
    req, land_req, resp, land_disp, dispc, cellv, rall, bmat0, bmat1, bmat2, acc, pack,
    land_below, land_above, land_right, land_left, land_corner,
    nrm, load_out, land_load, oht, part, land_part,
    flexhl, uwin, zmat, gsend, land_gg, gsum, land_gb, linv,
    rmsg, land_rg, tmsg, land_t, rsend, land_r, coef, dout,
    lsem, rsem, osem, bs, br, gs, gr, hs, hr,
):
    g = lax.axis_index("grp")
    b = lax.axis_index("blk")
    y, z = lax.div(b, 4), lax.rem(b, 4)
    a = pl.multiple_of(window(g), 8)
    off = g * OWN - window(g)

    def peer(o):
        return lax.rem(y + HOPS[o][0], 4) * 4 + lax.rem(z + HOPS[o][1], 4)

    loads = [
        (tile_h, tile),
        (cells_h, cells),
        (disp_h, disp),
        (secv_h.at[:, :, pl.ds(a, WIN), :], secv),
        (flow_h, force_q.at[:, pl.ds(8, CX), pl.ds(0, CY)]),
        (normal_h, normal),
        (flex_h.at[pl.ds(a, WIN)], flex),
        (jx_h, jx),
        (jy_h, jy),
        (secw_h, secw),
    ]
    loads = [pltpu.make_async_copy(s, d, lsem.at[i]) for i, (s, d) in enumerate(loads)]
    l_tile, l_cells, l_disp, l_secv, l_flow, l_normal, l_flex, l_jx, l_jy, l_secw = loads
    l_rbf = [
        pltpu.make_async_copy(rbf_h.at[pl.ds(peer(o) * SEND, SEND)], rbf.at[o], rsem.at[o]) for o in range(NB)
    ]
    for c in loads[:4] + l_rbf + loads[4:]:
        c.start()

    barrier = pltpu.get_barrier_semaphore()
    g_up, g_dn = lax.rem(g + 1, NG), lax.rem(g + NG - 1, NG)
    b_up, b_dn = lax.rem(b + 1, NB), lax.rem(b + NB - 1, NB)
    hello = [(g, peer(o)) for o in reversed(range(NB)) if o != ME]
    hello += [(g_dn, b_dn), (g_dn, b_up), (g_up, b_dn), (g_up, b_up)]
    hello += [(lax.rem(g + o, NG), b) for o in range(1, NG)]
    for dev in hello:
        pl.semaphore_signal(barrier, inc=1, device_id=dev, device_id_type=MESH)

    def blk_copy(src, land, ph, o):
        return pltpu.make_async_remote_copy(
            src_ref=src(o), dst_ref=land.at[BACK[o]], send_sem=bs.at[ph, o], recv_sem=br.at[ph, BACK[o]],
            device_id=(g, peer(o)), device_id_type=MESH,
        )

    def grp_copy(src, dst, ph, o, dev):
        return pltpu.make_async_remote_copy(
            src_ref=src, dst_ref=dst, send_sem=gs.at[ph, o], recv_sem=gr.at[ph, o],
            device_id=(dev, b), device_id_type=MESH,
        )

    def each(n, step):
        def body(o, _):
            step(o)
            return 0

        lax.fori_loop(1, n, body, 0)

    pending = []

    def finish():
        for wait in pending:
            wait()

    far_first = [o for o in reversed(range(NB)) if o != ME]

    def blk_send(src, land, ph, peers=far_first):
        for o in peers:
            copy = blk_copy(src, land, ph, o)
            copy.start()
            pending.append(copy.wait_send)

    def blk_recv(src, land, ph, peers=far_first[::-1]):
        for o in peers:
            pltpu.make_async_remote_copy(
                src_ref=src(o), dst_ref=land.at[o], send_sem=bs.at[ph, o], recv_sem=br.at[ph, o],
                device_id=(g, peer(o)), device_id_type=MESH,
            ).wait_recv()

    def grp_send(src, land, ph):
        def step(o):
            d = lax.rem(g + o, NG)
            grp_copy(src(d), land.at[g], ph, o, d).start()

        def last(o):
            grp_copy(src(0), land.at[0], ph, o, 0).wait_send()

        each(NG, step)
        pending.append(lambda: each(NG, last))

    def grp_recv(src, land, ph):
        def step(o):
            d = lax.rem(g + NG - o, NG)
            grp_copy(src(d), land.at[d], ph, o, d).wait_recv()

        each(NG, step)

    l_tile.wait()
    row = iota((NB * 16, 64), 0)
    hit = iota((NB * 16, 64), 1) == lax.shift_right_logical(row, 4) * SEND + (row & 3)
    wanted = jnp.sum(jnp.where(hit, tile[...].astype(F32), 0.0), axis=1, keepdims=True)
    row = iota((NB * 16, 128), 0)
    wanted = jnp.where((row & 15) < 12, jnp.broadcast_to(wanted, (NB * 16, 128)), -1.0)
    req[...] = wanted.reshape(NB, 16, 128)
    land_req[ME] = req[b]

    l_cells.wait()
    for o in range(NB):
        cellv[o, 0:SEND, :] = cells[pl.ds(peer(o) * SEND, SEND), :]

    def rows_of(o, _):
        for j in range(SEND):
            cell = cellv[o, j : j + 1, :]
            r = (lax.shift_right_logical(cell, 7) & 1) * 128 + lax.shift_right_logical(cell, 8)
            one = jnp.where(iota((256, 128), 0) == r, 1.0, 0.0).astype(BF16)
            rall[o, :, 128 * j : 128 * (j + 1)] = one
        return 0

    lax.fori_loop(0, NB, rows_of, 0)
    l_disp.wait()
    dispc[...] = jnp.zeros(dispc.shape, BF16)
    for c in range(3):
        dispc[128 * c : 128 * c + ST, :] = disp[c].astype(BF16)
    pl.semaphore_wait(barrier, len(hello))
    blk_send(lambda o: req.at[peer(o)], land_req, 0)

    def answer(first, last):
        n = (last - first) * 16
        asked = land_req[first:last].reshape(n, 128)
        row_c = lax.shift_right_logical(iota((n, 128), 0), 2) & 3
        found = asked == iota((n, 128), 1).astype(F32)
        pick = jnp.concatenate([jnp.where(found & (row_c == c), 1.0, 0.0).astype(BF16) for c in range(3)], axis=1)
        return dot(pick, dispc[...], NN).astype(BF16).reshape(last - first, 16, 128)

    land_disp[ME] = answer(ME, ME + 1)[0]
    for first, last in CLASSES:
        blk_recv(lambda o: req.at[peer(o)], land_req, 0, range(first, last))
        resp[first:last] = answer(first, last)
        blk_send(lambda o: resp.at[o], land_disp, 1, range(first, last))

    l_secv.wait()
    zero8 = jnp.zeros((8, 128), F32)
    for c in range(3):
        for i in range(WIN):
            x = secv[:, c, i, :]
            x = jnp.where((i >= off) & (i < off + OWN), x, 0.0)
            x = jnp.concatenate([x, zero8], axis=0)
            hi, lo = split(x)
            at = (c * WIN + i) * 128
            zmat[0:32, at : at + 128] = hi
            zmat[32:64, at : at + 128] = lo
    zz = zmat[...]
    top = dot(zz, zz[0:32], NT)
    low = dot(zz, zz[32:64], NT)
    gram = top[0:32] + top[32:64] + low[0:32] + low[32:64]
    gsend[...] = jnp.zeros(gsend.shape, F32)
    gsend[:, 0:32] = gram
    land_gg[g] = gsend[...]
    grp_send(lambda d: gsend, land_gg, 0)

    bmats = (bmat0, bmat1, bmat2)
    acc[...] = jnp.zeros(acc.shape, F32)

    def spread(first):
        for h in range(2):
            o = dot(land_disp[first + h], rbf[first + h].reshape(SEND * 128, 128), NT)
            for j in range(SEND):
                mask = iota((128, 128), 0) == (cellv[first + h, j : j + 1, :] & 127)
                at = 512 * h + 128 * j
                for c in range(3):
                    v = o[4 * c + j : 4 * c + j + 1, 128 * j : 128 * (j + 1)] * FORCING
                    vh = v.astype(BF16).astype(F32)
                    vl = v - vh
                    bmats[c][0:128, at : at + 128] = jnp.where(mask, vh, 0.0).astype(BF16)
                    bmats[c][128:256, at : at + 128] = jnp.where(mask, vl, 0.0).astype(BF16)
        for c in range(3):
            acc[c] += dot(bmats[c][:, 0:512], rall[first], NT) + dot(bmats[c][:, 512:1024], rall[first + 1], NT)

    for first, last in CLASSES:
        blk_recv(lambda o: resp.at[o], land_disp, 1, range(first, last))
        for o in range(first, last):
            l_rbf[o].wait()
        if last - first == 1:
            l_rbf[ME].wait()
            spread(ME)
        else:
            lax.fori_loop(first // 2, last // 2, lambda p, _: (spread(2 * p), 0)[1], 0)
    l_flow.wait()
    for c in range(3):
        s = acc[c, 0:128, :] + acc[c, 128:256, :]
        force_q[1 + c, 8 : 8 + CX, 0:128] += s[:, 0:128].T
        force_q[1 + c, 8 : 8 + CX, 128:256] += s[:, 128:256].T

    lane = iota((128, 128), 1)
    strip = lax.shift_right_logical((lane + 4) & 127, 3)
    packed = jnp.zeros((128, 128), F32)
    for v in range(NV):
        t = jnp.where(lane < 64, force_q[v, 8 : 8 + CX, 0:128], force_q[v, 8 : 8 + CX, 128:256])
        if v:
            t = pltpu.roll(t, 8 * v, 1)
        packed = jnp.where(strip == v, t, packed)
    lane64 = iota((64, 128), 1)
    pack[...] = jnp.where(((lane64 + 4) & 127) < 64, packed[0:64], pltpu.roll(packed[64:128], 64, 1))
    top_rows = force_q.at[:, pl.ds(8, 8), pl.ds(0, CY)]
    low_rows = force_q.at[:, pl.ds(CX, 8), pl.ds(0, CY)]
    halo = [
        (pack.at[pl.ds(0, 8)], land_corner.at[0], (g_dn, b_dn)),
        (pack.at[pl.ds(0, 8)], land_corner.at[1], (g_dn, b_up)),
        (pack.at[pl.ds(56, 8)], land_corner.at[2], (g_up, b_dn)),
        (pack.at[pl.ds(56, 8)], land_corner.at[3], (g_up, b_up)),
        (pack, land_right, (g, b_dn)),
        (pack, land_left, (g, b_up)),
        (top_rows, land_below, (g_dn, b)),
        (low_rows, land_above, (g_up, b)),
    ]
    halo = [
        pltpu.make_async_remote_copy(
            src_ref=s, dst_ref=d, send_sem=hs.at[i], recv_sem=hr.at[i], device_id=dev, device_id_type=MESH
        )
        for i, (s, d, dev) in enumerate(halo)
    ]
    for c in halo:
        c.start()
        pending.append(c.wait_send)

    grp_recv(lambda d: gsend, land_gg, 0)
    gsum[...] = jnp.sum(land_gg[...], axis=0)
    land_gb[ME] = gsum[...]
    blk_send(lambda o: gsum, land_gb, 2)
    l_normal.wait()
    nrm[...] = jnp.zeros(nrm.shape, F32)
    for c in range(3):
        for j in range(SEND):
            nrm[pl.ds(4 * c + j, NB, stride=16), :] = normal[c, pl.ds(j, NB, stride=SEND), :]
    asked_t = land_req[...].reshape(NB * 16, 128).T[0:1, :]
    rr, kk = iota((48, NB * 16), 0), iota((48, NB * 16), 1)
    w = rr & 15
    same_c = (lax.shift_right_logical(kk, 2) & 3) == lax.shift_right_logical(rr, 4)
    for p in range(NG):
        first = (p * OWN) // 8 * 8
        skip = p * OWN - first
        ok = same_c & (w >= skip) & (w < skip + OWN)
        oht[48 * p : 48 * (p + 1), :] = jnp.where(ok & (asked_t == (w + first).astype(F32)), 1.0, 0.0).astype(BF16)
    l_flex.wait()
    for i in range(WIN):
        hi, lo = split(flex[i])
        flexhl[128 * i : 128 * (i + 1), 0:128] = hi
        flexhl[128 * i : 128 * (i + 1), 128:256] = lo
        vh, vl = split(jnp.concatenate([secv[:, c, i, :] for c in range(3)], axis=0))
        u = dot(jnp.concatenate([vh, vl], axis=0), hi, NN)
        u = u[0:72] + u[72:144] + dot(vh, lo, NN)
        for c in range(3):
            uwin[:, c, i, :] = u[COLS * c : COLS * (c + 1)]

    for c in halo:
        c.wait_recv()
    is_up, is_dn = g < NG - 1, g > 0
    is_right, is_left = b < NB - 1, b > 0
    force_q[:, 8 + CX : 16 + CX, 0:CY] = jnp.where(is_up, land_below[...], 0.0)
    force_q[:, 0:8, 0:CY] = jnp.where(is_dn, land_above[...], 0.0)

    def sides(right, left, ok):
        from_right = (iota(right.shape, 1) & 7) < 4
        return jnp.where(from_right, jnp.where(is_right & ok, right, 0.0), jnp.where(is_left & ok, left, 0.0))

    mid = sides(land_right[...], land_left[...], True)
    mid = jnp.concatenate([mid, pltpu.roll(mid, 64, 1)], axis=0)
    below = sides(land_corner[0], land_corner[1], is_up)
    above = pltpu.roll(sides(land_corner[2], land_corner[3], is_dn), 64, 1)
    edge = jnp.concatenate([above, mid, below], axis=0)
    for v in range(NV):
        force_q[v, :, CY : CY + 128] = pltpu.roll(edge, 128 - 8 * v, 1) if v else edge

    l_jx.wait()
    l_jy.wait()
    lane = iota((8, CY + 128), 1)
    sub = iota((8, CY + 128), 0)
    outside = ((lane >= CY) & (lane < CY + 64) & jnp.logical_not(is_right)) | (
        (lane >= CY + 64) & jnp.logical_not(is_left)
    )
    inside = jnp.where(outside, 0.0, TIME_STEP).astype(F32)
    ax = [[-0.5 * jx[u, v] for v in range(NV)] for u in range(NV)]
    ay = [[-0.5 * jy[u, v] for v in range(NV)] for u in range(NV)]

    def stage(src, dst, rate, last):
        def tile_at(i):
            r = pl.multiple_of(i * 8, 8)
            rp = pl.multiple_of(jnp.maximum(i - 1, 0) * 8, 8)
            rn = pl.multiple_of(jnp.minimum(i + 1, 17) * 8, 8)
            row_ok = jnp.where(i == 0, is_dn, jnp.where(i == 17, is_up, True))
            scale = jnp.where(row_ok, rate, 0.0).astype(F32) * inside
            dx, dy, near = [], [], []
            for v in range(NV):
                cur = src[v, pl.ds(r, 8), :]
                up = pltpu.roll(jnp.where(sub == 0, src[v, pl.ds(rn, 8), :], cur), 7, 0)
                dn = pltpu.roll(jnp.where(sub == 7, src[v, pl.ds(rp, 8), :], cur), 1, 0)
                rt = pltpu.roll(cur, CY + 127, 1)
                lt = pltpu.roll(cur, 1, 1)
                dx.append(up - dn)
                dy.append(rt - lt)
                near.append(DAMPING * ((up + dn) + (rt + lt)) - 4.0 * DAMPING * cur)
            for u in range(NV):
                res = near[u]
                for v in range(NV):
                    res = res + (ax[u][v] * dx[v] + ay[u][v] * dy[v])
                new = force_q[u, pl.ds(r, 8), :] + scale * res
                if last:
                    qout[u, pl.ds(pl.multiple_of(r - 8, 8), 8), :] = new[:, 0:CY]
                else:
                    dst[u, pl.ds(r, 8), :] = new

        def body(p, _):
            first = 2 * p + (1 if last else 0)
            tile_at(first)
            tile_at(first + 1)
            return 0

        lax.fori_loop(0, 8 if last else 9, body, 0)

    stage(force_q, qa, RATES[0], False)
    stage(qa, qb, RATES[1], False)
    stage(qb, qa, RATES[2], False)
    stage(qa, None, RATES[3], True)
    flow_out = pltpu.make_async_copy(qout, flow_o, osem.at[0])
    flow_out.start()
    pending.append(flow_out.wait)

    pres = qout[4]
    pres = jnp.concatenate([pres[:, 0:128].T, pres[:, 128:256].T], axis=1)
    ph, plow = split(pres)
    pres2 = jnp.concatenate([ph, plow], axis=0)
    row16 = iota((16, 128), 0)
    for o in range(NB):
        cellv[o, SEND : 2 * SEND, :] = cellv[o, 0:SEND, :] & 127
    norms = [nrm[pl.ds(pl.multiple_of(peer(o) * 16, 16), 16), :] for o in range(NB)]
    for o in range(NB):
        resp_n = norms[o]
        load_out[o] = resp_n

    def gather(o):
        h = dot(pres2, rall[o], NN)
        h = h[0:128] + h[128:256]
        n16 = load_out[o]
        forces = []
        for j in range(SEND):
            mask = iota((128, 128), 0) == cellv[o, SEND + j : SEND + j + 1, :]
            p = jnp.sum(jnp.where(mask, h[:, 128 * j : 128 * (j + 1)], 0.0), axis=0, keepdims=True)
            forces.append(jnp.where((row16 & 3) == j, n16 * p, 0.0).astype(BF16))
        load_out[o] = dot(jnp.concatenate(forces, axis=1), rbf[o].reshape(SEND * 128, 128), NN)

    def gather_pair(p, _):
        gather(2 * p)
        gather(2 * p + 1)
        return 0

    for first, last in CLASSES[::-1]:
        if last - first == 1:
            gather_pair(ME // 2, 0)
            land_load[ME] = load_out[ME]
        else:
            lax.fori_loop(first // 2, last // 2, gather_pair, 0)
        blk_send(lambda o: load_out.at[o], land_load, 3, range(first, last))

    blk_recv(lambda o: gsum, land_gb, 2)
    gram = jnp.sum(land_gb[...], axis=0)[0:COLS]
    row = iota((COLS, 128), 0)
    lane = iota((COLS, 128), 1)
    m = jnp.where(lane < COLS, gram, jnp.where(lane == row + 32, 1.0, 0.0))
    fac = jnp.zeros((COLS, 128), F32)
    for k in range(COLS):
        pivot = lax.rsqrt(jnp.broadcast_to(m[k : k + 1, k : k + 1], (1, 128)))
        r = m[k : k + 1, :] * pivot
        col = jnp.broadcast_to(m[:, k : k + 1], (COLS, 128)) * pivot
        fac = jnp.where(row == k, r, fac)
        m = m - jnp.where(row > k, col * r, 0.0)
    linv[...] = jnp.where((lane >= 32) & (lane < 32 + COLS), fac, 0.0)
    wrow = iota((48, 128), 0) & 15
    mine = (wrow >= off) & (wrow < off + OWN)
    d_in = jnp.where(mine, disp[:, pl.ds(a, WIN), :].reshape(48, 128), 0.0)
    rhs_in = jnp.sum(secv[...].reshape(COLS, 48, 128) * d_in[None], axis=1)
    diag = lane == row + 32

    blk_recv(lambda o: load_out.at[o], land_load, 3)
    got = land_load[...].reshape(NB * 16, 128)
    hi, lo = split(got)
    sums = dot(oht[...], jnp.concatenate([hi, lo], axis=1), NN)
    part[...] = (sums[:, 0:128] + sums[:, 128:256]).reshape(NG, 48, 128)
    land_part[g] = part[g]
    grp_send(lambda d: part.at[d], land_part, 1)
    grp_recv(lambda d: part.at[d], land_part, 1)
    tile_loads = jnp.sum(land_part[...], axis=0)

    prod = jnp.sum(uwin[...].reshape(COLS, 48, 128) * tile_loads[None], axis=1) - rhs_in
    rhs = jnp.sum(prod, axis=1, keepdims=True)
    rhs = jnp.sum(jnp.where(diag, rhs, 0.0), axis=0, keepdims=True)
    rmsg[...] = jnp.broadcast_to(rhs, (8, 128))
    land_rg[g] = rmsg[...]
    grp_send(lambda d: rmsg, land_rg, 2)
    hi, lo = split(tile_loads)
    lhs = jnp.concatenate(
        [jnp.concatenate([hi, hi], axis=1), jnp.concatenate([lo, jnp.zeros_like(lo)], axis=1)], axis=0
    )
    tilde = jnp.zeros((48, 128), F32)
    for u in range(WIN // 2):
        o = dot(lhs, flexhl[256 * u : 256 * (u + 1), :], NT)
        o = o[0:48] + o[48:96]
        tilde = jnp.where(wrow == 2 * u, o[:, 0:128], tilde)
        tilde = jnp.where(wrow == 2 * u + 1, o[:, 128:256], tilde)
    tmsg[...] = jnp.where(mine, tilde, 0.0)
    land_t[g] = tmsg[...]
    grp_send(lambda d: tmsg, land_t, 3)
    grp_recv(lambda d: rmsg, land_rg, 2)
    rsend[...] = jnp.sum(land_rg[...], axis=0)
    land_r[ME] = rsend[...]
    blk_send(lambda o: rsend, land_r, 4)
    l_secw.wait()
    grp_recv(lambda d: tmsg, land_t, 3)
    blk_recv(lambda o: rsend, land_r, 4)
    rhs = jnp.sum(land_r[...], axis=0)[0:1]

    li = linv[...]
    y = jnp.sum(li * rhs, axis=1, keepdims=True)
    x = jnp.sum(li * y, axis=0, keepdims=True)
    x = -jnp.sum(jnp.where(diag, x, 0.0), axis=1, keepdims=True)
    coef[...] = jnp.broadcast_to(x, (COLS, 128))
    for q in range(ST // 8):
        p, part_at = 2 * (q // 3), q % 3
        for c in range(3):
            if part_at == 0:
                t = land_t[p, 16 * c : 16 * c + 8, :]
            elif part_at == 1:
                t = land_t[p, 16 * c + 8 : 16 * c + 16, :] + land_t[p + 1, 16 * c : 16 * c + 8, :]
            else:
                t = land_t[p + 1, 16 * c + 8 : 16 * c + 16, :]
            for k in range(COLS):
                t = t + coef[k : k + 1, :] * secw[k, c, 8 * q : 8 * q + 8, :]
            dout[c, 8 * q : 8 * q + 8, :] = t
    disp_out = pltpu.make_async_copy(dout, disp_o, osem.at[1])
    disp_out.start()
    pending.append(disp_out.wait)

    finish()


def stay(x):
    return pltpu.with_memory_space_constraint(x, pltpu.HBM)


def on_device(flow_state, jx, jy, slot_tile, slot_cells, slot_normal, slot_rbf, disp_in, flex, secv, secw):
    hbm = pl.BlockSpec(memory_space=pl.ANY)
    vm, dma = pltpu.VMEM, pltpu.SemaphoreType.DMA
    state = (NV, CX + 16, CY + 128)
    scratch = [
        pltpu.SMEM((NV, NV), F32), pltpu.SMEM((NV, NV), F32),
        vm((1, 64), jnp.int32), vm((64, 128), jnp.int32), vm((3, 64, 128), F32), vm((NB, SEND, 128, 128), BF16),
        vm((3, ST, 128), F32), vm((WIN, 128, 128), F32), vm((COLS, 3, WIN, 128), F32), vm((COLS, 3, ST, 128), F32),
        vm(state, F32), vm(state, F32), vm(state, F32), vm((NV, CX, CY), F32),
        vm((NB, 16, 128), F32), vm((NB, 16, 128), F32), vm((NB, 16, 128), BF16), vm((NB, 16, 128), BF16),
        vm((384, 128), BF16),
        vm((NB, 8, 128), jnp.int32), vm((NB, 256, 512), BF16),
        vm((256, 1024), BF16), vm((256, 1024), BF16), vm((256, 1024), BF16), vm((3, 256, 256), F32),
        vm((64, 128), F32),
        vm((NV, 8, CY), F32), vm((NV, 8, CY), F32), vm((64, 128), F32), vm((64, 128), F32), vm((4, 8, 128), F32),
        vm((256, 128), F32), vm((NB, 16, 128), F32), vm((NB, 16, 128), F32), vm((384, 256), BF16),
        vm((NG, 48, 128), F32), vm((NG, 48, 128), F32),
        vm((WIN * 128, 256), BF16), vm((COLS, 3, WIN, 128), F32), vm((64, 48 * 128), BF16),
        vm((32, 128), F32), vm((NG, 32, 128), F32), vm((32, 128), F32), vm((NB, 32, 128), F32), vm((COLS, 128), F32),
        vm((8, 128), F32), vm((NG, 8, 128), F32), vm((48, 128), F32), vm((NG, 48, 128), F32),
        vm((8, 128), F32), vm((NB, 8, 128), F32), vm((COLS, 128), F32), vm((3, ST, 128), F32),
        dma((10,)), dma((NB,)), dma((2,)),
        dma((5, NB)), dma((5, NB)), dma((4, NG)), dma((4, NG)), dma((8,)), dma((8,)),
    ]
    flow_out, disp_out = pl.pallas_call(
        kernel,
        out_shape=(
            vm((NV, CX, CY), F32),
            vm((3, ST, 128), F32),
        ),
        in_specs=[hbm] * 11,
        out_specs=(hbm, hbm),
        scratch_shapes=scratch,
        compiler_params=pltpu.CompilerParams(
            collective_id=0, has_side_effects=True, vmem_limit_bytes=48 * 1024 * 1024
        ),
    )(*[
        stay(x) for x in (
            flow_state, jx, jy, slot_tile.reshape(1, -1), slot_cells, jnp.transpose(slot_normal, (1, 0, 2)), slot_rbf,
            jnp.transpose(disp_in, (1, 0, 2)), flex, jnp.transpose(secv, (0, 2, 1, 3)), jnp.transpose(secw, (0, 2, 1, 3)),
        )
    ])
    return flow_out, jnp.transpose(disp_out, (1, 0, 2))


def solution(mesh):
    placed = (
        P(None, "grp", "blk"), P(), P(),
        P(("grp", "blk")), P(("grp", "blk"), None),
        P(("grp", "blk"), None, None), P(("grp", "blk"), None, None),
        P("blk", None, None), P("blk", None, None),
        P(None, "blk", None, None), P(None, "blk", None, None),
    )
    return jax.shard_map(
        on_device, mesh=mesh, in_specs=placed,
        out_specs=(P(None, "grp", "blk"), P("blk", None, None)), check_vma=False,
    )
```

```python
import functools

import jax
import jax.numpy as jnp
from jax import lax
from jax.experimental import pallas as pl
from jax.experimental.pallas import tpu as pltpu
from jax.sharding import PartitionSpec as P

RATES = (0.25, 1.0 / 3.0, 0.5, 1.0)
TIME_STEP = 0.4
DAMPING = 0.25
FORCING = 1.0
F32 = jnp.float32
BF16 = jnp.bfloat16
MESH = pl.DeviceIdType.MESH
NG, NB = 8, 16
SEND, ST, COLS, NV = 4, 96, 24, 5
CX, CY = 128, 256
OWN = ST // NG
WIN = 16
HOPS = ((0, 1), (0, 3), (1, 0), (3, 0), (1, 1), (1, 3), (3, 1), (3, 3), (0, 2), (2, 0), (1, 2), (3, 2), (2, 1), (2, 3), (0, 0), (2, 2))
BACK = tuple(HOPS.index(((4 - dy) % 4, (4 - dz) % 4)) for dy, dz in HOPS)
ME = HOPS.index((0, 0))
CLASSES = ((0, 4), (4, 10), (10, 14), (15, 16))
NN = (((1,), (0,)), ((), ()))
NT = (((1,), (1,)), ((), ()))


def iota(shape, dim):
    return lax.broadcasted_iota(jnp.int32, shape, dim)


def dot(a, b, dims):
    return lax.dot_general(a, b, dims, preferred_element_type=F32)


def split(x):
    hi = x.astype(BF16)
    return hi, (x - hi.astype(F32)).astype(BF16)


def window(g):
    return lax.div(g * OWN, 8) * 8


def kernel(
    flow_h, jx_h, jy_h, tile_h, cells_h, normal_h, rbf_h, disp_h, flex_h, secv_h, secw_h,
    flow_o, disp_o,
    jx, jy, tile, cells, normal, rbf, disp, flex, secv, secw,
    force_q, qa, qb, qout, rows0, rows1, rows2,
    req, land_req, resp, land_disp, dispc, cellv, rall, bmat0, bmat1, bmat2, acc, pack,
    land_below, land_above, land_right, land_left, land_corner,
    nrm, norms, load_out, land_load, oht, part, land_part,
    flexhl, uwin, zmat, gsend, land_gg, gsum, land_gb, linv,
    rmsg, land_rg, tmsg, land_t, rsend, land_r, coef, dout,
    lsem, rsem, osem, bs, br, gs, gr, hs, hr,
):
    g = lax.axis_index("grp")
    b = lax.axis_index("blk")
    y, z = lax.div(b, 4), lax.rem(b, 4)
    a = pl.multiple_of(window(g), 8)
    off = g * OWN - window(g)

    def peer(o):
        return lax.rem(y + HOPS[o][0], 4) * 4 + lax.rem(z + HOPS[o][1], 4)

    loads = [
        (tile_h, tile),
        (cells_h, cells),
        (disp_h, disp),
        (secv_h.at[:, :, pl.ds(a, WIN), :], secv),
        (flow_h, force_q.at[:, pl.ds(8, CX), pl.ds(0, CY)]),
        (normal_h, normal),
        (flex_h.at[pl.ds(a, WIN)], flex),
        (jx_h, jx),
        (jy_h, jy),
        (secw_h, secw),
    ]
    loads = [pltpu.make_async_copy(s, d, lsem.at[i]) for i, (s, d) in enumerate(loads)]
    l_tile, l_cells, l_disp, l_secv, l_flow, l_normal, l_flex, l_jx, l_jy, l_secw = loads
    l_rbf = [
        pltpu.make_async_copy(rbf_h.at[pl.ds(peer(o) * SEND, SEND)], rbf.at[o], rsem.at[o]) for o in range(NB)
    ]
    l_tile.start()

    barrier = pltpu.get_barrier_semaphore()
    g_up, g_dn = lax.rem(g + 1, NG), lax.rem(g + NG - 1, NG)
    b_up, b_dn = lax.rem(b + 1, NB), lax.rem(b + NB - 1, NB)
    hello = [(g, peer(o)) for o in reversed(range(NB)) if o != ME]
    hello += [(g_dn, b_dn), (g_dn, b_up), (g_up, b_dn), (g_up, b_up)]
    hello += [(lax.rem(g + o, NG), b) for o in range(1, NG)]
    for dev in hello:
        pl.semaphore_signal(barrier, inc=1, device_id=dev, device_id_type=MESH)

    for c in loads[1:4] + l_rbf + loads[4:]:
        c.start()

    def blk_copy(src, land, ph, o):
        return pltpu.make_async_remote_copy(
            src_ref=src(o), dst_ref=land.at[BACK[o]], send_sem=bs.at[ph, o], recv_sem=br.at[ph, BACK[o]],
            device_id=(g, peer(o)), device_id_type=MESH,
        )

    def grp_copy(src, dst, ph, o, dev):
        return pltpu.make_async_remote_copy(
            src_ref=src, dst_ref=dst, send_sem=gs.at[ph, o], recv_sem=gr.at[ph, o],
            device_id=(dev, b), device_id_type=MESH,
        )

    def each(n, step):
        def body(o, _):
            step(o)
            return 0

        lax.fori_loop(1, n, body, 0)

    pending = []

    def finish():
        for wait in pending:
            wait()

    far_first = [o for o in reversed(range(NB)) if o != ME]

    def blk_send(src, land, ph, peers=far_first):
        for o in peers:
            copy = blk_copy(src, land, ph, o)
            copy.start()
            pending.append(copy.wait_send)

    def blk_recv(src, land, ph, peers=far_first[::-1]):
        for o in peers:
            pltpu.make_async_remote_copy(
                src_ref=src(o), dst_ref=land.at[o], send_sem=bs.at[ph, o], recv_sem=br.at[ph, o],
                device_id=(g, peer(o)), device_id_type=MESH,
            ).wait_recv()

    def grp_send(src, land, ph):
        def step(o):
            d = lax.rem(g + o, NG)
            grp_copy(src(d), land.at[g], ph, o, d).start()

        def last(o):
            grp_copy(src(0), land.at[0], ph, o, 0).wait_send()

        each(NG, step)
        pending.append(lambda: each(NG, last))

    def grp_recv(src, land, ph):
        def step(o):
            d = lax.rem(g + NG - o, NG)
            grp_copy(src(d), land.at[d], ph, o, d).wait_recv()

        each(NG, step)

    l_tile.wait()
    row = iota((NB * 16, 64), 0)
    hit = iota((NB * 16, 64), 1) == lax.shift_right_logical(row, 4) * SEND + (row & 3)
    wanted = jnp.sum(jnp.where(hit, tile[...].astype(F32), 0.0), axis=1, keepdims=True)
    row = iota((NB * 16, 128), 0)
    wanted = jnp.where((row & 15) < 12, jnp.broadcast_to(wanted, (NB * 16, 128)), -1.0)
    req[...] = wanted.reshape(NB, 16, 128)
    land_req[ME] = req[b]

    pl.semaphore_wait(barrier, len(hello))
    blk_send(lambda o: req.at[peer(o)], land_req, 0)

    l_cells.wait()
    for o in range(NB):
        cellv[o, 0:SEND, :] = cells[pl.ds(peer(o) * SEND, SEND), :]

    def rows_of(o, _):
        for j in range(SEND):
            cell = cellv[o, j : j + 1, :]
            r = (lax.shift_right_logical(cell, 7) & 1) * 128 + lax.shift_right_logical(cell, 8)
            one = jnp.where(iota((256, 128), 0) == r, 1.0, 0.0).astype(BF16)
            rall[o, :, 128 * j : 128 * (j + 1)] = one
            cellv[o, SEND + j : SEND + j + 1, :] = cell & 127
        return 0

    lax.fori_loop(0, NB, rows_of, 0)
    l_normal.wait()
    nrm[...] = jnp.zeros(nrm.shape, F32)
    for c in range(3):
        for j in range(SEND):
            nrm[pl.ds(4 * c + j, NB, stride=16), :] = normal[c, pl.ds(j, NB, stride=SEND), :]
    for o in range(NB):
        norms[o] = nrm[pl.ds(pl.multiple_of(peer(o) * 16, 16), 16), :]
    force_q[:, 0:8, :] = jnp.zeros((NV, 8, CY + 128), F32)
    force_q[:, 8 + CX : 16 + CX, :] = jnp.zeros((NV, 8, CY + 128), F32)
    force_q[:, 8 : 8 + CX, CY : CY + 128] = jnp.zeros((NV, CX, 128), F32)
    l_disp.wait()
    dispc[...] = jnp.zeros(dispc.shape, BF16)
    for c in range(3):
        dispc[128 * c : 128 * c + ST, :] = disp[c].astype(BF16)
    l_secv.wait()
    zero8 = jnp.zeros((8, 128), F32)

    def gram_row(i, _):
        for c in range(3):
            x = secv[:, c, pl.ds(i, 1), :].reshape(COLS, 128)
            x = jnp.where((i >= off) & (i < off + OWN), x, 0.0)
            hi, lo = split(jnp.concatenate([x, zero8], axis=0))
            at = pl.multiple_of((c * WIN + i) * 128, 128)
            zmat[0:32, pl.ds(at, 128)] = hi
            zmat[32:64, pl.ds(at, 128)] = lo
        return 0

    lax.fori_loop(0, WIN, gram_row, 0)
    zz = zmat[...]
    top = dot(zz, zz[0:32], NT)
    low = dot(zz, zz[32:64], NT)
    gram = top[0:32] + top[32:64] + low[0:32] + low[32:64]
    gsend[...] = jnp.zeros(gsend.shape, F32)
    gsend[:, 0:32] = gram
    land_gg[g] = gsend[...]
    grp_send(lambda d: gsend, land_gg, 0)

    def answer(first, last):
        n = (last - first) * 16
        asked = land_req[first:last].reshape(n, 128)
        row_c = lax.shift_right_logical(iota((n, 128), 0), 2) & 3
        found = asked == iota((n, 128), 1).astype(F32)
        pick = jnp.concatenate([jnp.where(found & (row_c == c), 1.0, 0.0).astype(BF16) for c in range(3)], axis=1)
        return dot(pick, dispc[...], NN).astype(BF16).reshape(last - first, 16, 128)

    land_disp[ME] = answer(ME, ME + 1)[0]
    for first, last in CLASSES:
        blk_recv(lambda o: req.at[peer(o)], land_req, 0, range(first, last))
        resp[first:last] = answer(first, last)
        blk_send(lambda o: resp.at[o], land_disp, 1, range(first, last))

    acc[...] = jnp.zeros(acc.shape, F32)
    bmats = (bmat0, bmat1, bmat2)

    def spread(first):
        for h in range(2):
            o = dot(land_disp[first + h], rbf[first + h].reshape(SEND * 128, 128), NT) * FORCING
            high = o.astype(BF16).astype(F32)
            low = o - high
            for j in range(SEND):
                mask = iota((128, 128), 0) == cellv[first + h, SEND + j : SEND + j + 1, :]
                at = 512 * h + 128 * j
                for c in range(3):
                    vh = high[4 * c + j : 4 * c + j + 1, 128 * j : 128 * (j + 1)]
                    vl = low[4 * c + j : 4 * c + j + 1, 128 * j : 128 * (j + 1)]
                    bmats[c][0:128, at : at + 128] = jnp.where(mask, vh, 0.0).astype(BF16)
                    bmats[c][128:256, at : at + 128] = jnp.where(mask, vl, 0.0).astype(BF16)
        for c in range(3):
            acc[c] += dot(bmats[c][:, 0:512], rall[first], NT) + dot(bmats[c][:, 512:1024], rall[first + 1], NT)

    def spread_pair(p, _):
        spread(2 * p)
        return 0

    for first, last in CLASSES:
        blk_recv(lambda o: resp.at[o], land_disp, 1, range(first, last))
        for o in range(first, last):
            l_rbf[o].wait()
        if last == NB:
            l_rbf[ME].wait()
        lax.fori_loop(first // 2, NB // 2 if last == NB else last // 2, spread_pair, 0)
    l_flow.wait()
    for c in range(3):
        s = acc[c, 0:128, :] + acc[c, 128:256, :]
        force_q[1 + c, 8 : 8 + CX, 0:128] += s[:, 0:128].T
        force_q[1 + c, 8 : 8 + CX, 128:256] += s[:, 128:256].T

    lane = iota((128, 128), 1)
    strip = lax.shift_right_logical((lane + 4) & 127, 3)
    packed = jnp.zeros((128, 128), F32)
    for v in range(NV):
        t = jnp.where(lane < 64, force_q[v, 8 : 8 + CX, 0:128], force_q[v, 8 : 8 + CX, 128:256])
        if v:
            t = pltpu.roll(t, 8 * v, 1)
        packed = jnp.where(strip == v, t, packed)
    lane64 = iota((64, 128), 1)
    pack[...] = jnp.where(((lane64 + 4) & 127) < 64, packed[0:64], pltpu.roll(packed[64:128], 64, 1))
    top_rows = force_q.at[:, pl.ds(8, 8), pl.ds(0, CY)]
    low_rows = force_q.at[:, pl.ds(CX, 8), pl.ds(0, CY)]
    halo = [
        (pack.at[pl.ds(0, 8)], land_corner.at[0], (g_dn, b_dn)),
        (pack.at[pl.ds(0, 8)], land_corner.at[1], (g_dn, b_up)),
        (pack.at[pl.ds(56, 8)], land_corner.at[2], (g_up, b_dn)),
        (pack.at[pl.ds(56, 8)], land_corner.at[3], (g_up, b_up)),
        (pack, land_right, (g, b_dn)),
        (pack, land_left, (g, b_up)),
        (top_rows, land_below, (g_dn, b)),
        (low_rows, land_above, (g_up, b)),
    ]
    halo = [
        pltpu.make_async_remote_copy(
            src_ref=s, dst_ref=d, send_sem=hs.at[i], recv_sem=hr.at[i], device_id=dev, device_id_type=MESH
        )
        for i, (s, d, dev) in enumerate(halo)
    ]
    for c in halo:
        c.start()
        pending.append(c.wait_send)

    grp_recv(lambda d: gsend, land_gg, 0)
    gsum[...] = jnp.sum(land_gg[...], axis=0)
    land_gb[ME] = gsum[...]
    blk_send(lambda o: gsum, land_gb, 2)
    is_up, is_dn = g < NG - 1, g > 0
    is_right, is_left = b < NB - 1, b > 0
    l_jx.wait()
    l_jy.wait()
    lane = iota((8, CY + 128), 1)
    sub = iota((8, CY + 128), 0)
    outside = ((lane >= CY) & (lane < CY + 64) & jnp.logical_not(is_right)) | (
        (lane >= CY + 64) & jnp.logical_not(is_left)
    )
    inside = jnp.where(outside, 0.0, TIME_STEP).astype(F32)
    ax = [[-0.5 * jx[u, v] for v in range(NV)] for u in range(NV)]
    ay = [[-0.5 * jy[u, v] for v in range(NV)] for u in range(NV)]

    def advance(cur, up, dn, rt, lt, start, scale):
        dx = [p - m for p, m in zip(up, dn)]
        dy = [p - m for p, m in zip(rt, lt)]
        out = []
        for u in range(NV):
            res = DAMPING * ((up[u] + dn[u]) + (rt[u] + lt[u])) - 4.0 * DAMPING * cur[u]
            for v in range(NV):
                res = res + (ax[u][v] * dx[v] + ay[u][v] * dy[v])
            out.append(start[u] + scale * res)
        return out

    def step(cur, prev, nxt, start, scale):
        up = [pltpu.roll(jnp.where(sub == 0, n, q), 7, 0) for n, q in zip(nxt, cur)]
        dn = [pltpu.roll(jnp.where(sub == 7, p, q), 1, 0) for p, q in zip(prev, cur)]
        rt = [pltpu.roll(q, CY + 127, 1) for q in cur]
        lt = [pltpu.roll(q, 1, 1) for q in cur]
        return advance(cur, up, dn, rt, lt, start, scale)

    def rows_at(ref, i):
        r = pl.multiple_of(i * 8, 8)
        return [ref[v, pl.ds(r, 8), :] for v in range(NV)]

    def stage(src, dst, rate, last):
        def tile_at(i):
            row_ok = jnp.where(i == 0, is_dn, jnp.where(i == 17, is_up, True))
            scale = jnp.where(row_ok, rate, 0.0).astype(F32) * inside
            prev, nxt = rows_at(src, jnp.maximum(i - 1, 0)), rows_at(src, jnp.minimum(i + 1, 17))
            new = step(rows_at(src, i), prev, nxt, rows_at(force_q, i), scale)
            for u in range(NV):
                if last:
                    qout[u, pl.ds(pl.multiple_of(i * 8 - 8, 8), 8), :] = new[u][:, 0:CY]
                else:
                    dst[u, pl.ds(pl.multiple_of(i * 8, 8), 8), :] = new[u]

        width = 4 if last else 6

        def body(p, _):
            for t in range(width):
                tile_at(width * p + t + (1 if last else 0))
            return 0

        lax.fori_loop(0, 4 if last else 3, body, 0)

    stage(force_q, qa, RATES[0], False)
    stage(qa, qb, RATES[1], False)
    stage(qb, qa, RATES[2], False)
    stage(qa, None, RATES[3], True)

    for c in halo:
        c.wait_recv()
    zero = jnp.zeros((8, CY + 128), F32)
    zero128 = jnp.zeros((8, 128), F32)

    def wide(x, ok):
        return jnp.concatenate([jnp.where(ok, x, 0.0), zero128], axis=1)

    start = [
        [wide(land_above[v], is_dn) for v in range(NV)],
        [zero] * NV,
        [zero] * NV,
        [wide(land_below[v], is_up) for v in range(NV)],
    ]
    for t in (0, 3):
        for v in range(NV):
            rows0[v, 8 * t : 8 * t + 8, :] = start[t][v]
    nothing = [zero] * NV
    for i, rate in enumerate(RATES):
        src, dst = ((rows0, rows1), (rows1, rows2), (rows2, rows1), (rows1, None))[i]
        for t in (1, 2) if dst is None else range(4):
            def at(k):
                if i == 0 and k in (1, 2):
                    return nothing
                return [src[v, 8 * k : 8 * k + 8, :] for v in range(NV)]

            first = [rows0[v, 8 * t : 8 * t + 8, :] for v in range(NV)] if t in (0, 3) else nothing
            scale = rate * inside
            if t in (0, 3):
                scale = jnp.where(is_dn if t == 0 else is_up, scale, 0.0)
            new = step(at(t), at(t - 1) if t in (1, 3) else nothing, at(t + 1) if t in (0, 2) else nothing, first, scale)
            for u in range(NV):
                if dst is None:
                    r = 0 if t == 1 else CX - 8
                    qout[u, r : r + 8, :] += new[u][:, 0:CY]
                else:
                    dst[u, 8 * t : 8 * t + 8, :] = new[u]

    def sides(right, left, ok):
        from_right = (iota(right.shape, 1) & 7) < 4
        return jnp.where(from_right, jnp.where(is_right & ok, right, 0.0), jnp.where(is_left & ok, left, 0.0))

    mid = sides(land_right[...], land_left[...], True)
    mid = jnp.concatenate([mid, pltpu.roll(mid, 64, 1)], axis=0)
    below = sides(land_corner[0], land_corner[1], is_up)
    above = pltpu.roll(sides(land_corner[2], land_corner[3], is_dn), 64, 1)
    ends = jnp.concatenate([below, jnp.zeros((112, 128), F32), above], axis=0)
    strips = pltpu.roll(jnp.concatenate([mid.T, ends.T], axis=1), 4, 0)
    sub2 = iota((8, 256), 0)
    lane2 = iota((8, 256), 1)
    out_rows = ((lane2 >= 128) & (lane2 < 192) & jnp.logical_not(is_up)) | ((lane2 >= 192) & jnp.logical_not(is_dn))
    inside2 = jnp.where(out_rows, 0.0, TIME_STEP).astype(F32)
    done = []
    for near_side in (True, False):
        start = []
        for v in range(NV):
            x = strips[8 * v : 8 * v + 8]
            start.append(jnp.where((sub2 < 4) == near_side, x, 0.0))
        cur = start
        for rate in RATES:
            up = [pltpu.roll(q, 255, 1) for q in cur]
            dn = [pltpu.roll(q, 1, 1) for q in cur]
            rt = [jnp.where(sub2 == 7, 0.0, pltpu.roll(q, 7, 0)) for q in cur]
            lt = [jnp.where(sub2 == 0, 0.0, pltpu.roll(q, 1, 0)) for q in cur]
            cur = advance(cur, up, dn, rt, lt, start, rate * inside2)
        done.append([q[:, 0:128] for q in cur])
    sub1 = iota((8, 128), 0)
    joined = [jnp.where(sub1 < 4, far, near) for near, far in zip(*done)]
    joined = jnp.concatenate(joined + [jnp.zeros((128 - 8 * NV, 128), F32)], axis=0).T
    lane1 = iota((128, 128), 1)
    for v in range(NV):
        x = pltpu.roll(joined, (124 - 8 * v) % 128, 1)
        qout[v, :, 0:128] += jnp.where(lane1 < 4, x, 0.0)
        qout[v, :, 128:256] += jnp.where(lane1 >= 124, x, 0.0)
    flow_out = pltpu.make_async_copy(qout, flow_o, osem.at[0])
    flow_out.start()
    pending.append(flow_out.wait)

    pres = qout[4]
    pres = jnp.concatenate([pres[:, 0:128].T, pres[:, 128:256].T], axis=1)
    ph, plow = split(pres)
    pres2 = jnp.concatenate([ph, plow], axis=0)
    row16 = iota((16, 128), 0)

    def gather(o):
        h = dot(pres2, rall[o], NN)
        h = h[0:128] + h[128:256]
        n16 = norms[o]
        forces = []
        for j in range(SEND):
            mask = iota((128, 128), 0) == cellv[o, SEND + j : SEND + j + 1, :]
            p = jnp.sum(jnp.where(mask, h[:, 128 * j : 128 * (j + 1)], 0.0), axis=0, keepdims=True)
            forces.append(jnp.where((row16 & 3) == j, n16 * p, 0.0).astype(BF16))
        return dot(jnp.concatenate(forces, axis=1), rbf[o].reshape(SEND * 128, 128), NN)

    def gather_pair(p, _):
        one, two = gather(2 * p), gather(2 * p + 1)
        load_out[2 * p] = one
        load_out[2 * p + 1] = two
        return 0


    for first, last in CLASSES[::-1]:
        lax.fori_loop(first // 2, NB // 2 if last == NB else last // 2, gather_pair, 0)
        blk_send(lambda o: load_out.at[o], land_load, 3, range(first, last))
    land_load[ME] = load_out[ME]

    blk_recv(lambda o: gsum, land_gb, 2)
    gram = jnp.sum(land_gb[...], axis=0)[0:COLS]
    row = iota((COLS, 128), 0)
    lane = iota((COLS, 128), 1)
    m = jnp.where(lane < COLS, gram, jnp.where(lane == row + 32, 1.0, 0.0))
    fac = jnp.zeros((COLS, 128), F32)
    for k in range(COLS):
        pivot = lax.rsqrt(jnp.broadcast_to(m[k : k + 1, k : k + 1], (1, 128)))
        r = m[k : k + 1, :] * pivot
        col = jnp.broadcast_to(m[:, k : k + 1], (COLS, 128)) * pivot
        fac = jnp.where(row == k, r, fac)
        m = m - jnp.where(row > k, col * r, 0.0)
    linv[...] = jnp.where((lane >= 32) & (lane < 32 + COLS), fac, 0.0)
    wrow = iota((48, 128), 0) & 15
    mine = (wrow >= off) & (wrow < off + OWN)
    d_in = jnp.where(mine, disp[:, pl.ds(a, WIN), :].reshape(48, 128), 0.0)
    rhs_in = jnp.sum(secv[...].reshape(COLS, 48, 128) * d_in[None], axis=1)
    diag = lane == row + 32

    asked_t = land_req[...].reshape(NB * 16, 128).T[0:1, :]
    rr, kk = iota((48, NB * 16), 0), iota((48, NB * 16), 1)
    w = rr & 15
    same_c = (lax.shift_right_logical(kk, 2) & 3) == lax.shift_right_logical(rr, 4)
    for p in range(NG):
        first = (p * OWN) // 8 * 8
        skip = p * OWN - first
        ok = same_c & (w >= skip) & (w < skip + OWN)
        oht[48 * p : 48 * (p + 1), :] = jnp.where(ok & (asked_t == (w + first).astype(F32)), 1.0, 0.0).astype(BF16)

    blk_recv(lambda o: load_out.at[o], land_load, 3)
    got = land_load[...].reshape(NB * 16, 128)
    hi, lo = split(got)
    sums = dot(oht[...], jnp.concatenate([hi, lo], axis=1), NN)
    part[...] = (sums[:, 0:128] + sums[:, 128:256]).reshape(NG, 48, 128)
    land_part[g] = part[g]
    grp_send(lambda d: part.at[d], land_part, 1)
    l_flex.wait()

    def project(i, _):
        at = pl.multiple_of(128 * i, 128)
        hi, lo = split(flex[i])
        flexhl[pl.ds(at, 128), 0:128] = hi
        flexhl[pl.ds(at, 128), 128:256] = lo
        vh, vl = split(jnp.concatenate([secv[:, c, pl.ds(i, 1), :].reshape(COLS, 128) for c in range(3)], axis=0))
        u = dot(jnp.concatenate([vh, vl], axis=0), hi, NN)
        u = u[0:72] + u[72:144] + dot(vh, lo, NN)
        for c in range(3):
            uwin[:, c, pl.ds(i, 1), :] = u[COLS * c : COLS * (c + 1)].reshape(COLS, 1, 128)
        return 0

    lax.fori_loop(0, WIN, project, 0)
    grp_recv(lambda d: part.at[d], land_part, 1)
    tile_loads = jnp.sum(land_part[...], axis=0)

    prod = jnp.sum(uwin[...].reshape(COLS, 48, 128) * tile_loads[None], axis=1) - rhs_in
    rhs = jnp.sum(prod, axis=1, keepdims=True)
    rhs = jnp.sum(jnp.where(diag, rhs, 0.0), axis=0, keepdims=True)
    rmsg[...] = jnp.broadcast_to(rhs, (8, 128))
    land_rg[g] = rmsg[...]
    grp_send(lambda d: rmsg, land_rg, 2)
    hi, lo = split(tile_loads)
    lhs = jnp.concatenate(
        [jnp.concatenate([hi, hi], axis=1), jnp.concatenate([lo, jnp.zeros_like(lo)], axis=1)], axis=0
    )
    tilde = jnp.zeros((48, 128), F32)
    for u in range(WIN // 2):
        o = dot(lhs, flexhl[256 * u : 256 * (u + 1), :], NT)
        o = o[0:48] + o[48:96]
        tilde = jnp.where(wrow == 2 * u, o[:, 0:128], tilde)
        tilde = jnp.where(wrow == 2 * u + 1, o[:, 128:256], tilde)
    tmsg[...] = jnp.where(mine, tilde, 0.0)
    land_t[g] = tmsg[...]
    grp_send(lambda d: tmsg, land_t, 3)
    grp_recv(lambda d: rmsg, land_rg, 2)
    rsend[...] = jnp.sum(land_rg[...], axis=0)
    land_r[ME] = rsend[...]
    blk_send(lambda o: rsend, land_r, 4)
    l_secw.wait()
    grp_recv(lambda d: tmsg, land_t, 3)
    blk_recv(lambda o: rsend, land_r, 4)
    rhs = jnp.sum(land_r[...], axis=0)[0:1]

    li = linv[...]
    y = jnp.sum(li * rhs, axis=1, keepdims=True)
    x = jnp.sum(li * y, axis=0, keepdims=True)
    x = -jnp.sum(jnp.where(diag, x, 0.0), axis=1, keepdims=True)
    coef[...] = jnp.broadcast_to(x, (COLS, 128))

    def update(p, _):
        for c in range(3):
            even, odd = land_t[2 * p, 16 * c : 16 * c + 16, :], land_t[2 * p + 1, 16 * c : 16 * c + 16, :]
            for q, t in enumerate((even[0:8], even[8:16] + odd[0:8], odd[8:16])):
                at = pl.multiple_of(24 * p + 8 * q, 8)
                for k in range(COLS):
                    t = t + coef[k : k + 1, :] * secw[k, c, pl.ds(at, 8), :]
                dout[c, pl.ds(at, 8), :] = t
        return 0

    lax.fori_loop(0, NG // 2, update, 0)
    disp_out = pltpu.make_async_copy(dout, disp_o, osem.at[1])
    disp_out.start()
    pending.append(disp_out.wait)

    finish()


def stay(x):
    return pltpu.with_memory_space_constraint(x, pltpu.HBM)


def on_device(flow_state, jx, jy, slot_tile, slot_cells, slot_normal, slot_rbf, disp_in, flex, secv, secw):
    hbm = pl.BlockSpec(memory_space=pl.ANY)
    vm, dma = pltpu.VMEM, pltpu.SemaphoreType.DMA
    state = (NV, CX + 16, CY + 128)
    scratch = [
        pltpu.SMEM((NV, NV), F32), pltpu.SMEM((NV, NV), F32),
        vm((1, 64), jnp.int32), vm((64, 128), jnp.int32), vm((3, 64, 128), F32), vm((NB, SEND, 128, 128), BF16),
        vm((3, ST, 128), F32), vm((WIN, 128, 128), F32), vm((COLS, 3, WIN, 128), F32), vm((COLS, 3, ST, 128), F32),
        vm(state, F32), vm(state, F32), vm(state, F32), vm((NV, CX, CY), F32),
        vm((NV, 32, CY + 128), F32), vm((NV, 32, CY + 128), F32), vm((NV, 32, CY + 128), F32),
        vm((NB, 16, 128), F32), vm((NB, 16, 128), F32), vm((NB, 16, 128), BF16), vm((NB, 16, 128), BF16),
        vm((384, 128), BF16),
        vm((NB, 8, 128), jnp.int32), vm((NB, 256, 512), BF16),
        vm((256, 1024), BF16), vm((256, 1024), BF16), vm((256, 1024), BF16), vm((3, 256, 256), F32),
        vm((64, 128), F32),
        vm((NV, 8, CY), F32), vm((NV, 8, CY), F32), vm((64, 128), F32), vm((64, 128), F32), vm((4, 8, 128), F32),
        vm((256, 128), F32), vm((NB, 16, 128), F32), vm((NB, 16, 128), F32), vm((NB, 16, 128), F32), vm((384, 256), BF16),
        vm((NG, 48, 128), F32), vm((NG, 48, 128), F32),
        vm((WIN * 128, 256), BF16), vm((COLS, 3, WIN, 128), F32), vm((64, 48 * 128), BF16),
        vm((32, 128), F32), vm((NG, 32, 128), F32), vm((32, 128), F32), vm((NB, 32, 128), F32), vm((COLS, 128), F32),
        vm((8, 128), F32), vm((NG, 8, 128), F32), vm((48, 128), F32), vm((NG, 48, 128), F32),
        vm((8, 128), F32), vm((NB, 8, 128), F32), vm((COLS, 128), F32), vm((3, ST, 128), F32),
        dma((10,)), dma((NB,)), dma((2,)),
        dma((5, NB)), dma((5, NB)), dma((4, NG)), dma((4, NG)), dma((8,)), dma((8,)),
    ]
    flow_out, disp_out = pl.pallas_call(
        kernel,
        out_shape=(
            vm((NV, CX, CY), F32),
            vm((3, ST, 128), F32),
        ),
        in_specs=[hbm] * 11,
        out_specs=(hbm, hbm),
        scratch_shapes=scratch,
        compiler_params=pltpu.CompilerParams(
            collective_id=0, has_side_effects=True, vmem_limit_bytes=48 * 1024 * 1024
        ),
    )(*[
        stay(x) for x in (
            flow_state, jx, jy, slot_tile.reshape(1, -1), slot_cells, jnp.transpose(slot_normal, (1, 0, 2)), slot_rbf,
            jnp.transpose(disp_in, (1, 0, 2)), flex, jnp.transpose(secv, (0, 2, 1, 3)), jnp.transpose(secw, (0, 2, 1, 3)),
        )
    ])
    return flow_out, jnp.transpose(disp_out, (1, 0, 2))


def solution(mesh):
    placed = (
        P(None, "grp", "blk"), P(), P(),
        P(("grp", "blk")), P(("grp", "blk"), None),
        P(("grp", "blk"), None, None), P(("grp", "blk"), None, None),
        P("blk", None, None), P("blk", None, None),
        P(None, "blk", None, None), P(None, "blk", None, None),
    )
    return jax.shard_map(
        on_device, mesh=mesh, in_specs=placed,
        out_specs=(P(None, "grp", "blk"), P("blk", None, None)), check_vma=False,
    )
```

```python
import functools

import jax
import jax.numpy as jnp
from jax import lax
from jax.experimental import pallas as pl
from jax.experimental.pallas import tpu as pltpu
from jax.sharding import PartitionSpec as P

RATES = (0.25, 1.0 / 3.0, 0.5, 1.0)
TIME_STEP = 0.4
DAMPING = 0.25
FORCING = 1.0
F32 = jnp.float32
BF16 = jnp.bfloat16
MESH = pl.DeviceIdType.MESH
NG, NB = 8, 16
SEND, ST, COLS, NV = 4, 96, 24, 5
CX, CY = 128, 256
OWN = ST // NG
WIN = 16
HOPS = ((0, 0), (0, 1), (0, 3), (1, 0), (3, 0), (1, 1), (1, 3), (3, 1), (3, 3), (0, 2), (2, 0), (1, 2), (3, 2), (2, 1), (2, 3), (2, 2))
BACK = tuple(HOPS.index(((4 - dy) % 4, (4 - dz) % 4)) for dy, dz in HOPS)
ME = HOPS.index((0, 0))
CLASSES = ((1, 5), (5, 11), (11, 15))
FAR = NB - 1
NN = (((1,), (0,)), ((), ()))
NT = (((1,), (1,)), ((), ()))


def iota(shape, dim):
    return lax.broadcasted_iota(jnp.int32, shape, dim)


def dot(a, b, dims):
    return lax.dot_general(a, b, dims, preferred_element_type=F32)


def split(x):
    hi = x.astype(BF16)
    return hi, (x - hi.astype(F32)).astype(BF16)


def window(g):
    return lax.div(g * OWN, 8) * 8


def kernel(
    flow_h, jx_h, jy_h, tile_h, cells_h, normal_h, rbf_h, disp_h, flex_h, secv_h, secw_h,
    flow_o, disp_o,
    jx, jy, tile, cells, normal, rbf, disp, flex, secv, secw,
    force_q, qa, qb, qout, rows0, rows1, rows2,
    req, land_req, resp, land_disp, dispc, cellv, rall, bmat, acc, table, pack,
    land_below, land_above, land_right, land_left, land_corner,
    nrm, norms, load_out, land_load, oht, part, land_part,
    flexhl, uwin, zmat, gsend, land_gg, gsum, land_gb, linv,
    rmsg, land_rg, tmsg, land_t, rsend, land_r, coef, dout,
    lsem, rsem, osem, bs, br, gs, gr, hs, hr,
):
    g = lax.axis_index("grp")
    b = lax.axis_index("blk")
    y, z = lax.div(b, 4), lax.rem(b, 4)
    a = pl.multiple_of(window(g), 8)
    off = g * OWN - window(g)

    def peer(o):
        return lax.rem(y + HOPS[o][0], 4) * 4 + lax.rem(z + HOPS[o][1], 4)

    loads = [
        (tile_h, tile),
        (cells_h, cells),
        (disp_h, disp),
        (secv_h.at[:, :, pl.ds(a, WIN), :], secv),
        (flow_h, force_q.at[:, pl.ds(8, CX), pl.ds(0, CY)]),
        (normal_h, normal),
        (flex_h.at[pl.ds(a, WIN)], flex),
        (jx_h, jx),
        (jy_h, jy),
        (secw_h, secw),
    ]
    loads = [pltpu.make_async_copy(s, d, lsem.at[i]) for i, (s, d) in enumerate(loads)]
    l_tile, l_cells, l_disp, l_secv, l_flow, l_normal, l_flex, l_jx, l_jy, l_secw = loads
    l_rbf = [
        pltpu.make_async_copy(rbf_h.at[pl.ds(peer(o) * SEND, SEND)], rbf.at[o], rsem.at[o]) for o in range(NB)
    ]
    l_tile.start()

    barrier = pltpu.get_barrier_semaphore()
    g_up, g_dn = lax.rem(g + 1, NG), lax.rem(g + NG - 1, NG)
    b_up, b_dn = lax.rem(b + 1, NB), lax.rem(b + NB - 1, NB)
    hello = [(g, peer(o)) for o in reversed(range(NB)) if o != ME]
    hello += [(g_dn, b_dn), (g_dn, b_up), (g_up, b_dn), (g_up, b_up)]
    hello += [(lax.rem(g + o, NG), b) for o in range(1, NG)]
    for dev in hello:
        pl.semaphore_signal(barrier, inc=1, device_id=dev, device_id_type=MESH)

    for c in loads[1:4] + l_rbf + loads[4:]:
        c.start()

    def blk_copy(src, land, ph, o):
        return pltpu.make_async_remote_copy(
            src_ref=src(o), dst_ref=land.at[BACK[o]], send_sem=bs.at[ph, o], recv_sem=br.at[ph, BACK[o]],
            device_id=(g, peer(o)), device_id_type=MESH,
        )

    def grp_copy(src, dst, ph, o, dev):
        return pltpu.make_async_remote_copy(
            src_ref=src, dst_ref=dst, send_sem=gs.at[ph, o], recv_sem=gr.at[ph, o],
            device_id=(dev, b), device_id_type=MESH,
        )

    def each(n, step):
        def body(o, _):
            step(o)
            return 0

        lax.fori_loop(1, n, body, 0)

    pending = []

    def finish():
        for wait in pending:
            wait()

    far_first = [o for o in reversed(range(NB)) if o != ME]

    def blk_send(src, land, ph, peers=far_first):
        for o in peers:
            copy = blk_copy(src, land, ph, o)
            copy.start()
            pending.append(copy.wait_send)

    def blk_recv(src, land, ph, peers=far_first[::-1]):
        for o in peers:
            pltpu.make_async_remote_copy(
                src_ref=src(o), dst_ref=land.at[o], send_sem=bs.at[ph, o], recv_sem=br.at[ph, o],
                device_id=(g, peer(o)), device_id_type=MESH,
            ).wait_recv()

    def grp_send(src, land, ph):
        def step(o):
            d = lax.rem(g + o, NG)
            grp_copy(src(d), land.at[g], ph, o, d).start()

        def last(o):
            grp_copy(src(0), land.at[0], ph, o, 0).wait_send()

        each(NG, step)
        pending.append(lambda: each(NG, last))

    def grp_recv(src, land, ph):
        def step(o):
            d = lax.rem(g + NG - o, NG)
            grp_copy(src(d), land.at[d], ph, o, d).wait_recv()

        each(NG, step)

    l_tile.wait()
    row = iota((NB * 16, 64), 0)
    hit = iota((NB * 16, 64), 1) == lax.shift_right_logical(row, 4) * SEND + (row & 3)
    wanted = jnp.sum(jnp.where(hit, tile[...].astype(F32), 0.0), axis=1, keepdims=True)
    row = iota((NB * 16, 128), 0)
    wanted = jnp.where((row & 15) < 12, jnp.broadcast_to(wanted, (NB * 16, 128)), -1.0)
    req[...] = wanted.reshape(NB, 16, 128)
    land_req[ME] = req[b]

    pl.semaphore_wait(barrier, len(hello))
    blk_send(lambda o: req.at[peer(o)], land_req, 0)

    l_disp.wait()
    dispc[...] = jnp.zeros(dispc.shape, BF16)
    for c in range(3):
        dispc[128 * c : 128 * c + ST, :] = disp[c].astype(BF16)
    to_far = pltpu.make_async_remote_copy(
        src_ref=dispc, dst_ref=table, send_sem=osem.at[2], recv_sem=osem.at[3],
        device_id=(g, peer(FAR)), device_id_type=MESH,
    )
    to_far.start()
    pending.append(to_far.wait_send)

    l_cells.wait()
    for o in range(NB):
        cellv[o, 0:SEND, :] = cells[pl.ds(peer(o) * SEND, SEND), :]

    def rows_of(p, _):
        for i in range(4):
            for j in range(SEND):
                cell = cellv[4 * p + i, j : j + 1, :]
                r = (lax.shift_right_logical(cell, 7) & 1) * 128 + lax.shift_right_logical(cell, 8)
                one = jnp.where(iota((256, 128), 0) == r, 1.0, 0.0).astype(BF16)
                rall[p, :, 512 * i + 128 * j : 512 * i + 128 * (j + 1)] = one
                cellv[4 * p + i, SEND + j : SEND + j + 1, :] = cell & 127
        return 0

    lax.fori_loop(0, 4, rows_of, 0)
    l_normal.wait()
    nrm[...] = jnp.zeros(nrm.shape, F32)
    for c in range(3):
        for j in range(SEND):
            nrm[pl.ds(4 * c + j, NB, stride=16), :] = normal[c, pl.ds(j, NB, stride=SEND), :]
    for o in range(NB):
        norms[o] = nrm[pl.ds(pl.multiple_of(peer(o) * 16, 16), 16), :]
    force_q[:, 0:8, :] = jnp.zeros((NV, 8, CY + 128), F32)
    force_q[:, 8 + CX : 16 + CX, :] = jnp.zeros((NV, 8, CY + 128), F32)
    force_q[:, 8 : 8 + CX, CY : CY + 128] = jnp.zeros((NV, CX, 128), F32)
    def answer(asked, shown):
        n = asked.shape[0] * 16
        asked = asked.reshape(n, 128)
        row_c = lax.shift_right_logical(iota((n, 128), 0), 2) & 3
        found = asked == iota((n, 128), 1).astype(F32)
        pick = jnp.concatenate([jnp.where(found & (row_c == c), 1.0, 0.0).astype(BF16) for c in range(3)], axis=1)
        return dot(pick, shown, NN).astype(BF16).reshape(n // 16, 16, 128)

    land_disp[ME] = answer(land_req[ME][None], dispc[...])[0]
    for first, last in CLASSES:
        blk_recv(lambda o: req.at[peer(o)], land_req, 0, range(first, last))
        resp[first:last] = answer(land_req[first:last], dispc[...])
        blk_send(lambda o: resp.at[o], land_disp, 1, range(first, last))
    to_far.wait_recv()
    land_disp[FAR] = answer(req[peer(FAR)][None], table[...])[0]

    acc[...] = jnp.zeros(acc.shape, F32)
    none16 = jnp.zeros((16, 128), BF16)

    def spread(p, _):
        for i in range(4):
            o = 4 * p + i

            @pl.when((o != ME) & (o != FAR))
            def _():
                pltpu.make_async_remote_copy(
                    src_ref=resp.at[o], dst_ref=land_disp.at[o], send_sem=bs.at[1, o], recv_sem=br.at[1, o],
                    device_id=(g, peer(FAR)), device_id_type=MESH,
                ).wait_recv()

            pltpu.make_async_copy(rbf_h.at[pl.ds(0, SEND)], rbf.at[o], rsem.at[o]).wait()
        for h in (0, 2):
            o = 4 * p + h
            x = jnp.concatenate(
                [
                    jnp.concatenate([land_disp[o], none16], axis=1),
                    jnp.concatenate([none16, land_disp[o + 1]], axis=1),
                ],
                axis=0,
            )
            weights = [rbf[o + i].reshape(SEND * 128, 128) for i in range(2)]
            moved = dot(x, jnp.concatenate(weights, axis=1), NT) * FORCING
            high = moved.astype(BF16).astype(F32)
            low = moved - high
            for i in range(2):
                for j in range(SEND):
                    mask = iota((128, 128), 0) == cellv[o + i, SEND + j : SEND + j + 1, :]
                    at = 512 * (h + i) + 128 * j
                    for c in range(3):
                        r = 16 * i + 4 * c + j
                        vh = high[r : r + 1, 128 * j : 128 * (j + 1)]
                        vl = low[r : r + 1, 128 * j : 128 * (j + 1)]
                        bmat[256 * c : 256 * c + 128, at : at + 128] = jnp.where(mask, vh, 0.0).astype(BF16)
                        bmat[256 * c + 128 : 256 * c + 256, at : at + 128] = jnp.where(mask, vl, 0.0).astype(BF16)
        acc[...] += dot(bmat[...], rall[p], NT)
        return 0

    lax.fori_loop(0, 4, spread, 0)
    l_flow.wait()
    for c in range(3):
        s = acc[256 * c : 256 * c + 128, :] + acc[256 * c + 128 : 256 * c + 256, :]
        force_q[1 + c, 8 : 8 + CX, 0:128] += s[:, 0:128].T
        force_q[1 + c, 8 : 8 + CX, 128:256] += s[:, 128:256].T

    lane = iota((128, 128), 1)
    strip = lax.shift_right_logical((lane + 4) & 127, 3)
    packed = jnp.zeros((128, 128), F32)
    for v in range(NV):
        t = jnp.where(lane < 64, force_q[v, 8 : 8 + CX, 0:128], force_q[v, 8 : 8 + CX, 128:256])
        if v:
            t = pltpu.roll(t, 8 * v, 1)
        packed = jnp.where(strip == v, t, packed)
    lane64 = iota((64, 128), 1)
    pack[...] = jnp.where(((lane64 + 4) & 127) < 64, packed[0:64], pltpu.roll(packed[64:128], 64, 1))
    top_rows = force_q.at[:, pl.ds(8, 8), pl.ds(0, CY)]
    low_rows = force_q.at[:, pl.ds(CX, 8), pl.ds(0, CY)]
    halo = [
        (pack.at[pl.ds(0, 8)], land_corner.at[0], (g_dn, b_dn)),
        (pack.at[pl.ds(0, 8)], land_corner.at[1], (g_dn, b_up)),
        (pack.at[pl.ds(56, 8)], land_corner.at[2], (g_up, b_dn)),
        (pack.at[pl.ds(56, 8)], land_corner.at[3], (g_up, b_up)),
        (pack, land_right, (g, b_dn)),
        (pack, land_left, (g, b_up)),
        (top_rows, land_below, (g_dn, b)),
        (low_rows, land_above, (g_up, b)),
    ]
    halo = [
        pltpu.make_async_remote_copy(
            src_ref=s, dst_ref=d, send_sem=hs.at[i], recv_sem=hr.at[i], device_id=dev, device_id_type=MESH
        )
        for i, (s, d, dev) in enumerate(halo)
    ]
    for c in halo:
        c.start()
        pending.append(c.wait_send)

    is_up, is_dn = g < NG - 1, g > 0
    is_right, is_left = b < NB - 1, b > 0
    l_jx.wait()
    l_jy.wait()
    lane = iota((8, CY + 128), 1)
    sub = iota((8, CY + 128), 0)
    outside = ((lane >= CY) & (lane < CY + 64) & jnp.logical_not(is_right)) | (
        (lane >= CY + 64) & jnp.logical_not(is_left)
    )
    inside = jnp.where(outside, 0.0, TIME_STEP).astype(F32)
    ax = [[-0.5 * jx[u, v] for v in range(NV)] for u in range(NV)]
    ay = [[-0.5 * jy[u, v] for v in range(NV)] for u in range(NV)]

    def advance(cur, up, dn, rt, lt, start, scale):
        dx = [p - m for p, m in zip(up, dn)]
        dy = [p - m for p, m in zip(rt, lt)]
        out = []
        for u in range(NV):
            res = DAMPING * ((up[u] + dn[u]) + (rt[u] + lt[u])) - 4.0 * DAMPING * cur[u]
            for v in range(NV):
                res = res + (ax[u][v] * dx[v] + ay[u][v] * dy[v])
            out.append(start[u] + scale * res)
        return out

    def step(cur, prev, nxt, start, scale):
        up = [pltpu.roll(jnp.where(sub == 0, n, q), 7, 0) for n, q in zip(nxt, cur)]
        dn = [pltpu.roll(jnp.where(sub == 7, p, q), 1, 0) for p, q in zip(prev, cur)]
        rt = [pltpu.roll(q, CY + 127, 1) for q in cur]
        lt = [pltpu.roll(q, 1, 1) for q in cur]
        return advance(cur, up, dn, rt, lt, start, scale)

    def rows_at(ref, i):
        r = pl.multiple_of(i * 8, 8)
        return [ref[v, pl.ds(r, 8), :] for v in range(NV)]

    def stage(src, dst, rate, last):
        def tile_at(i):
            row_ok = jnp.where(i == 0, is_dn, jnp.where(i == 17, is_up, True))
            scale = jnp.where(row_ok, rate, 0.0).astype(F32) * inside
            prev, nxt = rows_at(src, jnp.maximum(i - 1, 0)), rows_at(src, jnp.minimum(i + 1, 17))
            new = step(rows_at(src, i), prev, nxt, rows_at(force_q, i), scale)
            for u in range(NV):
                if last:
                    qout[u, pl.ds(pl.multiple_of(i * 8 - 8, 8), 8), :] = new[u][:, 0:CY]
                else:
                    dst[u, pl.ds(pl.multiple_of(i * 8, 8), 8), :] = new[u]

        width = 4 if last else 6

        def body(p, _):
            for t in range(width):
                tile_at(width * p + t + (1 if last else 0))
            return 0

        lax.fori_loop(0, 4 if last else 3, body, 0)

    stage(force_q, qa, RATES[0], False)
    stage(qa, qb, RATES[1], False)
    stage(qb, qa, RATES[2], False)
    stage(qa, None, RATES[3], True)

    for c in halo:
        c.wait_recv()
    zero = jnp.zeros((8, CY + 128), F32)
    zero128 = jnp.zeros((8, 128), F32)

    def wide(x, ok):
        return jnp.concatenate([jnp.where(ok, x, 0.0), zero128], axis=1)

    start = [
        [wide(land_above[v], is_dn) for v in range(NV)],
        [zero] * NV,
        [zero] * NV,
        [wide(land_below[v], is_up) for v in range(NV)],
    ]
    for t in (0, 3):
        for v in range(NV):
            rows0[v, 8 * t : 8 * t + 8, :] = start[t][v]
    nothing = [zero] * NV
    for i, rate in enumerate(RATES):
        src, dst = ((rows0, rows1), (rows1, rows2), (rows2, rows1), (rows1, None))[i]
        for t in (1, 2) if dst is None else range(4):
            def at(k):
                if i == 0 and k in (1, 2):
                    return nothing
                return [src[v, 8 * k : 8 * k + 8, :] for v in range(NV)]

            first = [rows0[v, 8 * t : 8 * t + 8, :] for v in range(NV)] if t in (0, 3) else nothing
            scale = rate * inside
            if t in (0, 3):
                scale = jnp.where(is_dn if t == 0 else is_up, scale, 0.0)
            new = step(at(t), at(t - 1) if t in (1, 3) else nothing, at(t + 1) if t in (0, 2) else nothing, first, scale)
            for u in range(NV):
                if dst is None:
                    r = 0 if t == 1 else CX - 8
                    qout[u, r : r + 8, :] += new[u][:, 0:CY]
                else:
                    dst[u, 8 * t : 8 * t + 8, :] = new[u]

    def sides(right, left, ok):
        from_right = (iota(right.shape, 1) & 7) < 4
        return jnp.where(from_right, jnp.where(is_right & ok, right, 0.0), jnp.where(is_left & ok, left, 0.0))

    mid = sides(land_right[...], land_left[...], True)
    mid = jnp.concatenate([mid, pltpu.roll(mid, 64, 1)], axis=0)
    below = sides(land_corner[0], land_corner[1], is_up)
    above = pltpu.roll(sides(land_corner[2], land_corner[3], is_dn), 64, 1)
    ends = jnp.concatenate([below, jnp.zeros((112, 128), F32), above], axis=0)
    strips = pltpu.roll(jnp.concatenate([mid.T, ends.T], axis=1), 4, 0)
    sub2 = iota((8, 256), 0)
    lane2 = iota((8, 256), 1)
    out_rows = ((lane2 >= 128) & (lane2 < 192) & jnp.logical_not(is_up)) | ((lane2 >= 192) & jnp.logical_not(is_dn))
    inside2 = jnp.where(out_rows, 0.0, TIME_STEP).astype(F32)
    done = []
    for near_side in (True, False):
        start = []
        for v in range(NV):
            x = strips[8 * v : 8 * v + 8]
            start.append(jnp.where((sub2 < 4) == near_side, x, 0.0))
        cur = start
        for rate in RATES:
            up = [pltpu.roll(q, 255, 1) for q in cur]
            dn = [pltpu.roll(q, 1, 1) for q in cur]
            rt = [jnp.where(sub2 == 7, 0.0, pltpu.roll(q, 7, 0)) for q in cur]
            lt = [jnp.where(sub2 == 0, 0.0, pltpu.roll(q, 1, 0)) for q in cur]
            cur = advance(cur, up, dn, rt, lt, start, rate * inside2)
        done.append([q[:, 0:128] for q in cur])
    sub1 = iota((8, 128), 0)
    joined = [jnp.where(sub1 < 4, far, near) for near, far in zip(*done)]
    joined = jnp.concatenate(joined + [jnp.zeros((128 - 8 * NV, 128), F32)], axis=0).T
    lane1 = iota((128, 128), 1)
    for v in range(NV):
        x = pltpu.roll(joined, (124 - 8 * v) % 128, 1)
        qout[v, :, 0:128] += jnp.where(lane1 < 4, x, 0.0)
        qout[v, :, 128:256] += jnp.where(lane1 >= 124, x, 0.0)
    flow_out = pltpu.make_async_copy(qout, flow_o, osem.at[0])
    flow_out.start()
    pending.append(flow_out.wait)

    pres = qout[4]
    pres = jnp.concatenate([pres[:, 0:128].T, pres[:, 128:256].T], axis=1)
    ph, plow = split(pres)
    pres2 = jnp.concatenate([ph, plow], axis=0)
    row16 = iota((16, 128), 0)

    def gather(o, cols):
        h = dot(pres2, cols, NN)
        h = h[0:128] + h[128:256]
        n16 = norms[o]
        forces = []
        for j in range(SEND):
            mask = iota((128, 128), 0) == cellv[o, SEND + j : SEND + j + 1, :]
            p = jnp.sum(jnp.where(mask, h[:, 128 * j : 128 * (j + 1)], 0.0), axis=0, keepdims=True)
            forces.append(jnp.where((row16 & 3) == j, n16 * p, 0.0).astype(BF16))
        return jnp.concatenate(forces, axis=1)

    def gather_pair(p, _):
        q, half = lax.div(p, 2), lax.rem(p, 2)
        forces = [
            gather(2 * p + i, rall[q, :, pl.ds(pl.multiple_of(1024 * half + 512 * i, 512), 512)]) for i in range(2)
        ]
        weights = [rbf[2 * p + i].reshape(SEND * 128, 128) for i in range(2)]
        both = dot(jnp.concatenate(forces, axis=0), jnp.concatenate(weights, axis=1), NN)
        load_out[2 * p] = both[0:16, 0:128]
        load_out[2 * p + 1] = both[16:32, 128:256]
        return 0

    for first, last in ((14, 16), (10, 14), (4, 10), (0, 4)):
        lax.fori_loop(first // 2, last // 2, gather_pair, 0)
        blk_send(lambda o: load_out.at[o], land_load, 3, [o for o in reversed(range(first, last)) if o != ME])
    land_load[ME] = load_out[ME]

    l_secv.wait()
    zero8 = jnp.zeros((8, 128), F32)

    def gram_row(i, _):
        for c in range(3):
            x = secv[:, c, pl.ds(i, 1), :].reshape(COLS, 128)
            x = jnp.where((i >= off) & (i < off + OWN), x, 0.0)
            hi, lo = split(jnp.concatenate([x, zero8], axis=0))
            at = pl.multiple_of((c * WIN + i) * 128, 128)
            zmat[0:32, pl.ds(at, 128)] = hi
            zmat[32:64, pl.ds(at, 128)] = lo
        return 0

    lax.fori_loop(0, WIN, gram_row, 0)
    zz = zmat[...]
    top = dot(zz, zz[0:32], NT)
    low = dot(zz, zz[32:64], NT)
    gram = top[0:32] + top[32:64] + low[0:32] + low[32:64]
    gsend[...] = jnp.zeros(gsend.shape, F32)
    gsend[:, 0:32] = gram
    land_gg[g] = gsend[...]
    grp_send(lambda d: gsend, land_gg, 0)

    row = iota((COLS, 128), 0)
    lane = iota((COLS, 128), 1)
    wrow = iota((48, 128), 0) & 15
    mine = (wrow >= off) & (wrow < off + OWN)
    d_in = jnp.where(mine, disp[:, pl.ds(a, WIN), :].reshape(48, 128), 0.0)
    rhs_in = jnp.sum(secv[...].reshape(COLS, 48, 128) * d_in[None], axis=1)
    diag = lane == row + 32

    blk_recv(lambda o: req.at[peer(o)], land_req, 0, [FAR])
    asked_t = land_req[...].reshape(NB * 16, 128).T[0:1, :]
    rr, kk = iota((48, NB * 16), 0), iota((48, NB * 16), 1)
    w = rr & 15
    same_c = (lax.shift_right_logical(kk, 2) & 3) == lax.shift_right_logical(rr, 4)
    for p in range(NG):
        first = (p * OWN) // 8 * 8
        skip = p * OWN - first
        ok = same_c & (w >= skip) & (w < skip + OWN)
        oht[48 * p : 48 * (p + 1), :] = jnp.where(ok & (asked_t == (w + first).astype(F32)), 1.0, 0.0).astype(BF16)

    blk_recv(lambda o: load_out.at[o], land_load, 3)
    got = land_load[...].reshape(NB * 16, 128)
    hi, lo = split(got)
    sums = dot(oht[...], jnp.concatenate([hi, lo], axis=1), NN)
    part[...] = (sums[:, 0:128] + sums[:, 128:256]).reshape(NG, 48, 128)
    land_part[g] = part[g]
    grp_send(lambda d: part.at[d], land_part, 1)
    l_flex.wait()

    def project(i, _):
        at = pl.multiple_of(128 * i, 128)
        hi, lo = split(flex[i])
        flexhl[pl.ds(at, 128), 0:128] = hi
        flexhl[pl.ds(at, 128), 128:256] = lo
        vh, vl = split(jnp.concatenate([secv[:, c, pl.ds(i, 1), :].reshape(COLS, 128) for c in range(3)], axis=0))
        u = dot(jnp.concatenate([vh, vl], axis=0), hi, NN)
        u = u[0:72] + u[72:144] + dot(vh, lo, NN)
        for c in range(3):
            uwin[:, c, pl.ds(i, 1), :] = u[COLS * c : COLS * (c + 1)].reshape(COLS, 1, 128)
        return 0

    lax.fori_loop(0, WIN, project, 0)
    grp_recv(lambda d: gsend, land_gg, 0)
    gsum[...] = jnp.sum(land_gg[...], axis=0)
    land_gb[ME] = gsum[...]
    blk_send(lambda o: gsum, land_gb, 2)
    grp_recv(lambda d: part.at[d], land_part, 1)
    tile_loads = jnp.sum(land_part[...], axis=0)

    prod = jnp.sum(uwin[...].reshape(COLS, 48, 128) * tile_loads[None], axis=1) - rhs_in
    rhs = jnp.sum(prod, axis=1, keepdims=True)
    rhs = jnp.sum(jnp.where(diag, rhs, 0.0), axis=0, keepdims=True)
    rmsg[...] = jnp.broadcast_to(rhs, (8, 128))
    land_rg[g] = rmsg[...]
    grp_send(lambda d: rmsg, land_rg, 2)
    hi, lo = split(tile_loads)
    lhs = jnp.concatenate(
        [jnp.concatenate([hi, hi], axis=1), jnp.concatenate([lo, jnp.zeros_like(lo)], axis=1)], axis=0
    )
    tilde = jnp.zeros((48, 128), F32)
    for u in range(WIN // 2):
        o = dot(lhs, flexhl[256 * u : 256 * (u + 1), :], NT)
        o = o[0:48] + o[48:96]
        tilde = jnp.where(wrow == 2 * u, o[:, 0:128], tilde)
        tilde = jnp.where(wrow == 2 * u + 1, o[:, 128:256], tilde)
    tmsg[...] = jnp.where(mine, tilde, 0.0)
    land_t[g] = tmsg[...]
    grp_send(lambda d: tmsg, land_t, 3)
    grp_recv(lambda d: rmsg, land_rg, 2)
    rsend[...] = jnp.sum(land_rg[...], axis=0)
    land_r[ME] = rsend[...]
    blk_send(lambda o: rsend, land_r, 4)
    l_secw.wait()
    blk_recv(lambda o: gsum, land_gb, 2)
    gram = jnp.sum(land_gb[...], axis=0)[0:COLS]
    row = iota((COLS, 128), 0)
    lane = iota((COLS, 128), 1)
    m = jnp.where(lane < COLS, gram, jnp.where(lane == row + 32, 1.0, 0.0))
    fac = jnp.zeros((COLS, 128), F32)
    for k in range(COLS):
        pivot = lax.rsqrt(jnp.broadcast_to(m[k : k + 1, k : k + 1], (1, 128)))
        r = m[k : k + 1, :] * pivot
        col = jnp.broadcast_to(m[:, k : k + 1], (COLS, 128)) * pivot
        fac = jnp.where(row == k, r, fac)
        m = m - jnp.where(row > k, col * r, 0.0)
    linv[...] = jnp.where((lane >= 32) & (lane < 32 + COLS), fac, 0.0)
    grp_recv(lambda d: tmsg, land_t, 3)
    blk_recv(lambda o: rsend, land_r, 4)
    rhs = jnp.sum(land_r[...], axis=0)[0:1]

    li = linv[...]
    y = jnp.sum(li * rhs, axis=1, keepdims=True)
    x = jnp.sum(li * y, axis=0, keepdims=True)
    x = -jnp.sum(jnp.where(diag, x, 0.0), axis=1, keepdims=True)
    coef[...] = jnp.broadcast_to(x, (COLS, 128))

    def update(p, _):
        for c in range(3):
            even, odd = land_t[2 * p, 16 * c : 16 * c + 16, :], land_t[2 * p + 1, 16 * c : 16 * c + 16, :]
            for q, t in enumerate((even[0:8], even[8:16] + odd[0:8], odd[8:16])):
                at = pl.multiple_of(24 * p + 8 * q, 8)
                for k in range(COLS):
                    t = t + coef[k : k + 1, :] * secw[k, c, pl.ds(at, 8), :]
                dout[c, pl.ds(at, 8), :] = t
        return 0

    lax.fori_loop(0, NG // 2, update, 0)
    disp_out = pltpu.make_async_copy(dout, disp_o, osem.at[1])
    disp_out.start()
    pending.append(disp_out.wait)

    finish()


def stay(x):
    return pltpu.with_memory_space_constraint(x, pltpu.HBM)


def on_device(flow_state, jx, jy, slot_tile, slot_cells, slot_normal, slot_rbf, disp_in, flex, secv, secw):
    hbm = pl.BlockSpec(memory_space=pl.ANY)
    vm, dma = pltpu.VMEM, pltpu.SemaphoreType.DMA
    state = (NV, CX + 16, CY + 128)
    scratch = [
        pltpu.SMEM((NV, NV), F32), pltpu.SMEM((NV, NV), F32),
        vm((1, 64), jnp.int32), vm((64, 128), jnp.int32), vm((3, 64, 128), F32), vm((NB, SEND, 128, 128), BF16),
        vm((3, ST, 128), F32), vm((WIN, 128, 128), F32), vm((COLS, 3, WIN, 128), F32), vm((COLS, 3, ST, 128), F32),
        vm(state, F32), vm(state, F32), vm(state, F32), vm((NV, CX, CY), F32),
        vm((NV, 32, CY + 128), F32), vm((NV, 32, CY + 128), F32), vm((NV, 32, CY + 128), F32),
        vm((NB, 16, 128), F32), vm((NB, 16, 128), F32), vm((NB, 16, 128), BF16), vm((NB, 16, 128), BF16),
        vm((384, 128), BF16),
        vm((NB, 8, 128), jnp.int32), vm((4, 256, 2048), BF16),
        vm((768, 2048), BF16), vm((768, 256), F32), vm((384, 128), BF16),
        vm((64, 128), F32),
        vm((NV, 8, CY), F32), vm((NV, 8, CY), F32), vm((64, 128), F32), vm((64, 128), F32), vm((4, 8, 128), F32),
        vm((256, 128), F32), vm((NB, 16, 128), F32), vm((NB, 16, 128), F32), vm((NB, 16, 128), F32), vm((384, 256), BF16),
        vm((NG, 48, 128), F32), vm((NG, 48, 128), F32),
        vm((WIN * 128, 256), BF16), vm((COLS, 3, WIN, 128), F32), vm((64, 48 * 128), BF16),
        vm((32, 128), F32), vm((NG, 32, 128), F32), vm((32, 128), F32), vm((NB, 32, 128), F32), vm((COLS, 128), F32),
        vm((8, 128), F32), vm((NG, 8, 128), F32), vm((48, 128), F32), vm((NG, 48, 128), F32),
        vm((8, 128), F32), vm((NB, 8, 128), F32), vm((COLS, 128), F32), vm((3, ST, 128), F32),
        dma((10,)), dma((NB,)), dma((4,)),
        dma((5, NB)), dma((5, NB)), dma((4, NG)), dma((4, NG)), dma((8,)), dma((8,)),
    ]
    flow_out, disp_out = pl.pallas_call(
        kernel,
        out_shape=(
            vm((NV, CX, CY), F32),
            vm((3, ST, 128), F32),
        ),
        in_specs=[hbm] * 11,
        out_specs=(hbm, hbm),
        scratch_shapes=scratch,
        compiler_params=pltpu.CompilerParams(
            collective_id=0, has_side_effects=True, vmem_limit_bytes=48 * 1024 * 1024
        ),
    )(*[
        stay(x) for x in (
            flow_state, jx, jy, slot_tile.reshape(1, -1), slot_cells, jnp.transpose(slot_normal, (1, 0, 2)), slot_rbf,
            jnp.transpose(disp_in, (1, 0, 2)), flex, jnp.transpose(secv, (0, 2, 1, 3)), jnp.transpose(secw, (0, 2, 1, 3)),
        )
    ])
    return flow_out, jnp.transpose(disp_out, (1, 0, 2))


def solution(mesh):
    placed = (
        P(None, "grp", "blk"), P(), P(),
        P(("grp", "blk")), P(("grp", "blk"), None),
        P(("grp", "blk"), None, None), P(("grp", "blk"), None, None),
        P("blk", None, None), P("blk", None, None),
        P(None, "blk", None, None), P(None, "blk", None, None),
    )
    return jax.shard_map(
        on_device, mesh=mesh, in_specs=placed,
        out_specs=(P(None, "grp", "blk"), P("blk", None, None)), check_vma=False,
    )
```

```python
import functools

import jax
import jax.numpy as jnp
from jax import lax
from jax.experimental import pallas as pl
from jax.experimental.pallas import tpu as pltpu
from jax.sharding import PartitionSpec as P

RATES = (0.25, 1.0 / 3.0, 0.5, 1.0)
TIME_STEP = 0.4
DAMPING = 0.25
FORCING = 1.0
F32 = jnp.float32
BF16 = jnp.bfloat16
MESH = pl.DeviceIdType.MESH
NG, NB = 8, 16
SEND, ST, COLS, NV = 4, 96, 24, 5
CX, CY = 128, 256
OWN = ST // NG
WIN = 16
HOPS = ((0, 0), (0, 1), (0, 3), (1, 0), (3, 0), (2, 2), (1, 1), (1, 3), (3, 1), (3, 3), (0, 2), (2, 0), (1, 2), (3, 2), (2, 1), (2, 3))
BACK = tuple(HOPS.index(((4 - dy) % 4, (4 - dz) % 4)) for dy, dz in HOPS)
ME = HOPS.index((0, 0))
CLASSES = ((1, 5), (6, 12), (12, 16))
FAR = 5
NN = (((1,), (0,)), ((), ()))
NT = (((1,), (1,)), ((), ()))


def iota(shape, dim):
    return lax.broadcasted_iota(jnp.int32, shape, dim)


def dot(a, b, dims):
    return lax.dot_general(a, b, dims, preferred_element_type=F32)


def split(x):
    hi = x.astype(BF16)
    return hi, (x - hi.astype(F32)).astype(BF16)


def window(g):
    return lax.div(g * OWN, 8) * 8


def kernel(
    flow_h, jx_h, jy_h, tile_h, cells_h, normal_h, rbf_h, disp_h, flex_h, secv_h, secw_h,
    flow_o, disp_o,
    jx, jy, tile, cells, normal, rbf, disp, flex, secv, secw,
    force_q, qa, qb, qout, rows0, rows1, rows2,
    req, land_req, resp, land_disp, dispc, cellv, rall, bmat, acc, table, pack,
    land_below, land_above, land_right, land_left, land_corner,
    nrm, norms, load_out, land_load, oht, part, land_part,
    flexhl, uwin, zmat, gsend, land_gg, gsum, land_gb, linv,
    rmsg, land_rg, tmsg, land_t, rsend, land_r, coef, dout,
    lsem, rsem, osem, bs, br, gs, gr, hs, hr,
):
    g = lax.axis_index("grp")
    b = lax.axis_index("blk")
    y, z = lax.div(b, 4), lax.rem(b, 4)
    a = pl.multiple_of(window(g), 8)
    off = g * OWN - window(g)

    def peer(o):
        return lax.rem(y + HOPS[o][0], 4) * 4 + lax.rem(z + HOPS[o][1], 4)

    loads = [
        (tile_h, tile),
        (cells_h, cells),
        (disp_h, disp),
        (secv_h.at[:, :, pl.ds(a, WIN), :], secv),
        (flow_h, force_q.at[:, pl.ds(8, CX), pl.ds(0, CY)]),
        (normal_h, normal),
        (flex_h.at[pl.ds(a, WIN)], flex),
        (jx_h, jx),
        (jy_h, jy),
        (secw_h, secw),
    ]
    loads = [pltpu.make_async_copy(s, d, lsem.at[i]) for i, (s, d) in enumerate(loads)]
    l_tile, l_cells, l_disp, l_secv, l_flow, l_normal, l_flex, l_jx, l_jy, l_secw = loads
    l_rbf = [
        pltpu.make_async_copy(rbf_h.at[pl.ds(peer(o) * SEND, SEND)], rbf.at[o], rsem.at[o]) for o in range(NB)
    ]
    l_tile.start()

    barrier = pltpu.get_barrier_semaphore()
    g_up, g_dn = lax.rem(g + 1, NG), lax.rem(g + NG - 1, NG)
    b_up, b_dn = lax.rem(b + 1, NB), lax.rem(b + NB - 1, NB)
    hello = [(g, peer(o)) for o in reversed(range(NB)) if o != ME]
    hello += [(g_dn, b_dn), (g_dn, b_up), (g_up, b_dn), (g_up, b_up)]
    hello += [(lax.rem(g + o, NG), b) for o in range(1, NG)]
    for dev in hello:
        pl.semaphore_signal(barrier, inc=1, device_id=dev, device_id_type=MESH)

    for c in loads[1:4] + l_rbf + loads[4:]:
        c.start()

    def blk_copy(src, land, ph, o):
        return pltpu.make_async_remote_copy(
            src_ref=src(o), dst_ref=land.at[BACK[o]], send_sem=bs.at[ph, o], recv_sem=br.at[ph, BACK[o]],
            device_id=(g, peer(o)), device_id_type=MESH,
        )

    def grp_copy(src, dst, ph, o, dev):
        return pltpu.make_async_remote_copy(
            src_ref=src, dst_ref=dst, send_sem=gs.at[ph, o], recv_sem=gr.at[ph, o],
            device_id=(dev, b), device_id_type=MESH,
        )

    def each(n, step):
        def body(o, _):
            step(o)
            return 0

        lax.fori_loop(1, n, body, 0)

    pending = []

    def finish():
        for wait in pending:
            wait()

    far_first = [FAR] + [o for o in reversed(range(NB)) if o not in (ME, FAR)]

    def blk_send(src, land, ph, peers=far_first):
        for o in peers:
            copy = blk_copy(src, land, ph, o)
            copy.start()
            pending.append(copy.wait_send)

    def blk_recv(src, land, ph, peers=far_first[::-1]):
        for o in peers:
            pltpu.make_async_remote_copy(
                src_ref=src(o), dst_ref=land.at[o], send_sem=bs.at[ph, o], recv_sem=br.at[ph, o],
                device_id=(g, peer(o)), device_id_type=MESH,
            ).wait_recv()

    def grp_send(src, land, ph):
        def step(o):
            d = lax.rem(g + o, NG)
            grp_copy(src(d), land.at[g], ph, o, d).start()

        def last(o):
            grp_copy(src(0), land.at[0], ph, o, 0).wait_send()

        each(NG, step)
        pending.append(lambda: each(NG, last))

    def grp_recv(src, land, ph):
        def step(o):
            d = lax.rem(g + NG - o, NG)
            grp_copy(src(d), land.at[d], ph, o, d).wait_recv()

        each(NG, step)

    l_tile.wait()
    row = iota((NB * 16, 64), 0)
    hit = iota((NB * 16, 64), 1) == lax.shift_right_logical(row, 4) * SEND + (row & 3)
    wanted = jnp.sum(jnp.where(hit, tile[...].astype(F32), 0.0), axis=1, keepdims=True)
    row = iota((NB * 16, 128), 0)
    wanted = jnp.where((row & 15) < 12, jnp.broadcast_to(wanted, (NB * 16, 128)), -1.0)
    req[...] = wanted.reshape(NB, 16, 128)
    land_req[ME] = req[b]

    pl.semaphore_wait(barrier, len(hello))
    blk_send(lambda o: req.at[peer(o)], land_req, 0)

    l_disp.wait()
    dispc[...] = jnp.zeros(dispc.shape, BF16)
    for c in range(3):
        dispc[128 * c : 128 * c + ST, :] = disp[c].astype(BF16)
    to_far = pltpu.make_async_remote_copy(
        src_ref=dispc, dst_ref=table, send_sem=osem.at[2], recv_sem=osem.at[3],
        device_id=(g, peer(FAR)), device_id_type=MESH,
    )
    to_far.start()
    pending.append(to_far.wait_send)

    l_cells.wait()
    for o in range(NB):
        cellv[o, 0:SEND, :] = cells[pl.ds(peer(o) * SEND, SEND), :]

    def rows_of(p, _):
        for i in range(4):
            for j in range(SEND):
                cell = cellv[4 * p + i, j : j + 1, :]
                r = (lax.shift_right_logical(cell, 7) & 1) * 128 + lax.shift_right_logical(cell, 8)
                one = jnp.where(iota((256, 128), 0) == r, 1.0, 0.0).astype(BF16)
                rall[p, :, 512 * i + 128 * j : 512 * i + 128 * (j + 1)] = one
                cellv[4 * p + i, SEND + j : SEND + j + 1, :] = cell & 127
        return 0

    lax.fori_loop(0, 4, rows_of, 0)
    l_normal.wait()
    nrm[...] = jnp.zeros(nrm.shape, F32)
    for c in range(3):
        for j in range(SEND):
            nrm[pl.ds(4 * c + j, NB, stride=16), :] = normal[c, pl.ds(j, NB, stride=SEND), :]
    for o in range(NB):
        norms[o] = nrm[pl.ds(pl.multiple_of(peer(o) * 16, 16), 16), :]
    force_q[:, 0:8, :] = jnp.zeros((NV, 8, CY + 128), F32)
    force_q[:, 8 + CX : 16 + CX, :] = jnp.zeros((NV, 8, CY + 128), F32)
    force_q[:, 8 : 8 + CX, CY : CY + 128] = jnp.zeros((NV, CX, 128), F32)
    def answer(asked, shown):
        n = asked.shape[0] * 16
        asked = asked.reshape(n, 128)
        row_c = lax.shift_right_logical(iota((n, 128), 0), 2) & 3
        found = asked == iota((n, 128), 1).astype(F32)
        pick = jnp.concatenate([jnp.where(found & (row_c == c), 1.0, 0.0).astype(BF16) for c in range(3)], axis=1)
        return dot(pick, shown, NN).astype(BF16).reshape(n // 16, 16, 128)

    land_disp[ME] = answer(land_req[ME][None], dispc[...])[0]
    for first, last in CLASSES:
        blk_recv(lambda o: req.at[peer(o)], land_req, 0, range(first, last))
        resp[first:last] = answer(land_req[first:last], dispc[...])
        blk_send(lambda o: resp.at[o], land_disp, 1, range(first, last))

    acc[...] = jnp.zeros(acc.shape, F32)
    none16 = jnp.zeros((16, 128), BF16)

    def spread(p, _):
        @pl.when(p == FAR // 4)
        def _():
            to_far.wait_recv()
            land_disp[FAR] = answer(req[peer(FAR)][None], table[...])[0]

        for i in range(4):
            o = 4 * p + i

            @pl.when((o != ME) & (o != FAR))
            def _():
                pltpu.make_async_remote_copy(
                    src_ref=resp.at[o], dst_ref=land_disp.at[o], send_sem=bs.at[1, o], recv_sem=br.at[1, o],
                    device_id=(g, peer(FAR)), device_id_type=MESH,
                ).wait_recv()

            pltpu.make_async_copy(rbf_h.at[pl.ds(0, SEND)], rbf.at[o], rsem.at[o]).wait()
        for h in (0, 2):
            o = 4 * p + h
            x = jnp.concatenate(
                [
                    jnp.concatenate([land_disp[o], none16], axis=1),
                    jnp.concatenate([none16, land_disp[o + 1]], axis=1),
                ],
                axis=0,
            )
            weights = [rbf[o + i].reshape(SEND * 128, 128) for i in range(2)]
            moved = dot(x, jnp.concatenate(weights, axis=1), NT) * FORCING
            high = moved.astype(BF16).astype(F32)
            low = moved - high
            for i in range(2):
                for j in range(SEND):
                    mask = iota((128, 128), 0) == cellv[o + i, SEND + j : SEND + j + 1, :]
                    at = 512 * (h + i) + 128 * j
                    for c in range(3):
                        r = 16 * i + 4 * c + j
                        vh = high[r : r + 1, 128 * j : 128 * (j + 1)]
                        vl = low[r : r + 1, 128 * j : 128 * (j + 1)]
                        bmat[256 * c : 256 * c + 128, at : at + 128] = jnp.where(mask, vh, 0.0).astype(BF16)
                        bmat[256 * c + 128 : 256 * c + 256, at : at + 128] = jnp.where(mask, vl, 0.0).astype(BF16)
        acc[...] += dot(bmat[...], rall[p], NT)
        return 0

    lax.fori_loop(0, 4, spread, 0)
    l_flow.wait()
    for c in range(3):
        s = acc[256 * c : 256 * c + 128, :] + acc[256 * c + 128 : 256 * c + 256, :]
        force_q[1 + c, 8 : 8 + CX, 0:128] += s[:, 0:128].T
        force_q[1 + c, 8 : 8 + CX, 128:256] += s[:, 128:256].T

    lane = iota((128, 128), 1)
    strip = lax.shift_right_logical((lane + 4) & 127, 3)
    packed = jnp.zeros((128, 128), F32)
    for v in range(NV):
        t = jnp.where(lane < 64, force_q[v, 8 : 8 + CX, 0:128], force_q[v, 8 : 8 + CX, 128:256])
        if v:
            t = pltpu.roll(t, 8 * v, 1)
        packed = jnp.where(strip == v, t, packed)
    lane64 = iota((64, 128), 1)
    pack[...] = jnp.where(((lane64 + 4) & 127) < 64, packed[0:64], pltpu.roll(packed[64:128], 64, 1))
    top_rows = force_q.at[:, pl.ds(8, 8), pl.ds(0, CY)]
    low_rows = force_q.at[:, pl.ds(CX, 8), pl.ds(0, CY)]
    halo = [
        (pack.at[pl.ds(0, 8)], land_corner.at[0], (g_dn, b_dn)),
        (pack.at[pl.ds(0, 8)], land_corner.at[1], (g_dn, b_up)),
        (pack.at[pl.ds(56, 8)], land_corner.at[2], (g_up, b_dn)),
        (pack.at[pl.ds(56, 8)], land_corner.at[3], (g_up, b_up)),
        (pack, land_right, (g, b_dn)),
        (pack, land_left, (g, b_up)),
        (top_rows, land_below, (g_dn, b)),
        (low_rows, land_above, (g_up, b)),
    ]
    halo = [
        pltpu.make_async_remote_copy(
            src_ref=s, dst_ref=d, send_sem=hs.at[i], recv_sem=hr.at[i], device_id=dev, device_id_type=MESH
        )
        for i, (s, d, dev) in enumerate(halo)
    ]
    for c in halo:
        c.start()
        pending.append(c.wait_send)

    is_up, is_dn = g < NG - 1, g > 0
    is_right, is_left = b < NB - 1, b > 0
    l_jx.wait()
    l_jy.wait()
    lane = iota((8, CY + 128), 1)
    sub = iota((8, CY + 128), 0)
    outside = ((lane >= CY) & (lane < CY + 64) & jnp.logical_not(is_right)) | (
        (lane >= CY + 64) & jnp.logical_not(is_left)
    )
    inside = jnp.where(outside, 0.0, TIME_STEP).astype(F32)
    ax = [[-0.5 * jx[u, v] for v in range(NV)] for u in range(NV)]
    ay = [[-0.5 * jy[u, v] for v in range(NV)] for u in range(NV)]

    def advance(cur, up, dn, rt, lt, start, scale):
        dx = [p - m for p, m in zip(up, dn)]
        dy = [p - m for p, m in zip(rt, lt)]
        out = []
        for u in range(NV):
            res = DAMPING * ((up[u] + dn[u]) + (rt[u] + lt[u])) - 4.0 * DAMPING * cur[u]
            for v in range(NV):
                res = res + (ax[u][v] * dx[v] + ay[u][v] * dy[v])
            out.append(start[u] + scale * res)
        return out

    def step(cur, prev, nxt, start, scale):
        up = [pltpu.roll(jnp.where(sub == 0, n, q), 7, 0) for n, q in zip(nxt, cur)]
        dn = [pltpu.roll(jnp.where(sub == 7, p, q), 1, 0) for p, q in zip(prev, cur)]
        rt = [pltpu.roll(q, CY + 127, 1) for q in cur]
        lt = [pltpu.roll(q, 1, 1) for q in cur]
        return advance(cur, up, dn, rt, lt, start, scale)

    def rows_at(ref, i):
        r = pl.multiple_of(i * 8, 8)
        return [ref[v, pl.ds(r, 8), :] for v in range(NV)]

    def stage(src, dst, rate, last):
        def tile_at(i):
            row_ok = jnp.where(i == 0, is_dn, jnp.where(i == 17, is_up, True))
            scale = jnp.where(row_ok, rate, 0.0).astype(F32) * inside
            prev, nxt = rows_at(src, jnp.maximum(i - 1, 0)), rows_at(src, jnp.minimum(i + 1, 17))
            new = step(rows_at(src, i), prev, nxt, rows_at(force_q, i), scale)
            for u in range(NV):
                if last:
                    qout[u, pl.ds(pl.multiple_of(i * 8 - 8, 8), 8), :] = new[u][:, 0:CY]
                else:
                    dst[u, pl.ds(pl.multiple_of(i * 8, 8), 8), :] = new[u]

        width = 4 if last else 6

        def body(p, _):
            for t in range(width):
                tile_at(width * p + t + (1 if last else 0))
            return 0

        lax.fori_loop(0, 4 if last else 3, body, 0)

    stage(force_q, qa, RATES[0], False)
    stage(qa, qb, RATES[1], False)
    stage(qb, qa, RATES[2], False)
    stage(qa, None, RATES[3], True)

    for c in halo:
        c.wait_recv()
    zero = jnp.zeros((8, CY + 128), F32)
    zero128 = jnp.zeros((8, 128), F32)

    def wide(x, ok):
        return jnp.concatenate([jnp.where(ok, x, 0.0), zero128], axis=1)

    start = [
        [wide(land_above[v], is_dn) for v in range(NV)],
        [zero] * NV,
        [zero] * NV,
        [wide(land_below[v], is_up) for v in range(NV)],
    ]
    for t in (0, 3):
        for v in range(NV):
            rows0[v, 8 * t : 8 * t + 8, :] = start[t][v]
    nothing = [zero] * NV
    for i, rate in enumerate(RATES):
        src, dst = ((rows0, rows1), (rows1, rows2), (rows2, rows1), (rows1, None))[i]
        for t in (1, 2) if dst is None else range(4):
            def at(k):
                if i == 0 and k in (1, 2):
                    return nothing
                return [src[v, 8 * k : 8 * k + 8, :] for v in range(NV)]

            first = [rows0[v, 8 * t : 8 * t + 8, :] for v in range(NV)] if t in (0, 3) else nothing
            scale = rate * inside
            if t in (0, 3):
                scale = jnp.where(is_dn if t == 0 else is_up, scale, 0.0)
            new = step(at(t), at(t - 1) if t in (1, 3) else nothing, at(t + 1) if t in (0, 2) else nothing, first, scale)
            for u in range(NV):
                if dst is None:
                    r = 0 if t == 1 else CX - 8
                    qout[u, r : r + 8, :] += new[u][:, 0:CY]
                else:
                    dst[u, 8 * t : 8 * t + 8, :] = new[u]

    def sides(right, left, ok):
        from_right = (iota(right.shape, 1) & 7) < 4
        return jnp.where(from_right, jnp.where(is_right & ok, right, 0.0), jnp.where(is_left & ok, left, 0.0))

    mid = sides(land_right[...], land_left[...], True)
    mid = jnp.concatenate([mid, pltpu.roll(mid, 64, 1)], axis=0)
    below = sides(land_corner[0], land_corner[1], is_up)
    above = pltpu.roll(sides(land_corner[2], land_corner[3], is_dn), 64, 1)
    ends = jnp.concatenate([below, jnp.zeros((112, 128), F32), above], axis=0)
    strips = pltpu.roll(jnp.concatenate([mid.T, ends.T], axis=1), 4, 0)
    sub2 = iota((8, 256), 0)
    lane2 = iota((8, 256), 1)
    out_rows = ((lane2 >= 128) & (lane2 < 192) & jnp.logical_not(is_up)) | ((lane2 >= 192) & jnp.logical_not(is_dn))
    inside2 = jnp.where(out_rows, 0.0, TIME_STEP).astype(F32)
    done = []
    for near_side in (True, False):
        start = []
        for v in range(NV):
            x = strips[8 * v : 8 * v + 8]
            start.append(jnp.where((sub2 < 4) == near_side, x, 0.0))
        cur = start
        for rate in RATES:
            up = [pltpu.roll(q, 255, 1) for q in cur]
            dn = [pltpu.roll(q, 1, 1) for q in cur]
            rt = [jnp.where(sub2 == 7, 0.0, pltpu.roll(q, 7, 0)) for q in cur]
            lt = [jnp.where(sub2 == 0, 0.0, pltpu.roll(q, 1, 0)) for q in cur]
            cur = advance(cur, up, dn, rt, lt, start, rate * inside2)
        done.append([q[:, 0:128] for q in cur])
    sub1 = iota((8, 128), 0)
    joined = [jnp.where(sub1 < 4, far, near) for near, far in zip(*done)]
    joined = jnp.concatenate(joined + [jnp.zeros((128 - 8 * NV, 128), F32)], axis=0).T
    lane1 = iota((128, 128), 1)
    for v in range(NV):
        x = pltpu.roll(joined, (124 - 8 * v) % 128, 1)
        qout[v, :, 0:128] += jnp.where(lane1 < 4, x, 0.0)
        qout[v, :, 128:256] += jnp.where(lane1 >= 124, x, 0.0)
    flow_out = pltpu.make_async_copy(qout, flow_o, osem.at[0])
    flow_out.start()
    pending.append(flow_out.wait)

    pres = qout[4]
    pres = jnp.concatenate([pres[:, 0:128].T, pres[:, 128:256].T], axis=1)
    ph, plow = split(pres)
    pres2 = jnp.concatenate([ph, plow], axis=0)
    row16 = iota((16, 128), 0)

    def gather(o, cols):
        h = dot(pres2, cols, NN)
        h = h[0:128] + h[128:256]
        n16 = norms[o]
        forces = []
        for j in range(SEND):
            mask = iota((128, 128), 0) == cellv[o, SEND + j : SEND + j + 1, :]
            p = jnp.sum(jnp.where(mask, h[:, 128 * j : 128 * (j + 1)], 0.0), axis=0, keepdims=True)
            forces.append(jnp.where((row16 & 3) == j, n16 * p, 0.0).astype(BF16))
        return jnp.concatenate(forces, axis=1)

    def gather_four(q, _):
        for first in (0, 2):
            forces = [gather(4 * q + first + i, rall[q, :, 512 * (first + i) : 512 * (first + i + 1)]) for i in range(2)]
            weights = [rbf[4 * q + first + i].reshape(SEND * 128, 128) for i in range(2)]
            both = dot(jnp.concatenate(forces, axis=0), jnp.concatenate(weights, axis=1), NN)
            load_out[4 * q + first] = both[0:16, 0:128]
            load_out[4 * q + first + 1] = both[16:32, 128:256]
        return 0

    for q in (1, 3, 2, 0):
        lax.fori_loop(q, q + 1, gather_four, 0)
        blk_send(lambda o: load_out.at[o], land_load, 3, [o for o in reversed(range(4 * q, 4 * q + 4)) if o != ME])
    land_load[ME] = load_out[ME]

    l_secv.wait()
    zero8 = jnp.zeros((8, 128), F32)

    def gram_row(i, _):
        for c in range(3):
            x = secv[:, c, pl.ds(i, 1), :].reshape(COLS, 128)
            x = jnp.where((i >= off) & (i < off + OWN), x, 0.0)
            hi, lo = split(jnp.concatenate([x, zero8], axis=0))
            at = pl.multiple_of((c * WIN + i) * 128, 128)
            zmat[0:32, pl.ds(at, 128)] = hi
            zmat[32:64, pl.ds(at, 128)] = lo
        return 0

    lax.fori_loop(0, WIN, gram_row, 0)
    zz = zmat[...]
    top = dot(zz, zz[0:32], NT)
    low = dot(zz, zz[32:64], NT)
    gram = top[0:32] + top[32:64] + low[0:32] + low[32:64]
    gsend[...] = jnp.zeros(gsend.shape, F32)
    gsend[:, 0:32] = gram
    land_gg[g] = gsend[...]
    grp_send(lambda d: gsend, land_gg, 0)

    row = iota((COLS, 128), 0)
    lane = iota((COLS, 128), 1)
    wrow = iota((48, 128), 0) & 15
    mine = (wrow >= off) & (wrow < off + OWN)
    d_in = jnp.where(mine, disp[:, pl.ds(a, WIN), :].reshape(48, 128), 0.0)
    rhs_in = jnp.sum(secv[...].reshape(COLS, 48, 128) * d_in[None], axis=1)
    diag = lane == row + 32

    blk_recv(lambda o: req.at[peer(o)], land_req, 0, [FAR])
    asked_t = land_req[...].reshape(NB * 16, 128).T[0:1, :]
    rr, kk = iota((48, NB * 16), 0), iota((48, NB * 16), 1)
    w = rr & 15
    same_c = (lax.shift_right_logical(kk, 2) & 3) == lax.shift_right_logical(rr, 4)
    for p in range(NG):
        first = (p * OWN) // 8 * 8
        skip = p * OWN - first
        ok = same_c & (w >= skip) & (w < skip + OWN)
        oht[48 * p : 48 * (p + 1), :] = jnp.where(ok & (asked_t == (w + first).astype(F32)), 1.0, 0.0).astype(BF16)

    blk_recv(lambda o: load_out.at[o], land_load, 3)
    got = land_load[...].reshape(NB * 16, 128)
    hi, lo = split(got)
    sums = dot(oht[...], jnp.concatenate([hi, lo], axis=1), NN)
    part[...] = (sums[:, 0:128] + sums[:, 128:256]).reshape(NG, 48, 128)
    land_part[g] = part[g]
    grp_send(lambda d: part.at[d], land_part, 1)
    l_flex.wait()

    def project(i, _):
        at = pl.multiple_of(128 * i, 128)
        hi, lo = split(flex[i])
        flexhl[pl.ds(at, 128), 0:128] = hi
        flexhl[pl.ds(at, 128), 128:256] = lo
        vh, vl = split(jnp.concatenate([secv[:, c, pl.ds(i, 1), :].reshape(COLS, 128) for c in range(3)], axis=0))
        u = dot(jnp.concatenate([vh, vl], axis=0), hi, NN)
        u = u[0:72] + u[72:144] + dot(vh, lo, NN)
        for c in range(3):
            uwin[:, c, pl.ds(i, 1), :] = u[COLS * c : COLS * (c + 1)].reshape(COLS, 1, 128)
        return 0

    lax.fori_loop(0, WIN, project, 0)
    grp_recv(lambda d: gsend, land_gg, 0)
    gsum[...] = jnp.sum(land_gg[...], axis=0)
    land_gb[ME] = gsum[...]
    blk_send(lambda o: gsum, land_gb, 2)
    grp_recv(lambda d: part.at[d], land_part, 1)
    tile_loads = jnp.sum(land_part[...], axis=0)

    prod = jnp.sum(uwin[...].reshape(COLS, 48, 128) * tile_loads[None], axis=1) - rhs_in
    rhs = jnp.sum(prod, axis=1, keepdims=True)
    rhs = jnp.sum(jnp.where(diag, rhs, 0.0), axis=0, keepdims=True)
    rmsg[...] = jnp.broadcast_to(rhs, (8, 128))
    land_rg[g] = rmsg[...]
    grp_send(lambda d: rmsg, land_rg, 2)
    hi, lo = split(tile_loads)
    lhs = jnp.concatenate(
        [jnp.concatenate([hi, hi], axis=1), jnp.concatenate([lo, jnp.zeros_like(lo)], axis=1)], axis=0
    )
    tilde = jnp.zeros((48, 128), F32)
    for u in range(WIN // 2):
        o = dot(lhs, flexhl[256 * u : 256 * (u + 1), :], NT)
        o = o[0:48] + o[48:96]
        tilde = jnp.where(wrow == 2 * u, o[:, 0:128], tilde)
        tilde = jnp.where(wrow == 2 * u + 1, o[:, 128:256], tilde)
    tmsg[...] = jnp.where(mine, tilde, 0.0)
    land_t[g] = tmsg[...]
    grp_send(lambda d: tmsg, land_t, 3)
    grp_recv(lambda d: rmsg, land_rg, 2)
    rsend[...] = jnp.sum(land_rg[...], axis=0)
    land_r[ME] = rsend[...]
    blk_send(lambda o: rsend, land_r, 4)
    l_secw.wait()
    blk_recv(lambda o: gsum, land_gb, 2)
    gram = jnp.sum(land_gb[...], axis=0)[0:COLS]
    row = iota((COLS, 128), 0)
    lane = iota((COLS, 128), 1)
    m = jnp.where(lane < COLS, gram, jnp.where(lane == row + 32, 1.0, 0.0))
    fac = jnp.zeros((COLS, 128), F32)
    for k in range(COLS):
        pivot = lax.rsqrt(jnp.broadcast_to(m[k : k + 1, k : k + 1], (1, 128)))
        r = m[k : k + 1, :] * pivot
        col = jnp.broadcast_to(m[:, k : k + 1], (COLS, 128)) * pivot
        fac = jnp.where(row == k, r, fac)
        m = m - jnp.where(row > k, col * r, 0.0)
    linv[...] = jnp.where((lane >= 32) & (lane < 32 + COLS), fac, 0.0)
    grp_recv(lambda d: tmsg, land_t, 3)
    blk_recv(lambda o: rsend, land_r, 4)
    rhs = jnp.sum(land_r[...], axis=0)[0:1]

    li = linv[...]
    y = jnp.sum(li * rhs, axis=1, keepdims=True)
    x = jnp.sum(li * y, axis=0, keepdims=True)
    x = -jnp.sum(jnp.where(diag, x, 0.0), axis=1, keepdims=True)
    coef[...] = jnp.broadcast_to(x, (COLS, 128))

    def update(p, _):
        for c in range(3):
            even, odd = land_t[2 * p, 16 * c : 16 * c + 16, :], land_t[2 * p + 1, 16 * c : 16 * c + 16, :]
            for q, t in enumerate((even[0:8], even[8:16] + odd[0:8], odd[8:16])):
                at = pl.multiple_of(24 * p + 8 * q, 8)
                for k in range(COLS):
                    t = t + coef[k : k + 1, :] * secw[k, c, pl.ds(at, 8), :]
                dout[c, pl.ds(at, 8), :] = t
        return 0

    lax.fori_loop(0, NG // 2, update, 0)
    disp_out = pltpu.make_async_copy(dout, disp_o, osem.at[1])
    disp_out.start()
    pending.append(disp_out.wait)

    finish()


def deliver(flow, disp, flow_out, disp_out, sems):
    copies = [pltpu.make_async_copy(flow, flow_out, sems.at[0]), pltpu.make_async_copy(disp, disp_out, sems.at[1])]
    for c in copies:
        c.start()
    for c in copies:
        c.wait()


def stay(x):
    return pltpu.with_memory_space_constraint(x, pltpu.HBM)


def on_device(flow_state, jx, jy, slot_tile, slot_cells, slot_normal, slot_rbf, disp_in, flex, secv, secw):
    hbm = pl.BlockSpec(memory_space=pl.ANY)
    vm, dma = pltpu.VMEM, pltpu.SemaphoreType.DMA
    state = (NV, CX + 16, CY + 128)
    scratch = [
        pltpu.SMEM((NV, NV), F32), pltpu.SMEM((NV, NV), F32),
        vm((1, 64), jnp.int32), vm((64, 128), jnp.int32), vm((3, 64, 128), F32), vm((NB, SEND, 128, 128), BF16),
        vm((3, ST, 128), F32), vm((WIN, 128, 128), F32), vm((COLS, 3, WIN, 128), F32), vm((COLS, 3, ST, 128), F32),
        vm(state, F32), vm(state, F32), vm(state, F32), vm((NV, CX, CY), F32),
        vm((NV, 32, CY + 128), F32), vm((NV, 32, CY + 128), F32), vm((NV, 32, CY + 128), F32),
        vm((NB, 16, 128), F32), vm((NB, 16, 128), F32), vm((NB, 16, 128), BF16), vm((NB, 16, 128), BF16),
        vm((384, 128), BF16),
        vm((NB, 8, 128), jnp.int32), vm((4, 256, 2048), BF16),
        vm((768, 2048), BF16), vm((768, 256), F32), vm((384, 128), BF16),
        vm((64, 128), F32),
        vm((NV, 8, CY), F32), vm((NV, 8, CY), F32), vm((64, 128), F32), vm((64, 128), F32), vm((4, 8, 128), F32),
        vm((256, 128), F32), vm((NB, 16, 128), F32), vm((NB, 16, 128), F32), vm((NB, 16, 128), F32), vm((384, 256), BF16),
        vm((NG, 48, 128), F32), vm((NG, 48, 128), F32),
        vm((WIN * 128, 256), BF16), vm((COLS, 3, WIN, 128), F32), vm((64, 48 * 128), BF16),
        vm((32, 128), F32), vm((NG, 32, 128), F32), vm((32, 128), F32), vm((NB, 32, 128), F32), vm((COLS, 128), F32),
        vm((8, 128), F32), vm((NG, 8, 128), F32), vm((48, 128), F32), vm((NG, 48, 128), F32),
        vm((8, 128), F32), vm((NB, 8, 128), F32), vm((COLS, 128), F32), vm((3, ST, 128), F32),
        dma((10,)), dma((NB,)), dma((4,)),
        dma((5, NB)), dma((5, NB)), dma((4, NG)), dma((4, NG)), dma((8,)), dma((8,)),
    ]
    flow_out, disp_out = pl.pallas_call(
        kernel,
        out_shape=(
            vm((NV, CX, CY), F32),
            vm((3, ST, 128), F32),
        ),
        in_specs=[hbm] * 11,
        out_specs=(hbm, hbm),
        scratch_shapes=scratch,
        compiler_params=pltpu.CompilerParams(
            collective_id=0, has_side_effects=True, vmem_limit_bytes=48 * 1024 * 1024
        ),
    )(*[
        stay(x) for x in (
            flow_state, jx, jy, slot_tile.reshape(1, -1), slot_cells, jnp.transpose(slot_normal, (1, 0, 2)), slot_rbf,
            jnp.transpose(disp_in, (1, 0, 2)), flex, jnp.transpose(secv, (0, 2, 1, 3)), jnp.transpose(secw, (0, 2, 1, 3)),
        )
    ])
    flow_out, disp_out = pl.pallas_call(
        deliver,
        out_shape=(jax.ShapeDtypeStruct(flow_out.shape, F32), jax.ShapeDtypeStruct(disp_out.shape, F32)),
        in_specs=[hbm, hbm],
        out_specs=(hbm, hbm),
        scratch_shapes=[dma((2,))],
        compiler_params=pltpu.CompilerParams(vmem_limit_bytes=1024 * 1024),
    )(flow_out, disp_out)
    return flow_out, jnp.transpose(disp_out, (1, 0, 2))


def solution(mesh):
    placed = (
        P(None, "grp", "blk"), P(), P(),
        P(("grp", "blk")), P(("grp", "blk"), None),
        P(("grp", "blk"), None, None), P(("grp", "blk"), None, None),
        P("blk", None, None), P("blk", None, None),
        P(None, "blk", None, None), P(None, "blk", None, None),
    )
    return jax.shard_map(
        on_device, mesh=mesh, in_specs=placed,
        out_specs=(P(None, "grp", "blk"), P("blk", None, None)), check_vma=False,
    )
```

```python
import functools

import jax
import jax.numpy as jnp
from jax import lax
from jax.experimental import pallas as pl
from jax.experimental.pallas import tpu as pltpu
from jax.sharding import PartitionSpec as P

RATES = (0.25, 1.0 / 3.0, 0.5, 1.0)
TIME_STEP = 0.4
DAMPING = 0.25
FORCING = 1.0
F32 = jnp.float32
BF16 = jnp.bfloat16
F8 = jnp.float8_e4m3fn
LIFT = 64.0
MESH = pl.DeviceIdType.MESH
NG, NB = 8, 16
SEND, ST, COLS, NV = 4, 96, 24, 5
CX, CY = 128, 256
OWN = ST // NG
WIN = 16
HOPS = ((0, 0), (0, 1), (0, 3), (1, 0), (3, 0), (2, 2), (1, 1), (1, 3), (3, 1), (3, 3), (0, 2), (2, 0), (1, 2), (3, 2), (2, 1), (2, 3))
BACK = tuple(HOPS.index(((4 - dy) % 4, (4 - dz) % 4)) for dy, dz in HOPS)
ME = HOPS.index((0, 0))
CLASSES = ((1, 5), (6, 12), (12, 16))
FAR = 5
NN = (((1,), (0,)), ((), ()))
NT = (((1,), (1,)), ((), ()))


def iota(shape, dim):
    return lax.broadcasted_iota(jnp.int32, shape, dim)


def dot(a, b, dims):
    return lax.dot_general(a, b, dims, preferred_element_type=F32)


def split(x):
    hi = x.astype(BF16)
    return hi, (x - hi.astype(F32)).astype(BF16)


def window(g):
    return lax.div(g * OWN, 8) * 8


def kernel(
    flow_h, jx_h, jy_h, tile_h, cells_h, normal_h, rbf_h, disp_h, flex_h, secv_h, secw_h,
    flow_o, disp_o,
    jx, jy, tile, cells, normal, rbf, disp, flex, secv, secw,
    force_q, qa, qb, qout, rows0, rows1, rows2,
    req, land_req, resp, land_disp, dispc, cellv, rall, rall8, bmat, bmat8, acc, table, pack,
    land_below, land_above, land_right, land_left, land_corner,
    nrm, norms, load_out, land_load, oht, part, land_part,
    flexhl, uwin, zmat, gsend, land_gg, gsum, land_gb, linv,
    rmsg, land_rg, tmsg, land_t, rsend, land_r, coef, dout,
    lsem, rsem, osem, bs, br, gs, gr, hs, hr,
):
    g = lax.axis_index("grp")
    b = lax.axis_index("blk")
    y, z = lax.div(b, 4), lax.rem(b, 4)
    a = pl.multiple_of(window(g), 8)
    off = g * OWN - window(g)

    def peer(o):
        return lax.rem(y + HOPS[o][0], 4) * 4 + lax.rem(z + HOPS[o][1], 4)

    loads = [
        (tile_h, tile),
        (cells_h, cells),
        (disp_h, disp),
        (secv_h.at[:, :, pl.ds(a, WIN), :], secv),
        (flow_h, force_q.at[:, pl.ds(8, CX), pl.ds(0, CY)]),
        (normal_h, normal),
        (flex_h.at[pl.ds(a, WIN)], flex),
        (jx_h, jx),
        (jy_h, jy),
        (secw_h, secw),
    ]
    loads = [pltpu.make_async_copy(s, d, lsem.at[i]) for i, (s, d) in enumerate(loads)]
    l_tile, l_cells, l_disp, l_secv, l_flow, l_normal, l_flex, l_jx, l_jy, l_secw = loads
    l_rbf = [
        pltpu.make_async_copy(rbf_h.at[pl.ds(peer(o) * SEND, SEND)], rbf.at[o], rsem.at[o]) for o in range(NB)
    ]
    l_tile.start()

    barrier = pltpu.get_barrier_semaphore()
    g_up, g_dn = lax.rem(g + 1, NG), lax.rem(g + NG - 1, NG)
    b_up, b_dn = lax.rem(b + 1, NB), lax.rem(b + NB - 1, NB)
    hello = [(g, peer(o)) for o in reversed(range(NB)) if o != ME]
    hello += [(g_dn, b_dn), (g_dn, b_up), (g_up, b_dn), (g_up, b_up)]
    hello += [(lax.rem(g + o, NG), b) for o in range(1, NG)]
    for dev in hello:
        pl.semaphore_signal(barrier, inc=1, device_id=dev, device_id_type=MESH)

    for c in loads[1:4] + l_rbf + loads[4:]:
        c.start()

    def blk_copy(src, land, ph, o):
        return pltpu.make_async_remote_copy(
            src_ref=src(o), dst_ref=land.at[BACK[o]], send_sem=bs.at[ph, o], recv_sem=br.at[ph, BACK[o]],
            device_id=(g, peer(o)), device_id_type=MESH,
        )

    def grp_copy(src, dst, ph, o, dev):
        return pltpu.make_async_remote_copy(
            src_ref=src, dst_ref=dst, send_sem=gs.at[ph, o], recv_sem=gr.at[ph, o],
            device_id=(dev, b), device_id_type=MESH,
        )

    def each(n, step):
        def body(o, _):
            step(o)
            return 0

        lax.fori_loop(1, n, body, 0)

    pending = []

    def finish():
        for wait in pending:
            wait()

    far_first = [FAR] + [o for o in reversed(range(NB)) if o not in (ME, FAR)]

    def blk_send(src, land, ph, peers=far_first):
        for o in peers:
            copy = blk_copy(src, land, ph, o)
            copy.start()
            pending.append(copy.wait_send)

    def blk_recv(src, land, ph, peers=far_first[::-1]):
        for o in peers:
            pltpu.make_async_remote_copy(
                src_ref=src(o), dst_ref=land.at[o], send_sem=bs.at[ph, o], recv_sem=br.at[ph, o],
                device_id=(g, peer(o)), device_id_type=MESH,
            ).wait_recv()

    def grp_send(src, land, ph):
        def step(o):
            d = lax.rem(g + o, NG)
            grp_copy(src(d), land.at[g], ph, o, d).start()

        def last(o):
            grp_copy(src(0), land.at[0], ph, o, 0).wait_send()

        each(NG, step)
        pending.append(lambda: each(NG, last))

    def grp_recv(src, land, ph):
        def step(o):
            d = lax.rem(g + NG - o, NG)
            grp_copy(src(d), land.at[d], ph, o, d).wait_recv()

        each(NG, step)

    l_tile.wait()
    row = iota((NB * 16, 64), 0)
    hit = iota((NB * 16, 64), 1) == lax.shift_right_logical(row, 4) * SEND + (row & 3)
    wanted = jnp.sum(jnp.where(hit, tile[...].astype(F32), 0.0), axis=1, keepdims=True)
    row = iota((NB * 16, 128), 0)
    wanted = jnp.where((row & 15) < 12, jnp.broadcast_to(wanted, (NB * 16, 128)), -1.0)
    req[...] = wanted.reshape(NB, 16, 128)
    land_req[ME] = req[b]

    pl.semaphore_wait(barrier, len(hello))
    blk_send(lambda o: req.at[peer(o)], land_req, 0)

    l_disp.wait()
    dispc[...] = jnp.zeros(dispc.shape, BF16)
    for c in range(3):
        dispc[128 * c : 128 * c + ST, :] = disp[c].astype(BF16)
    to_far = pltpu.make_async_remote_copy(
        src_ref=dispc, dst_ref=table, send_sem=osem.at[2], recv_sem=osem.at[3],
        device_id=(g, peer(FAR)), device_id_type=MESH,
    )
    to_far.start()
    pending.append(to_far.wait_send)

    l_cells.wait()
    for o in range(NB):
        cellv[o, 0:SEND, :] = cells[pl.ds(peer(o) * SEND, SEND), :]

    def rows_of(p, _):
        for i in range(4):
            for j in range(SEND):
                cell = cellv[4 * p + i, j : j + 1, :]
                r = (lax.shift_right_logical(cell, 7) & 1) * 128 + lax.shift_right_logical(cell, 8)
                one = jnp.where(iota((256, 128), 0) == r, 1.0, 0.0)
                rall[p, :, 512 * i + 128 * j : 512 * i + 128 * (j + 1)] = one.astype(BF16)
                rall8[p, :, 512 * i + 128 * j : 512 * i + 128 * (j + 1)] = one.astype(F8)
                cellv[4 * p + i, SEND + j : SEND + j + 1, :] = cell & 127
        return 0

    lax.fori_loop(0, 4, rows_of, 0)
    l_normal.wait()
    nrm[...] = jnp.zeros(nrm.shape, F32)
    for c in range(3):
        for j in range(SEND):
            nrm[pl.ds(4 * c + j, NB, stride=16), :] = normal[c, pl.ds(j, NB, stride=SEND), :]
    for o in range(NB):
        norms[o] = nrm[pl.ds(pl.multiple_of(peer(o) * 16, 16), 16), :]
    force_q[:, 0:8, :] = jnp.zeros((NV, 8, CY + 128), F32)
    force_q[:, 8 + CX : 16 + CX, :] = jnp.zeros((NV, 8, CY + 128), F32)
    force_q[:, 8 : 8 + CX, CY : CY + 128] = jnp.zeros((NV, CX, 128), F32)
    def answer(asked, shown):
        n = asked.shape[0] * 16
        asked = asked.reshape(n, 128)
        row_c = lax.shift_right_logical(iota((n, 128), 0), 2) & 3
        found = asked == iota((n, 128), 1).astype(F32)
        pick = jnp.concatenate([jnp.where(found & (row_c == c), 1.0, 0.0).astype(BF16) for c in range(3)], axis=1)
        return dot(pick, shown, NN).astype(BF16).reshape(n // 16, 16, 128)

    land_disp[ME] = answer(land_req[ME][None], dispc[...])[0]
    for first, last in CLASSES:
        blk_recv(lambda o: req.at[peer(o)], land_req, 0, range(first, last))
        resp[first:last] = answer(land_req[first:last], dispc[...])
        blk_send(lambda o: resp.at[o], land_disp, 1, range(first, last))

    acc[...] = jnp.zeros(acc.shape, F32)
    none16 = jnp.zeros((16, 128), BF16)

    def spread(p, _):
        @pl.when(p == FAR // 4)
        def _():
            to_far.wait_recv()
            land_disp[FAR] = answer(req[peer(FAR)][None], table[...])[0]

        for i in range(4):
            o = 4 * p + i

            @pl.when((o != ME) & (o != FAR))
            def _():
                pltpu.make_async_remote_copy(
                    src_ref=resp.at[o], dst_ref=land_disp.at[o], send_sem=bs.at[1, o], recv_sem=br.at[1, o],
                    device_id=(g, peer(FAR)), device_id_type=MESH,
                ).wait_recv()

            pltpu.make_async_copy(rbf_h.at[pl.ds(0, SEND)], rbf.at[o], rsem.at[o]).wait()
        for h in (0, 2):
            o = 4 * p + h
            x = jnp.concatenate(
                [
                    jnp.concatenate([land_disp[o], none16], axis=1),
                    jnp.concatenate([none16, land_disp[o + 1]], axis=1),
                ],
                axis=0,
            )
            weights = [rbf[o + i].reshape(SEND * 128, 128) for i in range(2)]
            moved = dot(x, jnp.concatenate(weights, axis=1), NT) * FORCING
            high = moved.astype(BF16).astype(F32)
            low = (moved - high) * LIFT
            for i in range(2):
                for j in range(SEND):
                    mask = iota((128, 128), 0) == cellv[o + i, SEND + j : SEND + j + 1, :]
                    at = 512 * (h + i) + 128 * j
                    for c in range(3):
                        r = 16 * i + 4 * c + j
                        vh = high[r : r + 1, 128 * j : 128 * (j + 1)]
                        vl = low[r : r + 1, 128 * j : 128 * (j + 1)]
                        bmat[128 * c : 128 * c + 128, at : at + 128] = jnp.where(mask, vh, 0.0).astype(BF16)
                        bmat8[128 * c : 128 * c + 128, at : at + 128] = jnp.where(mask, vl, 0.0).astype(F8)
        acc[...] += dot(bmat[...], rall[p], NT) + dot(bmat8[...], rall8[p], NT) * (1.0 / LIFT)
        return 0

    lax.fori_loop(0, 4, spread, 0)
    l_flow.wait()
    for c in range(3):
        s = acc[128 * c : 128 * c + 128, :]
        force_q[1 + c, 8 : 8 + CX, 0:128] += s[:, 0:128].T
        force_q[1 + c, 8 : 8 + CX, 128:256] += s[:, 128:256].T

    lane = iota((128, 128), 1)
    strip = lax.shift_right_logical((lane + 4) & 127, 3)
    packed = jnp.zeros((128, 128), F32)
    for v in range(NV):
        t = jnp.where(lane < 64, force_q[v, 8 : 8 + CX, 0:128], force_q[v, 8 : 8 + CX, 128:256])
        if v:
            t = pltpu.roll(t, 8 * v, 1)
        packed = jnp.where(strip == v, t, packed)
    lane64 = iota((64, 128), 1)
    pack[...] = jnp.where(((lane64 + 4) & 127) < 64, packed[0:64], pltpu.roll(packed[64:128], 64, 1))
    top_rows = force_q.at[:, pl.ds(8, 8), pl.ds(0, CY)]
    low_rows = force_q.at[:, pl.ds(CX, 8), pl.ds(0, CY)]
    halo = [
        (pack.at[pl.ds(0, 8)], land_corner.at[0], (g_dn, b_dn)),
        (pack.at[pl.ds(0, 8)], land_corner.at[1], (g_dn, b_up)),
        (pack.at[pl.ds(56, 8)], land_corner.at[2], (g_up, b_dn)),
        (pack.at[pl.ds(56, 8)], land_corner.at[3], (g_up, b_up)),
        (pack, land_right, (g, b_dn)),
        (pack, land_left, (g, b_up)),
        (top_rows, land_below, (g_dn, b)),
        (low_rows, land_above, (g_up, b)),
    ]
    halo = [
        pltpu.make_async_remote_copy(
            src_ref=s, dst_ref=d, send_sem=hs.at[i], recv_sem=hr.at[i], device_id=dev, device_id_type=MESH
        )
        for i, (s, d, dev) in enumerate(halo)
    ]
    for c in halo:
        c.start()
        pending.append(c.wait_send)

    is_up, is_dn = g < NG - 1, g > 0
    is_right, is_left = b < NB - 1, b > 0
    l_jx.wait()
    l_jy.wait()
    lane = iota((8, CY + 128), 1)
    sub = iota((8, CY + 128), 0)
    outside = ((lane >= CY) & (lane < CY + 64) & jnp.logical_not(is_right)) | (
        (lane >= CY + 64) & jnp.logical_not(is_left)
    )
    inside = jnp.where(outside, 0.0, TIME_STEP).astype(F32)
    ax = [[-0.5 * jx[u, v] for v in range(NV)] for u in range(NV)]
    ay = [[-0.5 * jy[u, v] for v in range(NV)] for u in range(NV)]

    def advance(cur, up, dn, rt, lt, start, scale):
        dx = [p - m for p, m in zip(up, dn)]
        dy = [p - m for p, m in zip(rt, lt)]
        out = []
        for u in range(NV):
            res = DAMPING * ((up[u] + dn[u]) + (rt[u] + lt[u])) - 4.0 * DAMPING * cur[u]
            for v in range(NV):
                res = res + (ax[u][v] * dx[v] + ay[u][v] * dy[v])
            out.append(start[u] + scale * res)
        return out

    def step(cur, prev, nxt, start, scale):
        up = [pltpu.roll(jnp.where(sub == 0, n, q), 7, 0) for n, q in zip(nxt, cur)]
        dn = [pltpu.roll(jnp.where(sub == 7, p, q), 1, 0) for p, q in zip(prev, cur)]
        rt = [pltpu.roll(q, CY + 127, 1) for q in cur]
        lt = [pltpu.roll(q, 1, 1) for q in cur]
        return advance(cur, up, dn, rt, lt, start, scale)

    def rows_at(ref, i):
        r = pl.multiple_of(i * 8, 8)
        return [ref[v, pl.ds(r, 8), :] for v in range(NV)]

    def stage(src, dst, rate, last):
        def tile_at(i):
            row_ok = jnp.where(i == 0, is_dn, jnp.where(i == 17, is_up, True))
            scale = jnp.where(row_ok, rate, 0.0).astype(F32) * inside
            prev, nxt = rows_at(src, jnp.maximum(i - 1, 0)), rows_at(src, jnp.minimum(i + 1, 17))
            new = step(rows_at(src, i), prev, nxt, rows_at(force_q, i), scale)
            for u in range(NV):
                if last:
                    qout[u, pl.ds(pl.multiple_of(i * 8 - 8, 8), 8), :] = new[u][:, 0:CY]
                else:
                    dst[u, pl.ds(pl.multiple_of(i * 8, 8), 8), :] = new[u]

        width = 8 if last else 9

        def body(p, _):
            for t in range(width):
                tile_at(width * p + t + (1 if last else 0))
            return 0

        lax.fori_loop(0, 2, body, 0)

    stage(force_q, qa, RATES[0], False)
    stage(qa, qb, RATES[1], False)
    stage(qb, qa, RATES[2], False)
    stage(qa, None, RATES[3], True)

    for c in halo:
        c.wait_recv()
    zero = jnp.zeros((8, CY + 128), F32)
    zero128 = jnp.zeros((8, 128), F32)

    def wide(x, ok):
        return jnp.concatenate([jnp.where(ok, x, 0.0), zero128], axis=1)

    start = [
        [wide(land_above[v], is_dn) for v in range(NV)],
        [zero] * NV,
        [zero] * NV,
        [wide(land_below[v], is_up) for v in range(NV)],
    ]
    for t in (0, 3):
        for v in range(NV):
            rows0[v, 8 * t : 8 * t + 8, :] = start[t][v]
    nothing = [zero] * NV
    for i, rate in enumerate(RATES):
        src, dst = ((rows0, rows1), (rows1, rows2), (rows2, rows1), (rows1, None))[i]
        for t in (1, 2) if dst is None else range(4):
            def at(k):
                if i == 0 and k in (1, 2):
                    return nothing
                return [src[v, 8 * k : 8 * k + 8, :] for v in range(NV)]

            first = [rows0[v, 8 * t : 8 * t + 8, :] for v in range(NV)] if t in (0, 3) else nothing
            scale = rate * inside
            if t in (0, 3):
                scale = jnp.where(is_dn if t == 0 else is_up, scale, 0.0)
            new = step(at(t), at(t - 1) if t in (1, 3) else nothing, at(t + 1) if t in (0, 2) else nothing, first, scale)
            for u in range(NV):
                if dst is None:
                    r = 0 if t == 1 else CX - 8
                    qout[u, r : r + 8, :] += new[u][:, 0:CY]
                else:
                    dst[u, 8 * t : 8 * t + 8, :] = new[u]

    def sides(right, left, ok):
        from_right = (iota(right.shape, 1) & 7) < 4
        return jnp.where(from_right, jnp.where(is_right & ok, right, 0.0), jnp.where(is_left & ok, left, 0.0))

    mid = sides(land_right[...], land_left[...], True)
    mid = jnp.concatenate([mid, pltpu.roll(mid, 64, 1)], axis=0)
    below = sides(land_corner[0], land_corner[1], is_up)
    above = pltpu.roll(sides(land_corner[2], land_corner[3], is_dn), 64, 1)
    ends = jnp.concatenate([below, jnp.zeros((112, 128), F32), above], axis=0)
    strips = pltpu.roll(jnp.concatenate([mid.T, ends.T], axis=1), 4, 0)
    sub2 = iota((8, 256), 0)
    lane2 = iota((8, 256), 1)
    out_rows = ((lane2 >= 128) & (lane2 < 192) & jnp.logical_not(is_up)) | ((lane2 >= 192) & jnp.logical_not(is_dn))
    inside2 = jnp.where(out_rows, 0.0, TIME_STEP).astype(F32)
    done = []
    for near_side in (True, False):
        start = []
        for v in range(NV):
            x = strips[8 * v : 8 * v + 8]
            start.append(jnp.where((sub2 < 4) == near_side, x, 0.0))
        cur = start
        for rate in RATES:
            up = [pltpu.roll(q, 255, 1) for q in cur]
            dn = [pltpu.roll(q, 1, 1) for q in cur]
            rt = [jnp.where(sub2 == 7, 0.0, pltpu.roll(q, 7, 0)) for q in cur]
            lt = [jnp.where(sub2 == 0, 0.0, pltpu.roll(q, 1, 0)) for q in cur]
            cur = advance(cur, up, dn, rt, lt, start, rate * inside2)
        done.append([q[:, 0:128] for q in cur])
    sub1 = iota((8, 128), 0)
    joined = [jnp.where(sub1 < 4, far, near) for near, far in zip(*done)]
    joined = jnp.concatenate(joined + [jnp.zeros((128 - 8 * NV, 128), F32)], axis=0).T
    lane1 = iota((128, 128), 1)

    def add_columns(v):
        x = pltpu.roll(joined, (124 - 8 * v) % 128, 1)
        qout[v, :, 0:128] += jnp.where(lane1 < 4, x, 0.0)
        qout[v, :, 128:256] += jnp.where(lane1 >= 124, x, 0.0)

    add_columns(NV - 1)

    pres = qout[4]
    pres = jnp.concatenate([pres[:, 0:128].T, pres[:, 128:256].T], axis=1)
    ph, plow = split(pres)
    pres2 = jnp.concatenate([ph, plow], axis=0)
    row16 = iota((16, 128), 0)

    def gather(o, cols):
        h = dot(pres2, cols, NN)
        h = h[0:128] + h[128:256]
        n16 = norms[o]
        forces = []
        for j in range(SEND):
            mask = iota((128, 128), 0) == cellv[o, SEND + j : SEND + j + 1, :]
            p = jnp.sum(jnp.where(mask, h[:, 128 * j : 128 * (j + 1)], 0.0), axis=0, keepdims=True)
            forces.append(jnp.where((row16 & 3) == j, n16 * p, 0.0).astype(BF16))
        return jnp.concatenate(forces, axis=1)

    def gather_four(q, _):
        for first in (0, 2):
            forces = [gather(4 * q + first + i, rall[q, :, 512 * (first + i) : 512 * (first + i + 1)]) for i in range(2)]
            weights = [rbf[4 * q + first + i].reshape(SEND * 128, 128) for i in range(2)]
            both = dot(jnp.concatenate(forces, axis=0), jnp.concatenate(weights, axis=1), NN)
            load_out[4 * q + first] = both[0:16, 0:128]
            load_out[4 * q + first + 1] = both[16:32, 128:256]
        return 0

    for q in (1, 3, 2, 0):
        lax.fori_loop(q, q + 1, gather_four, 0)
        blk_send(lambda o: load_out.at[o], land_load, 3, [o for o in reversed(range(4 * q, 4 * q + 4)) if o != ME])
    land_load[ME] = load_out[ME]
    for v in range(NV - 1):
        add_columns(v)
    flow_out = pltpu.make_async_copy(qout, flow_o, osem.at[0])
    flow_out.start()
    pending.append(flow_out.wait)

    l_secv.wait()
    zero8 = jnp.zeros((8, 128), F32)

    def gram_row(i, _):
        for c in range(3):
            x = secv[:, c, pl.ds(i, 1), :].reshape(COLS, 128)
            x = jnp.where((i >= off) & (i < off + OWN), x, 0.0)
            hi, lo = split(jnp.concatenate([x, zero8], axis=0))
            at = pl.multiple_of((c * WIN + i) * 128, 128)
            zmat[0:32, pl.ds(at, 128)] = hi
            zmat[32:64, pl.ds(at, 128)] = lo
        return 0

    lax.fori_loop(0, WIN, gram_row, 0)
    zz = zmat[...]
    top = dot(zz, zz[0:32], NT)
    low = dot(zz, zz[32:64], NT)
    gram = top[0:32] + top[32:64] + low[0:32] + low[32:64]
    gsend[...] = jnp.zeros(gsend.shape, F32)
    gsend[:, 0:32] = gram
    land_gg[g] = gsend[...]
    grp_send(lambda d: gsend, land_gg, 0)

    row = iota((COLS, 128), 0)
    lane = iota((COLS, 128), 1)
    wrow = iota((48, 128), 0) & 15
    mine = (wrow >= off) & (wrow < off + OWN)
    d_in = jnp.where(mine, disp[:, pl.ds(a, WIN), :].reshape(48, 128), 0.0)
    rhs_in = jnp.sum(secv[...].reshape(COLS, 48, 128) * d_in[None], axis=1)
    diag = lane == row + 32

    blk_recv(lambda o: req.at[peer(o)], land_req, 0, [FAR])
    asked_t = land_req[...].reshape(NB * 16, 128).T[0:1, :]
    rr, kk = iota((48, NB * 16), 0), iota((48, NB * 16), 1)
    w = rr & 15
    same_c = (lax.shift_right_logical(kk, 2) & 3) == lax.shift_right_logical(rr, 4)
    for p in range(NG):
        first = (p * OWN) // 8 * 8
        skip = p * OWN - first
        ok = same_c & (w >= skip) & (w < skip + OWN)
        oht[48 * p : 48 * (p + 1), :] = jnp.where(ok & (asked_t == (w + first).astype(F32)), 1.0, 0.0).astype(BF16)

    blk_recv(lambda o: load_out.at[o], land_load, 3)
    got = land_load[...].reshape(NB * 16, 128)
    hi, lo = split(got)
    sums = dot(oht[...], jnp.concatenate([hi, lo], axis=1), NN)
    part[...] = (sums[:, 0:128] + sums[:, 128:256]).reshape(NG, 48, 128)
    land_part[g] = part[g]
    grp_send(lambda d: part.at[d], land_part, 1)
    l_flex.wait()

    def project(i, _):
        at = pl.multiple_of(128 * i, 128)
        hi, lo = split(flex[i])
        flexhl[pl.ds(at, 128), 0:128] = hi
        flexhl[pl.ds(at, 128), 128:256] = lo
        vh, vl = split(jnp.concatenate([secv[:, c, pl.ds(i, 1), :].reshape(COLS, 128) for c in range(3)], axis=0))
        u = dot(jnp.concatenate([vh, vl], axis=0), hi, NN)
        u = u[0:72] + u[72:144] + dot(vh, lo, NN)
        for c in range(3):
            uwin[:, c, pl.ds(i, 1), :] = u[COLS * c : COLS * (c + 1)].reshape(COLS, 1, 128)
        return 0

    lax.fori_loop(0, WIN, project, 0)
    grp_recv(lambda d: gsend, land_gg, 0)
    gsum[...] = jnp.sum(land_gg[...], axis=0)
    land_gb[ME] = gsum[...]
    blk_send(lambda o: gsum, land_gb, 2)
    grp_recv(lambda d: part.at[d], land_part, 1)
    tile_loads = jnp.sum(land_part[...], axis=0)

    prod = jnp.sum(uwin[...].reshape(COLS, 48, 128) * tile_loads[None], axis=1) - rhs_in
    rhs = jnp.sum(prod, axis=1, keepdims=True)
    rhs = jnp.sum(jnp.where(diag, rhs, 0.0), axis=0, keepdims=True)
    rmsg[...] = jnp.broadcast_to(rhs, (8, 128))
    land_rg[g] = rmsg[...]
    grp_send(lambda d: rmsg, land_rg, 2)
    hi, lo = split(tile_loads)
    lhs = jnp.concatenate(
        [jnp.concatenate([hi, hi], axis=1), jnp.concatenate([lo, jnp.zeros_like(lo)], axis=1)], axis=0
    )
    tilde = jnp.zeros((48, 128), F32)
    for u in range(WIN // 2):
        o = dot(lhs, flexhl[256 * u : 256 * (u + 1), :], NT)
        o = o[0:48] + o[48:96]
        tilde = jnp.where(wrow == 2 * u, o[:, 0:128], tilde)
        tilde = jnp.where(wrow == 2 * u + 1, o[:, 128:256], tilde)
    tmsg[...] = jnp.where(mine, tilde, 0.0)
    land_t[g] = tmsg[...]
    grp_send(lambda d: tmsg, land_t, 3)
    grp_recv(lambda d: rmsg, land_rg, 2)
    rsend[...] = jnp.sum(land_rg[...], axis=0)
    land_r[ME] = rsend[...]
    blk_send(lambda o: rsend, land_r, 4)
    l_secw.wait()
    blk_recv(lambda o: gsum, land_gb, 2)
    gram = jnp.sum(land_gb[...], axis=0)[0:COLS]
    row = iota((COLS, 128), 0)
    lane = iota((COLS, 128), 1)
    m = jnp.where(lane < COLS, gram, jnp.where(lane == row + 32, 1.0, 0.0))
    fac = jnp.zeros((COLS, 128), F32)
    for k in range(COLS):
        pivot = lax.rsqrt(jnp.broadcast_to(m[k : k + 1, k : k + 1], (1, 128)))
        r = m[k : k + 1, :] * pivot
        col = jnp.broadcast_to(m[:, k : k + 1], (COLS, 128)) * pivot
        fac = jnp.where(row == k, r, fac)
        m = m - jnp.where(row > k, col * r, 0.0)
    linv[...] = jnp.where((lane >= 32) & (lane < 32 + COLS), fac, 0.0)
    grp_recv(lambda d: tmsg, land_t, 3)
    blk_recv(lambda o: rsend, land_r, 4)
    rhs = jnp.sum(land_r[...], axis=0)[0:1]

    li = linv[...]
    y = jnp.sum(li * rhs, axis=1, keepdims=True)
    x = jnp.sum(li * y, axis=0, keepdims=True)
    x = -jnp.sum(jnp.where(diag, x, 0.0), axis=1, keepdims=True)
    coef[...] = jnp.broadcast_to(x, (COLS, 128))

    def update(p, _):
        for c in range(3):
            even, odd = land_t[2 * p, 16 * c : 16 * c + 16, :], land_t[2 * p + 1, 16 * c : 16 * c + 16, :]
            for q, t in enumerate((even[0:8], even[8:16] + odd[0:8], odd[8:16])):
                at = pl.multiple_of(24 * p + 8 * q, 8)
                for k in range(COLS):
                    t = t + coef[k : k + 1, :] * secw[k, c, pl.ds(at, 8), :]
                dout[c, pl.ds(at, 8), :] = t
        return 0

    lax.fori_loop(0, NG // 2, update, 0)
    disp_out = pltpu.make_async_copy(dout, disp_o, osem.at[1])
    disp_out.start()
    pending.append(disp_out.wait)

    finish()


def deliver(flow, disp, flow_out, disp_out, sems):
    copies = [pltpu.make_async_copy(flow, flow_out, sems.at[0]), pltpu.make_async_copy(disp, disp_out, sems.at[1])]
    for c in copies:
        c.start()
    for c in copies:
        c.wait()


def stay(x):
    return pltpu.with_memory_space_constraint(x, pltpu.HBM)


def on_device(flow_state, jx, jy, slot_tile, slot_cells, slot_normal, slot_rbf, disp_in, flex, secv, secw):
    hbm = pl.BlockSpec(memory_space=pl.ANY)
    vm, dma = pltpu.VMEM, pltpu.SemaphoreType.DMA
    state = (NV, CX + 16, CY + 128)
    scratch = [
        pltpu.SMEM((NV, NV), F32), pltpu.SMEM((NV, NV), F32),
        vm((1, 64), jnp.int32), vm((64, 128), jnp.int32), vm((3, 64, 128), F32), vm((NB, SEND, 128, 128), BF16),
        vm((3, ST, 128), F32), vm((WIN, 128, 128), F32), vm((COLS, 3, WIN, 128), F32), vm((COLS, 3, ST, 128), F32),
        vm(state, F32), vm(state, F32), vm(state, F32), vm((NV, CX, CY), F32),
        vm((NV, 32, CY + 128), F32), vm((NV, 32, CY + 128), F32), vm((NV, 32, CY + 128), F32),
        vm((NB, 16, 128), F32), vm((NB, 16, 128), F32), vm((NB, 16, 128), BF16), vm((NB, 16, 128), BF16),
        vm((384, 128), BF16),
        vm((NB, 8, 128), jnp.int32), vm((4, 256, 2048), BF16), vm((4, 256, 2048), F8),
        vm((384, 2048), BF16), vm((384, 2048), F8), vm((384, 256), F32), vm((384, 128), BF16),
        vm((64, 128), F32),
        vm((NV, 8, CY), F32), vm((NV, 8, CY), F32), vm((64, 128), F32), vm((64, 128), F32), vm((4, 8, 128), F32),
        vm((256, 128), F32), vm((NB, 16, 128), F32), vm((NB, 16, 128), F32), vm((NB, 16, 128), F32), vm((384, 256), BF16),
        vm((NG, 48, 128), F32), vm((NG, 48, 128), F32),
        vm((WIN * 128, 256), BF16), vm((COLS, 3, WIN, 128), F32), vm((64, 48 * 128), BF16),
        vm((32, 128), F32), vm((NG, 32, 128), F32), vm((32, 128), F32), vm((NB, 32, 128), F32), vm((COLS, 128), F32),
        vm((8, 128), F32), vm((NG, 8, 128), F32), vm((48, 128), F32), vm((NG, 48, 128), F32),
        vm((8, 128), F32), vm((NB, 8, 128), F32), vm((COLS, 128), F32), vm((3, ST, 128), F32),
        dma((10,)), dma((NB,)), dma((4,)),
        dma((5, NB)), dma((5, NB)), dma((4, NG)), dma((4, NG)), dma((8,)), dma((8,)),
    ]
    flow_out, disp_out = pl.pallas_call(
        kernel,
        out_shape=(
            vm((NV, CX, CY), F32),
            vm((3, ST, 128), F32),
        ),
        in_specs=[hbm] * 11,
        out_specs=(hbm, hbm),
        scratch_shapes=scratch,
        compiler_params=pltpu.CompilerParams(
            collective_id=0, has_side_effects=True, vmem_limit_bytes=48 * 1024 * 1024
        ),
    )(*[
        stay(x) for x in (
            flow_state, jx, jy, slot_tile.reshape(1, -1), slot_cells, jnp.transpose(slot_normal, (1, 0, 2)), slot_rbf,
            jnp.transpose(disp_in, (1, 0, 2)), flex, jnp.transpose(secv, (0, 2, 1, 3)), jnp.transpose(secw, (0, 2, 1, 3)),
        )
    ])
    flow_out, disp_out = pl.pallas_call(
        deliver,
        out_shape=(jax.ShapeDtypeStruct(flow_out.shape, F32), jax.ShapeDtypeStruct(disp_out.shape, F32)),
        in_specs=[hbm, hbm],
        out_specs=(hbm, hbm),
        scratch_shapes=[dma((2,))],
        compiler_params=pltpu.CompilerParams(vmem_limit_bytes=1024 * 1024),
    )(flow_out, disp_out)
    return flow_out, jnp.transpose(disp_out, (1, 0, 2))


def solution(mesh):
    placed = (
        P(None, "grp", "blk"), P(), P(),
        P(("grp", "blk")), P(("grp", "blk"), None),
        P(("grp", "blk"), None, None), P(("grp", "blk"), None, None),
        P("blk", None, None), P("blk", None, None),
        P(None, "blk", None, None), P(None, "blk", None, None),
    )
    return jax.shard_map(
        on_device, mesh=mesh, in_specs=placed,
        out_specs=(P(None, "grp", "blk"), P("blk", None, None)), check_vma=False,
    )
```

```python
import functools

import jax
import jax.numpy as jnp
from jax import lax
from jax.experimental import pallas as pl
from jax.experimental.pallas import tpu as pltpu
from jax.sharding import PartitionSpec as P

RATES = (0.25, 1.0 / 3.0, 0.5, 1.0)
TIME_STEP = 0.4
DAMPING = 0.25
FORCING = 1.0
F32 = jnp.float32
BF16 = jnp.bfloat16
F8 = jnp.float8_e4m3fn
LIFT = 64.0
MESH = pl.DeviceIdType.MESH
NG, NB = 8, 16
SEND, ST, COLS, NV = 4, 96, 24, 5
CX, CY = 128, 256
OWN = ST // NG
WIN = 16
HOPS = ((0, 0), (0, 1), (0, 3), (1, 0), (3, 0), (2, 2), (1, 1), (1, 3), (3, 1), (3, 3), (0, 2), (2, 0), (1, 2), (3, 2), (2, 1), (2, 3))
BACK = tuple(HOPS.index(((4 - dy) % 4, (4 - dz) % 4)) for dy, dz in HOPS)
ME = HOPS.index((0, 0))
CLASSES = ((1, 5), (6, 12), (12, 16))
FAR = 5
NN = (((1,), (0,)), ((), ()))
NT = (((1,), (1,)), ((), ()))


def iota(shape, dim):
    return lax.broadcasted_iota(jnp.int32, shape, dim)


def dot(a, b, dims):
    return lax.dot_general(a, b, dims, preferred_element_type=F32)


def split(x):
    hi = x.astype(BF16)
    return hi, (x - hi.astype(F32)).astype(BF16)


def window(g):
    return lax.div(g * OWN, 8) * 8


def kernel(
    flow_h, jx_h, jy_h, tile_h, cells_h, normal_h, rbf_h, disp_h, flex_h, secv_h, secw_h,
    flow_o, disp_o,
    jx, jy, tile, cells, normal, rbf, disp, flex, secv, secw,
    force_q, qa, qb, qout, rows0, rows1, rows2,
    req, land_req, resp, land_disp, dispc, cellv, rall, rall8, bmat, bmat8, acc, table, pack,
    land_below, land_above, land_right, land_left, land_corner,
    nrm, norms, load_out, land_load, oht, part, land_part,
    flexhl, uwin, zmat, gsend, land_gg, gsum, land_gb, linv,
    rmsg, land_rg, tmsg, land_t, rsend, land_r, coef, dout,
    lsem, rsem, osem, bs, br, gs, gr, hs, hr,
):
    g = lax.axis_index("grp")
    b = lax.axis_index("blk")
    y, z = lax.div(b, 4), lax.rem(b, 4)
    a = pl.multiple_of(window(g), 8)
    off = g * OWN - window(g)

    def peer(o):
        return lax.rem(y + HOPS[o][0], 4) * 4 + lax.rem(z + HOPS[o][1], 4)

    loads = [
        (tile_h, tile),
        (cells_h, cells),
        (disp_h, disp),
        (secv_h.at[:, :, pl.ds(a, WIN), :], secv),
        (flow_h, force_q.at[:, pl.ds(8, CX), pl.ds(0, CY)]),
        (normal_h, normal),
        (flex_h.at[pl.ds(a, WIN)], flex),
        (jx_h, jx),
        (jy_h, jy),
        (secw_h, secw),
    ]
    loads = [pltpu.make_async_copy(s, d, lsem.at[i]) for i, (s, d) in enumerate(loads)]
    l_tile, l_cells, l_disp, l_secv, l_flow, l_normal, l_flex, l_jx, l_jy, l_secw = loads
    l_rbf = [
        pltpu.make_async_copy(rbf_h.at[pl.ds(peer(o) * SEND, SEND)], rbf.at[o], rsem.at[o]) for o in range(NB)
    ]
    l_tile.start()

    barrier = pltpu.get_barrier_semaphore()
    g_up, g_dn = lax.rem(g + 1, NG), lax.rem(g + NG - 1, NG)
    b_up, b_dn = lax.rem(b + 1, NB), lax.rem(b + NB - 1, NB)
    hello = [(g, peer(o)) for o in reversed(range(NB)) if o != ME]
    hello += [(g_dn, b_dn), (g_dn, b_up), (g_up, b_dn), (g_up, b_up)]
    hello += [(lax.rem(g + o, NG), b) for o in range(1, NG)]
    for dev in hello:
        pl.semaphore_signal(barrier, inc=1, device_id=dev, device_id_type=MESH)

    for c in loads[1:4] + l_rbf + loads[4:]:
        c.start()

    def blk_copy(src, land, ph, o):
        return pltpu.make_async_remote_copy(
            src_ref=src(o), dst_ref=land.at[BACK[o]], send_sem=bs.at[ph, o], recv_sem=br.at[ph, BACK[o]],
            device_id=(g, peer(o)), device_id_type=MESH,
        )

    def grp_copy(src, dst, ph, o, dev):
        return pltpu.make_async_remote_copy(
            src_ref=src, dst_ref=dst, send_sem=gs.at[ph, o], recv_sem=gr.at[ph, o],
            device_id=(dev, b), device_id_type=MESH,
        )

    def each(n, step):
        def body(o, _):
            step(o)
            return 0

        lax.fori_loop(1, n, body, 0)

    pending = []

    def finish():
        for wait in pending:
            wait()

    far_first = [FAR] + [o for o in reversed(range(NB)) if o not in (ME, FAR)]

    def blk_send(src, land, ph, peers=far_first):
        for o in peers:
            copy = blk_copy(src, land, ph, o)
            copy.start()
            pending.append(copy.wait_send)

    def blk_recv(src, land, ph, peers=far_first[::-1]):
        for o in peers:
            pltpu.make_async_remote_copy(
                src_ref=src(o), dst_ref=land.at[o], send_sem=bs.at[ph, o], recv_sem=br.at[ph, o],
                device_id=(g, peer(o)), device_id_type=MESH,
            ).wait_recv()

    def grp_send(src, land, ph):
        def step(o):
            d = lax.rem(g + o, NG)
            grp_copy(src(d), land.at[g], ph, o, d).start()

        def last(o):
            grp_copy(src(0), land.at[0], ph, o, 0).wait_send()

        each(NG, step)
        pending.append(lambda: each(NG, last))

    def grp_recv(src, land, ph):
        def step(o):
            d = lax.rem(g + NG - o, NG)
            grp_copy(src(d), land.at[d], ph, o, d).wait_recv()

        each(NG, step)

    l_tile.wait()
    row = iota((NB * 16, 64), 0)
    hit = iota((NB * 16, 64), 1) == lax.shift_right_logical(row, 4) * SEND + (row & 3)
    wanted = jnp.sum(jnp.where(hit, tile[...].astype(F32), 0.0), axis=1, keepdims=True)
    row = iota((NB * 16, 128), 0)
    wanted = jnp.where((row & 15) < 12, jnp.broadcast_to(wanted, (NB * 16, 128)), -1.0)
    req[...] = wanted.reshape(NB, 16, 128)
    land_req[ME] = req[b]

    pl.semaphore_wait(barrier, len(hello))
    blk_send(lambda o: req.at[peer(o)], land_req, 0)

    l_disp.wait()
    dispc[...] = jnp.zeros(dispc.shape, BF16)
    for c in range(3):
        dispc[128 * c : 128 * c + ST, :] = disp[c].astype(BF16)
    to_far = pltpu.make_async_remote_copy(
        src_ref=dispc, dst_ref=table, send_sem=osem.at[2], recv_sem=osem.at[3],
        device_id=(g, peer(FAR)), device_id_type=MESH,
    )
    to_far.start()
    pending.append(to_far.wait_send)

    l_cells.wait()
    for o in range(NB):
        cellv[o, 0:SEND, :] = cells[pl.ds(peer(o) * SEND, SEND), :]

    def rows_of(p, _):
        for i in range(4):
            for j in range(SEND):
                cell = cellv[4 * p + i, j : j + 1, :]
                r = (lax.shift_right_logical(cell, 7) & 1) * 128 + lax.shift_right_logical(cell, 8)
                one = jnp.where(iota((256, 128), 0) == r, 1.0, 0.0)
                rall[p, :, 512 * i + 128 * j : 512 * i + 128 * (j + 1)] = one.astype(BF16)
                rall8[p, :, 512 * i + 128 * j : 512 * i + 128 * (j + 1)] = one.astype(F8)
                cellv[4 * p + i, SEND + j : SEND + j + 1, :] = cell & 127
        return 0

    lax.fori_loop(0, 4, rows_of, 0)
    l_normal.wait()
    nrm[...] = jnp.zeros(nrm.shape, F32)
    for c in range(3):
        for j in range(SEND):
            nrm[pl.ds(4 * c + j, NB, stride=16), :] = normal[c, pl.ds(j, NB, stride=SEND), :]
    for o in range(NB):
        norms[o] = nrm[pl.ds(pl.multiple_of(peer(o) * 16, 16), 16), :]
    force_q[:, 0:8, :] = jnp.zeros((NV, 8, CY + 128), F32)
    force_q[:, 8 + CX : 16 + CX, :] = jnp.zeros((NV, 8, CY + 128), F32)
    force_q[:, 8 : 8 + CX, CY : CY + 128] = jnp.zeros((NV, CX, 128), F32)
    def answer(asked, shown):
        n = asked.shape[0] * 16
        asked = asked.reshape(n, 128)
        row_c = lax.shift_right_logical(iota((n, 128), 0), 2) & 3
        found = asked == iota((n, 128), 1).astype(F32)
        pick = jnp.concatenate([jnp.where(found & (row_c == c), 1.0, 0.0).astype(BF16) for c in range(3)], axis=1)
        return dot(pick, shown, NN).astype(BF16).reshape(n // 16, 16, 128)

    land_disp[ME] = answer(land_req[ME][None], dispc[...])[0]
    for first, last in CLASSES:
        blk_recv(lambda o: req.at[peer(o)], land_req, 0, range(first, last))
        resp[first:last] = answer(land_req[first:last], dispc[...])
        blk_send(lambda o: resp.at[o], land_disp, 1, range(first, last))

    acc[...] = jnp.zeros(acc.shape, F32)
    none16 = jnp.zeros((16, 128), BF16)

    def spread(p, _):
        @pl.when(p == FAR // 4)
        def _():
            to_far.wait_recv()
            land_disp[FAR] = answer(req[peer(FAR)][None], table[...])[0]

        for i in range(4):
            o = 4 * p + i

            @pl.when((o != ME) & (o != FAR))
            def _():
                pltpu.make_async_remote_copy(
                    src_ref=resp.at[o], dst_ref=land_disp.at[o], send_sem=bs.at[1, o], recv_sem=br.at[1, o],
                    device_id=(g, peer(FAR)), device_id_type=MESH,
                ).wait_recv()

            pltpu.make_async_copy(rbf_h.at[pl.ds(0, SEND)], rbf.at[o], rsem.at[o]).wait()
        for h in (0, 2):
            o = 4 * p + h
            x = jnp.concatenate(
                [
                    jnp.concatenate([land_disp[o], none16], axis=1),
                    jnp.concatenate([none16, land_disp[o + 1]], axis=1),
                ],
                axis=0,
            )
            weights = [rbf[o + i].reshape(SEND * 128, 128) for i in range(2)]
            moved = dot(x, jnp.concatenate(weights, axis=1), NT) * FORCING
            high = moved.astype(BF16).astype(F32)
            low = (moved - high) * LIFT
            for i in range(2):
                for j in range(SEND):
                    mask = iota((128, 128), 0) == cellv[o + i, SEND + j : SEND + j + 1, :]
                    at = 512 * (h + i) + 128 * j
                    for c in range(3):
                        r = 16 * i + 4 * c + j
                        vh = high[r : r + 1, 128 * j : 128 * (j + 1)]
                        vl = low[r : r + 1, 128 * j : 128 * (j + 1)]
                        bmat[128 * c : 128 * c + 128, at : at + 128] = jnp.where(mask, vh, 0.0).astype(BF16)
                        bmat8[128 * c : 128 * c + 128, at : at + 128] = jnp.where(mask, vl, 0.0).astype(F8)
        acc[...] += dot(bmat[...], rall[p], NT) + dot(bmat8[...], rall8[p], NT) * (1.0 / LIFT)
        return 0

    lax.fori_loop(0, 4, spread, 0)
    l_flow.wait()
    for c in range(3):
        s = acc[128 * c : 128 * c + 128, :]
        force_q[1 + c, 8 : 8 + CX, 0:128] += s[:, 0:128].T
        force_q[1 + c, 8 : 8 + CX, 128:256] += s[:, 128:256].T

    lane = iota((128, 128), 1)
    strip = lax.shift_right_logical((lane + 4) & 127, 3)
    packed = jnp.zeros((128, 128), F32)
    for v in range(NV):
        t = jnp.where(lane < 64, force_q[v, 8 : 8 + CX, 0:128], force_q[v, 8 : 8 + CX, 128:256])
        if v:
            t = pltpu.roll(t, 8 * v, 1)
        packed = jnp.where(strip == v, t, packed)
    lane64 = iota((64, 128), 1)
    pack[...] = jnp.where(((lane64 + 4) & 127) < 64, packed[0:64], pltpu.roll(packed[64:128], 64, 1))
    top_rows = force_q.at[:, pl.ds(8, 8), pl.ds(0, CY)]
    low_rows = force_q.at[:, pl.ds(CX, 8), pl.ds(0, CY)]
    halo = [
        (pack.at[pl.ds(0, 8)], land_corner.at[0], (g_dn, b_dn)),
        (pack.at[pl.ds(0, 8)], land_corner.at[1], (g_dn, b_up)),
        (pack.at[pl.ds(56, 8)], land_corner.at[2], (g_up, b_dn)),
        (pack.at[pl.ds(56, 8)], land_corner.at[3], (g_up, b_up)),
        (pack, land_right, (g, b_dn)),
        (pack, land_left, (g, b_up)),
        (top_rows, land_below, (g_dn, b)),
        (low_rows, land_above, (g_up, b)),
    ]
    halo = [
        pltpu.make_async_remote_copy(
            src_ref=s, dst_ref=d, send_sem=hs.at[i], recv_sem=hr.at[i], device_id=dev, device_id_type=MESH
        )
        for i, (s, d, dev) in enumerate(halo)
    ]
    for c in halo:
        c.start()
        pending.append(c.wait_send)

    is_up, is_dn = g < NG - 1, g > 0
    is_right, is_left = b < NB - 1, b > 0
    l_jx.wait()
    l_jy.wait()
    lane = iota((8, CY + 128), 1)
    sub = iota((8, CY + 128), 0)
    outside = ((lane >= CY) & (lane < CY + 64) & jnp.logical_not(is_right)) | (
        (lane >= CY + 64) & jnp.logical_not(is_left)
    )
    inside = jnp.where(outside, 0.0, TIME_STEP).astype(F32)
    ax = [[-0.5 * jx[u, v] for v in range(NV)] for u in range(NV)]
    ay = [[-0.5 * jy[u, v] for v in range(NV)] for u in range(NV)]

    def advance(cur, up, dn, rt, lt, start, scale):
        dx = [p - m for p, m in zip(up, dn)]
        dy = [p - m for p, m in zip(rt, lt)]
        out = []
        for u in range(NV):
            res = DAMPING * ((up[u] + dn[u]) + (rt[u] + lt[u])) - 4.0 * DAMPING * cur[u]
            for v in range(NV):
                res = res + (ax[u][v] * dx[v] + ay[u][v] * dy[v])
            out.append(start[u] + scale * res)
        return out

    def step(cur, prev, nxt, start, scale):
        up = [pltpu.roll(jnp.where(sub == 0, n, q), 7, 0) for n, q in zip(nxt, cur)]
        dn = [pltpu.roll(jnp.where(sub == 7, p, q), 1, 0) for p, q in zip(prev, cur)]
        rt = [pltpu.roll(q, CY + 127, 1) for q in cur]
        lt = [pltpu.roll(q, 1, 1) for q in cur]
        return advance(cur, up, dn, rt, lt, start, scale)

    def rows_at(ref, i):
        r = pl.multiple_of(i * 8, 8)
        return [ref[v, pl.ds(r, 8), :] for v in range(NV)]

    def stage(src, dst, rate, last):
        def tile_at(i):
            row_ok = jnp.where(i == 0, is_dn, jnp.where(i == 17, is_up, True))
            scale = jnp.where(row_ok, rate, 0.0).astype(F32) * inside
            prev, nxt = rows_at(src, jnp.maximum(i - 1, 0)), rows_at(src, jnp.minimum(i + 1, 17))
            new = step(rows_at(src, i), prev, nxt, rows_at(force_q, i), scale)
            for u in range(NV):
                if last:
                    qout[u, pl.ds(pl.multiple_of(i * 8 - 8, 8), 8), :] = new[u][:, 0:CY]
                else:
                    dst[u, pl.ds(pl.multiple_of(i * 8, 8), 8), :] = new[u]

        width = 8 if last else 9

        def body(p, _):
            for t in range(width):
                tile_at(width * p + t + (1 if last else 0))
            return 0

        lax.fori_loop(0, 2, body, 0)

    stage(force_q, qa, RATES[0], False)
    stage(qa, qb, RATES[1], False)
    stage(qb, qa, RATES[2], False)
    stage(qa, None, RATES[3], True)

    for c in halo:
        c.wait_recv()
    zero = jnp.zeros((8, CY + 128), F32)
    zero128 = jnp.zeros((8, 128), F32)

    def wide(x, ok):
        return jnp.concatenate([jnp.where(ok, x, 0.0), zero128], axis=1)

    start = [
        [wide(land_above[v], is_dn) for v in range(NV)],
        [zero] * NV,
        [zero] * NV,
        [wide(land_below[v], is_up) for v in range(NV)],
    ]
    for t in (0, 3):
        for v in range(NV):
            rows0[v, 8 * t : 8 * t + 8, :] = start[t][v]
    nothing = [zero] * NV
    for i, rate in enumerate(RATES):
        src, dst = ((rows0, rows1), (rows1, rows2), (rows2, rows1), (rows1, None))[i]
        for t in (1, 2) if dst is None else range(4):
            def at(k):
                if i == 0 and k in (1, 2):
                    return nothing
                return [src[v, 8 * k : 8 * k + 8, :] for v in range(NV)]

            first = [rows0[v, 8 * t : 8 * t + 8, :] for v in range(NV)] if t in (0, 3) else nothing
            scale = rate * inside
            if t in (0, 3):
                scale = jnp.where(is_dn if t == 0 else is_up, scale, 0.0)
            new = step(at(t), at(t - 1) if t in (1, 3) else nothing, at(t + 1) if t in (0, 2) else nothing, first, scale)
            for u in range(NV):
                if dst is None:
                    r = 0 if t == 1 else CX - 8
                    qout[u, r : r + 8, :] += new[u][:, 0:CY]
                else:
                    dst[u, 8 * t : 8 * t + 8, :] = new[u]

    def sides(right, left, ok):
        from_right = (iota(right.shape, 1) & 7) < 4
        return jnp.where(from_right, jnp.where(is_right & ok, right, 0.0), jnp.where(is_left & ok, left, 0.0))

    mid = sides(land_right[...], land_left[...], True)
    mid = jnp.concatenate([mid, pltpu.roll(mid, 64, 1)], axis=0)
    below = sides(land_corner[0], land_corner[1], is_up)
    above = pltpu.roll(sides(land_corner[2], land_corner[3], is_dn), 64, 1)
    ends = jnp.concatenate([below, jnp.zeros((112, 128), F32), above], axis=0)
    strips = pltpu.roll(jnp.concatenate([mid.T, ends.T], axis=1), 4, 0)
    sub2 = iota((8, 256), 0)
    lane2 = iota((8, 256), 1)
    out_rows = ((lane2 >= 128) & (lane2 < 192) & jnp.logical_not(is_up)) | ((lane2 >= 192) & jnp.logical_not(is_dn))
    inside2 = jnp.where(out_rows, 0.0, TIME_STEP).astype(F32)
    done = []
    for near_side in (True, False):
        start = []
        for v in range(NV):
            x = strips[8 * v : 8 * v + 8]
            start.append(jnp.where((sub2 < 4) == near_side, x, 0.0))
        cur = start
        for rate in RATES:
            up = [pltpu.roll(q, 255, 1) for q in cur]
            dn = [pltpu.roll(q, 1, 1) for q in cur]
            rt = [jnp.where(sub2 == 7, 0.0, pltpu.roll(q, 7, 0)) for q in cur]
            lt = [jnp.where(sub2 == 0, 0.0, pltpu.roll(q, 1, 0)) for q in cur]
            cur = advance(cur, up, dn, rt, lt, start, rate * inside2)
        done.append([q[:, 0:128] for q in cur])
    sub1 = iota((8, 128), 0)
    joined = [jnp.where(sub1 < 4, far, near) for near, far in zip(*done)]
    joined = jnp.concatenate(joined + [jnp.zeros((128 - 8 * NV, 128), F32)], axis=0).T
    lane1 = iota((128, 128), 1)

    def add_columns(v):
        x = pltpu.roll(joined, (124 - 8 * v) % 128, 1)
        qout[v, :, 0:128] += jnp.where(lane1 < 4, x, 0.0)
        qout[v, :, 128:256] += jnp.where(lane1 >= 124, x, 0.0)

    add_columns(NV - 1)

    pres = qout[4]
    pres = jnp.concatenate([pres[:, 0:128].T, pres[:, 128:256].T], axis=1)
    ph, plow = split(pres)
    pres2 = jnp.concatenate([ph, plow], axis=0)
    row16 = iota((16, 128), 0)

    def gather(o, cols):
        h = dot(pres2, cols, NN)
        h = h[0:128] + h[128:256]
        n16 = norms[o]
        forces = []
        for j in range(SEND):
            mask = iota((128, 128), 0) == cellv[o, SEND + j : SEND + j + 1, :]
            p = jnp.sum(jnp.where(mask, h[:, 128 * j : 128 * (j + 1)], 0.0), axis=0, keepdims=True)
            forces.append(jnp.where((row16 & 3) == j, n16 * p, 0.0).astype(BF16))
        return jnp.concatenate(forces, axis=1)

    def gather_four(q, _):
        for first in (0, 2):
            forces = [gather(4 * q + first + i, rall[q, :, 512 * (first + i) : 512 * (first + i + 1)]) for i in range(2)]
            weights = [rbf[4 * q + first + i].reshape(SEND * 128, 128) for i in range(2)]
            both = dot(jnp.concatenate(forces, axis=0), jnp.concatenate(weights, axis=1), NN)
            load_out[4 * q + first] = both[0:16, 0:128]
            load_out[4 * q + first + 1] = both[16:32, 128:256]
        return 0

    for q in (1, 3, 2, 0):
        lax.fori_loop(q, q + 1, gather_four, 0)
        blk_send(lambda o: load_out.at[o], land_load, 3, [o for o in reversed(range(4 * q, 4 * q + 4)) if o != ME])
    land_load[ME] = load_out[ME]

    l_secv.wait()
    zero8 = jnp.zeros((8, 128), F32)

    def gram_row(i, _):
        for c in range(3):
            x = secv[:, c, pl.ds(i, 1), :].reshape(COLS, 128)
            x = jnp.where((i >= off) & (i < off + OWN), x, 0.0)
            hi, lo = split(jnp.concatenate([x, zero8], axis=0))
            at = pl.multiple_of((c * WIN + i) * 128, 128)
            zmat[0:32, pl.ds(at, 128)] = hi
            zmat[32:64, pl.ds(at, 128)] = lo
        return 0

    lax.fori_loop(0, WIN, gram_row, 0)
    zz = zmat[...]
    top = dot(zz, zz[0:32], NT)
    low = dot(zz, zz[32:64], NT)
    gram = top[0:32] + top[32:64] + low[0:32] + low[32:64]
    gsend[...] = jnp.zeros(gsend.shape, F32)
    gsend[:, 0:32] = gram
    land_gg[g] = gsend[...]
    grp_send(lambda d: gsend, land_gg, 0)

    row = iota((COLS, 128), 0)
    lane = iota((COLS, 128), 1)
    wrow = iota((48, 128), 0) & 15
    mine = (wrow >= off) & (wrow < off + OWN)
    diag = lane == row + 32

    blk_recv(lambda o: req.at[peer(o)], land_req, 0, [FAR])
    asked_t = land_req[...].reshape(NB * 16, 128).T[0:1, :]
    rr, kk = iota((48, NB * 16), 0), iota((48, NB * 16), 1)
    w = rr & 15
    same_c = (lax.shift_right_logical(kk, 2) & 3) == lax.shift_right_logical(rr, 4)
    for p in range(NG):
        first = (p * OWN) // 8 * 8
        skip = p * OWN - first
        ok = same_c & (w >= skip) & (w < skip + OWN)
        oht[48 * p : 48 * (p + 1), :] = jnp.where(ok & (asked_t == (w + first).astype(F32)), 1.0, 0.0).astype(BF16)

    blk_recv(lambda o: load_out.at[o], land_load, 3)
    got = land_load[...].reshape(NB * 16, 128)
    hi, lo = split(got)
    sums = dot(oht[...], jnp.concatenate([hi, lo], axis=1), NN)
    part[...] = (sums[:, 0:128] + sums[:, 128:256]).reshape(NG, 48, 128)
    land_part[g] = part[g]
    grp_send(lambda d: part.at[d], land_part, 1)
    for v in range(NV - 1):
        add_columns(v)
    flow_out = pltpu.make_async_copy(qout, flow_o, osem.at[0])
    flow_out.start()
    pending.append(flow_out.wait)
    d_in = jnp.where(mine, disp[:, pl.ds(a, WIN), :].reshape(48, 128), 0.0)
    rhs_in = jnp.sum(secv[...].reshape(COLS, 48, 128) * d_in[None], axis=1)
    l_flex.wait()

    def project(i, _):
        at = pl.multiple_of(128 * i, 128)
        hi, lo = split(flex[i])
        flexhl[pl.ds(at, 128), 0:128] = hi
        flexhl[pl.ds(at, 128), 128:256] = lo
        vh, vl = split(jnp.concatenate([secv[:, c, pl.ds(i, 1), :].reshape(COLS, 128) for c in range(3)], axis=0))
        u = dot(jnp.concatenate([vh, vl], axis=0), hi, NN)
        u = u[0:72] + u[72:144] + dot(vh, lo, NN)
        for c in range(3):
            uwin[:, c, pl.ds(i, 1), :] = u[COLS * c : COLS * (c + 1)].reshape(COLS, 1, 128)
        return 0

    lax.fori_loop(0, WIN, project, 0)
    grp_recv(lambda d: gsend, land_gg, 0)
    gsum[...] = jnp.sum(land_gg[...], axis=0)
    land_gb[ME] = gsum[...]
    blk_send(lambda o: gsum, land_gb, 2)
    grp_recv(lambda d: part.at[d], land_part, 1)
    tile_loads = jnp.sum(land_part[...], axis=0)

    prod = jnp.sum(uwin[...].reshape(COLS, 48, 128) * tile_loads[None], axis=1) - rhs_in
    rhs = jnp.sum(prod, axis=1, keepdims=True)
    rhs = jnp.sum(jnp.where(diag, rhs, 0.0), axis=0, keepdims=True)
    rmsg[...] = jnp.broadcast_to(rhs, (8, 128))
    land_rg[g] = rmsg[...]
    grp_send(lambda d: rmsg, land_rg, 2)
    hi, lo = split(tile_loads)
    lhs = jnp.concatenate(
        [jnp.concatenate([hi, hi], axis=1), jnp.concatenate([lo, jnp.zeros_like(lo)], axis=1)], axis=0
    )
    tilde = jnp.zeros((48, 128), F32)
    for u in range(WIN // 2):
        o = dot(lhs, flexhl[256 * u : 256 * (u + 1), :], NT)
        o = o[0:48] + o[48:96]
        tilde = jnp.where(wrow == 2 * u, o[:, 0:128], tilde)
        tilde = jnp.where(wrow == 2 * u + 1, o[:, 128:256], tilde)
    tmsg[...] = jnp.where(mine, tilde, 0.0)
    land_t[g] = tmsg[...]
    grp_send(lambda d: tmsg, land_t, 3)
    grp_recv(lambda d: rmsg, land_rg, 2)
    rsend[...] = jnp.sum(land_rg[...], axis=0)
    land_r[ME] = rsend[...]
    blk_send(lambda o: rsend, land_r, 4)
    l_secw.wait()
    blk_recv(lambda o: gsum, land_gb, 2)
    gram = jnp.sum(land_gb[...], axis=0)[0:COLS]
    row = iota((COLS, 128), 0)
    lane = iota((COLS, 128), 1)
    m = jnp.where(lane < COLS, gram, jnp.where(lane == row + 32, 1.0, 0.0))
    fac = jnp.zeros((COLS, 128), F32)
    for k in range(COLS):
        pivot = lax.rsqrt(jnp.broadcast_to(m[k : k + 1, k : k + 1], (1, 128)))
        r = m[k : k + 1, :] * pivot
        col = jnp.broadcast_to(m[:, k : k + 1], (COLS, 128)) * pivot
        fac = jnp.where(row == k, r, fac)
        m = m - jnp.where(row > k, col * r, 0.0)
    linv[...] = jnp.where((lane >= 32) & (lane < 32 + COLS), fac, 0.0)
    grp_recv(lambda d: tmsg, land_t, 3)
    blk_recv(lambda o: rsend, land_r, 4)
    rhs = jnp.sum(land_r[...], axis=0)[0:1]

    li = linv[...]
    y = jnp.sum(li * rhs, axis=1, keepdims=True)
    x = jnp.sum(li * y, axis=0, keepdims=True)
    x = -jnp.sum(jnp.where(diag, x, 0.0), axis=1, keepdims=True)
    coef[...] = jnp.broadcast_to(x, (COLS, 128))

    def update(p, _):
        for c in range(3):
            even, odd = land_t[2 * p, 16 * c : 16 * c + 16, :], land_t[2 * p + 1, 16 * c : 16 * c + 16, :]
            for q, t in enumerate((even[0:8], even[8:16] + odd[0:8], odd[8:16])):
                at = pl.multiple_of(24 * p + 8 * q, 8)
                for k in range(COLS):
                    t = t + coef[k : k + 1, :] * secw[k, c, pl.ds(at, 8), :]
                dout[c, pl.ds(at, 8), :] = t
        return 0

    lax.fori_loop(0, NG // 2, update, 0)
    disp_out = pltpu.make_async_copy(dout, disp_o, osem.at[1])
    disp_out.start()
    pending.append(disp_out.wait)

    finish()


def deliver(flow, disp, flow_out, disp_out, sems):
    copies = [pltpu.make_async_copy(flow, flow_out, sems.at[0]), pltpu.make_async_copy(disp, disp_out, sems.at[1])]
    for c in copies:
        c.start()
    for c in copies:
        c.wait()


def stay(x):
    return pltpu.with_memory_space_constraint(x, pltpu.HBM)


def on_device(flow_state, jx, jy, slot_tile, slot_cells, slot_normal, slot_rbf, disp_in, flex, secv, secw):
    hbm = pl.BlockSpec(memory_space=pl.ANY)
    vm, dma = pltpu.VMEM, pltpu.SemaphoreType.DMA
    state = (NV, CX + 16, CY + 128)
    scratch = [
        pltpu.SMEM((NV, NV), F32), pltpu.SMEM((NV, NV), F32),
        vm((1, 64), jnp.int32), vm((64, 128), jnp.int32), vm((3, 64, 128), F32), vm((NB, SEND, 128, 128), BF16),
        vm((3, ST, 128), F32), vm((WIN, 128, 128), F32), vm((COLS, 3, WIN, 128), F32), vm((COLS, 3, ST, 128), F32),
        vm(state, F32), vm(state, F32), vm(state, F32), vm((NV, CX, CY), F32),
        vm((NV, 32, CY + 128), F32), vm((NV, 32, CY + 128), F32), vm((NV, 32, CY + 128), F32),
        vm((NB, 16, 128), F32), vm((NB, 16, 128), F32), vm((NB, 16, 128), BF16), vm((NB, 16, 128), BF16),
        vm((384, 128), BF16),
        vm((NB, 8, 128), jnp.int32), vm((4, 256, 2048), BF16), vm((4, 256, 2048), F8),
        vm((384, 2048), BF16), vm((384, 2048), F8), vm((384, 256), F32), vm((384, 128), BF16),
        vm((64, 128), F32),
        vm((NV, 8, CY), F32), vm((NV, 8, CY), F32), vm((64, 128), F32), vm((64, 128), F32), vm((4, 8, 128), F32),
        vm((256, 128), F32), vm((NB, 16, 128), F32), vm((NB, 16, 128), F32), vm((NB, 16, 128), F32), vm((384, 256), BF16),
        vm((NG, 48, 128), F32), vm((NG, 48, 128), F32),
        vm((WIN * 128, 256), BF16), vm((COLS, 3, WIN, 128), F32), vm((64, 48 * 128), BF16),
        vm((32, 128), F32), vm((NG, 32, 128), F32), vm((32, 128), F32), vm((NB, 32, 128), F32), vm((COLS, 128), F32),
        vm((8, 128), F32), vm((NG, 8, 128), F32), vm((48, 128), F32), vm((NG, 48, 128), F32),
        vm((8, 128), F32), vm((NB, 8, 128), F32), vm((COLS, 128), F32), vm((3, ST, 128), F32),
        dma((10,)), dma((NB,)), dma((4,)),
        dma((5, NB)), dma((5, NB)), dma((4, NG)), dma((4, NG)), dma((8,)), dma((8,)),
    ]
    flow_out, disp_out = pl.pallas_call(
        kernel,
        out_shape=(
            vm((NV, CX, CY), F32),
            vm((3, ST, 128), F32),
        ),
        in_specs=[hbm] * 11,
        out_specs=(hbm, hbm),
        scratch_shapes=scratch,
        compiler_params=pltpu.CompilerParams(
            collective_id=0, has_side_effects=True, vmem_limit_bytes=48 * 1024 * 1024
        ),
    )(*[
        stay(x) for x in (
            flow_state, jx, jy, slot_tile.reshape(1, -1), slot_cells, jnp.transpose(slot_normal, (1, 0, 2)), slot_rbf,
            jnp.transpose(disp_in, (1, 0, 2)), flex, jnp.transpose(secv, (0, 2, 1, 3)), jnp.transpose(secw, (0, 2, 1, 3)),
        )
    ])
    flow_out, disp_out = pl.pallas_call(
        deliver,
        out_shape=(jax.ShapeDtypeStruct(flow_out.shape, F32), jax.ShapeDtypeStruct(disp_out.shape, F32)),
        in_specs=[hbm, hbm],
        out_specs=(hbm, hbm),
        scratch_shapes=[dma((2,))],
        compiler_params=pltpu.CompilerParams(vmem_limit_bytes=1024 * 1024),
    )(flow_out, disp_out)
    return flow_out, jnp.transpose(disp_out, (1, 0, 2))


def solution(mesh):
    placed = (
        P(None, "grp", "blk"), P(), P(),
        P(("grp", "blk")), P(("grp", "blk"), None),
        P(("grp", "blk"), None, None), P(("grp", "blk"), None, None),
        P("blk", None, None), P("blk", None, None),
        P(None, "blk", None, None), P(None, "blk", None, None),
    )
    return jax.shard_map(
        on_device, mesh=mesh, in_specs=placed,
        out_specs=(P(None, "grp", "blk"), P("blk", None, None)), check_vma=False,
    )
```
